32 devices in a mesh: ctx: 8 (over z, y), ep: 4 (over x, core).
Axes of the slice: x: 2, y: 2, z: 4, core: 2. Of those that a mesh axis runs over, the one named last changes fastest.
Arguments:
- q_nope: bfloat16 [1024, 8192], P('ctx', 'ep'), may hold values from -6 to 6
- q_rope: bfloat16 [1024, 4096], P('ctx', 'ep'), may hold values from -300 to 300
- latent: bfloat16 [1024, 512], P('ctx'), may hold values from -6 to 6
- k_rope: bfloat16 [1024, 64], P('ctx'), may hold values from -5 to 5
- w_uk: bfloat16 [512, 8192], P(None, 'ep'), may hold values from -0.25 to 0.25
- w_uv: bfloat16 [512, 8192], P(None, 'ep'), may hold values from -0.25 to 0.25
- positions: int32 [1024], replicated, may hold values from 0 to 1023, as said below
- moe_rows: bfloat16 [1024, 7168], P('ctx', 'ep'), may hold values from -6 to 6
- expert_ids: int32 [1024, 8], P('ctx'), may hold values from 0 to 255, all different within a row; in each aligned block of 128 rows (0 to 127, 128 to 255, ...) at most 8 rows name the same one
- expert_weights: float32 [1024, 8], P('ctx'), may hold values from 0.05 to 0.5
- w_gate: bfloat16 [8, 7168, 1024], P('ctx', None, 'ep'), may hold values from -0.0625 to 0.0625
- w_up: bfloat16 [8, 7168, 1024], P('ctx', None, 'ep'), may hold values from -0.0625 to 0.0625
- w_down: bfloat16 [8, 1024, 7168], P('ctx', 'ep'), may hold values from -0.1875 to 0.1875
Outputs:
- attention: bfloat16 [1024, 8192], P('ctx', 'ep')
- moe_out: bfloat16 [1024, 7168], P('ctx', 'ep')
The draws below stay inside these ranges and needn't reach their ends.
Inputs may be any that keep to these rules, and one draw needn't show every extreme that they name: `expert_ids`: each row names 8 different experts; in each aligned block of 128 rows (the rows of one index of ctx) no expert is named by more than 8 rows. A permutation of the positions; the 128 rows of each index of ctx are two runs of 64 consecutive positions, run j and run 2 * 8 - 1 - j of the prompt for some j.
All inputs are finite; a program needn't handle non-finite values.
Results may differ from the reference program's by a relative error of at most 0.017.
Values may be sent and summed in bfloat16 or wider, within the bound.
No kernel may reach another device: no remote copies, remote signals or barrier semaphores. Data moves between devices by JAX's collectives and lax.ppermute only.
A program may use at most 192 MiB of HBM per device.

```python
import math
import jax
import jax.numpy as jnp
import numpy as np
from jax import lax

D = 7168
F = 1024
HEADS = 64
NOPE = 128
ROPE = 64
VDIM = 128
LAT = 512
EXPERTS = 256
TOP = 8
TQ = 128
ROWS = 128
HALF = 64
SEQ = 1024
MOE_TOKENS = 1024
EXP_WIN = 8
CAP = 8
N_CTX = 8


def rope_pair(key):
    key_base = jax.random.fold_in(key, 0)
    key_query = jax.random.fold_in(key, 4)
    keys_rope = jnp.clip(jax.random.normal(key_base, (SEQ, ROPE), jnp.float32), -4.0, 4.0)
    keys_out = keys_rope
    queries = jnp.clip(jax.random.normal(key_query, (SEQ, HEADS, ROPE), jnp.float32), -6.0, 6.0)
    return (keys_out, queries.reshape(SEQ, HEADS * ROPE))


def draw_q_rope(key, part):
    keys_out, queries = rope_pair(key)
    return queries.astype(jnp.bfloat16)


def draw_k_rope(key, part):
    keys_out, queries = rope_pair(key)
    return keys_out.astype(jnp.bfloat16)


def draw_positions(key, part):
    key = jax.random.fold_in(key, 7)
    block_count = SEQ // TQ
    order = jax.random.permutation(key, block_count).astype(jnp.int32)
    lanes = jnp.arange(HALF, dtype=jnp.int32)
    first_run = order[:, None] * HALF + lanes[None, :]
    second_run = (2 * block_count - 1 - order)[:, None] * HALF + lanes[None, :]
    return jnp.concatenate([first_run, second_run], axis=1).reshape(SEQ).astype(jnp.int32)


def block_scale(stream_key, extent, pieces, least, largest):
    loudness, own = 1.0, jax.random.fold_in(stream_key, 6)
    for position, shards_of in pieces:
        steps = jnp.exp(jax.random.uniform(jax.random.fold_in(own, position), (shards_of,), jnp.float32, least / len(pieces), largest / len(pieces)))
        loudness = loudness * jnp.repeat(steps, extent[position] // shards_of).reshape([-1 if axis == position else 1 for axis in range(len(extent))])
    return loudness


def shared_out(stream_key, own, number, rows, amount, top, bound, lean):
    order = jax.random.permutation(stream_key, amount)
    heavy_load, ordinary = portions_of(amount, rows * top, bound, lean, True), portions_of(amount, rows * top, bound, lean, False)
    places = jnp.arange(amount)

    def named(sizes, offset_by):
        used = int((sizes > 0).sum())
        fixed = max(1, used // 4)
        shifted = fixed + (places - fixed + offset_by * (used - fixed)) % max(1, amount - fixed)
        return jnp.zeros((amount,), jnp.int32).at[order[jnp.where(places < fixed, places, shifted)]].set(jnp.asarray(sizes, jnp.int32))

    sizes = jnp.where(number % 4 == 0, named(heavy_load, number // 4), named(ordinary, number - number // 4 - 1))
    mixed = jax.random.permutation(jax.random.fold_in(own, 3), amount)
    donor, receiver = mixed[0:amount // 2 * 2:2], mixed[1:amount // 2 * 2:2]
    slack = jnp.minimum(sizes[donor] - 1, bound - sizes[receiver]) // 2
    slack = jnp.where((donor == order[0]) | (receiver == order[0]) | (sizes[receiver] == 0), 0, jnp.maximum(slack, 0))
    shifted = jax.random.randint(jax.random.fold_in(own, 4), (amount // 2,), 0, 1 << 20) % (slack + 1)
    sizes = sizes.at[donor].add(-shifted).at[receiver].add(shifted)
    labels = jnp.searchsorted(jnp.cumsum(sizes), jnp.arange(rows * top), side="right").astype(jnp.int32)
    grid = labels.reshape(top, rows).T
    grid = grid[jax.random.permutation(jax.random.fold_in(own, 1), rows)]
    offset_by = jax.random.randint(jax.random.fold_in(own, 2), (rows, 1), 0, top)
    return jnp.take_along_axis(grid, (jnp.arange(top)[None, :] + offset_by) % top, axis=1)


def portions_of(amount, total, bound, skew, full):
    portions = [(1 << 20) // math.isqrt(standing ** skew) + 1 for standing in range(1, amount + 1)]
    largest = bound if full else min(bound, max(-(-total // amount), total * portions[0] // sum(portions)))
    least = 1 if total - largest >= amount - 1 else 0
    counts, spare = [largest] + [least] * (amount - 1), total - largest - least * (amount - 1)
    while spare > 0:
        movable = [i for i in range(1, amount) if counts[i] < largest] or [i for i in range(1, amount) if counts[i] < bound]
        pool, remaining = sum([portions[i] for i in movable]), spare
        for i in movable:
            extra = min(bound - counts[i], max(1, remaining * portions[i] // pool), spare)
            counts[i] = counts[i] + extra
            spare = spare - extra
    return np.array(counts)


def centred(stream_key, shape, deviation, bound, cuts=(), kind=jnp.bfloat16):
    values = deviation * jax.random.normal(stream_key, shape, jnp.float32)
    if cuts:
        values = values * block_scale(stream_key, shape, cuts, -0.22, 0.18)
    return jnp.clip(values, -bound, bound).astype(kind)


def setup_inputs(seed: int = 0) -> dict:
    streams_of = jax.random.split(jax.random.key(seed), 14)
    q_nope = centred(streams_of[0], (SEQ, HEADS * NOPE), 1.0, 6.0, ((0, 8), (1, 4)))
    q_rope = draw_q_rope(jax.random.fold_in(streams_of[13], 71), 0)
    latent = centred(streams_of[2], (SEQ, LAT), 1.0, 6.0, ((0, 8),))
    k_rope = draw_k_rope(jax.random.fold_in(streams_of[13], 71), 0)
    w_uk = centred(streams_of[4], (LAT, HEADS * NOPE), LAT ** -0.5, 0.25, ((1, 4),))
    w_uv = centred(streams_of[5], (LAT, HEADS * VDIM), LAT ** -0.5, 0.25, ((1, 4),))
    positions = draw_positions(jax.random.fold_in(streams_of[13], 71), 0)
    moe_rows = centred(streams_of[7], (MOE_TOKENS, D), 1.0, 6.0, ((0, 8), (1, 4)))
    expert_ids_keys = jax.random.split(jax.random.fold_in(streams_of[8], 1), MOE_TOKENS // ROWS)
    expert_ids_turns = jax.random.permutation(jax.random.fold_in(streams_of[8], 3), MOE_TOKENS // ROWS)
    expert_ids = jax.vmap(lambda own, number: shared_out(jax.random.fold_in(streams_of[8], 2), own, number, ROWS, EXPERTS, TOP, CAP, 1))(expert_ids_keys, expert_ids_turns).reshape((MOE_TOKENS, TOP))
    expert_weights = jnp.clip(0.05 + 0.45 * jax.random.uniform(streams_of[9], (MOE_TOKENS, TOP), jnp.float32) ** block_scale(streams_of[9], (MOE_TOKENS, TOP), ((0, 8),), -0.2, 0.2), 0.05, 0.5)
    w_gate = centred(streams_of[10], (EXP_WIN, D, F), D ** -0.5, 0.0625, ((0, 8), (2, 4)))
    w_up = centred(streams_of[11], (EXP_WIN, D, F), D ** -0.5, 0.0625, ((0, 8), (2, 4)))
    w_down = centred(streams_of[12], (EXP_WIN, F, D), F ** -0.5, 0.1875, ((0, 8), (1, 4)))
    return dict(q_nope=q_nope, q_rope=q_rope, latent=latent, k_rope=k_rope, w_uk=w_uk, w_uv=w_uv, positions=positions, moe_rows=moe_rows, expert_ids=expert_ids, expert_weights=expert_weights, w_gate=w_gate, w_up=w_up, w_down=w_down)


def reference(q_nope, q_rope, latent, k_rope, w_uk, w_uv, positions, moe_rows, expert_ids, expert_weights, w_gate, w_up, w_down):
    seq_len = latent.shape[0]
    keys_nope = jnp.dot(latent, w_uk, preferred_element_type=jnp.float32).astype(jnp.bfloat16)
    values = jnp.dot(latent, w_uv, preferred_element_type=jnp.float32).astype(jnp.bfloat16)
    per_head = (q_nope.reshape(seq_len, HEADS, NOPE).transpose(1, 0, 2), q_rope.reshape(seq_len, HEADS, ROPE).transpose(1, 0, 2), keys_nope.reshape(seq_len, HEADS, NOPE).transpose(1, 0, 2), values.reshape(seq_len, HEADS, VDIM).transpose(1, 0, 2))
    visible = positions[None, :] <= positions[:, None]
    score_scale = 1.0 / math.sqrt(NOPE + ROPE)

    def one_head(operands):
        query_nope, query_rope, head_keys, head_values = operands
        scores = jnp.dot(query_nope, head_keys.T, preferred_element_type=jnp.float32)
        scores = (scores + jnp.dot(query_rope, k_rope.T, preferred_element_type=jnp.float32)) * score_scale
        scores = jnp.where(visible, scores, -jnp.inf)
        row_max = lax.optimization_barrier(jnp.max(scores, axis=1, keepdims=True))
        weights_exp = jnp.where(visible, jnp.exp(scores - row_max), 0.0)
        row_total = lax.optimization_barrier(jnp.sum(weights_exp, axis=1, keepdims=True))
        return jnp.dot(weights_exp.astype(jnp.bfloat16), head_values, preferred_element_type=jnp.float32) / row_total
    attended = lax.map(one_head, per_head)
    attention = attended.transpose(1, 0, 2).reshape(seq_len, HEADS * VDIM).astype(jnp.bfloat16)
    token_count = moe_rows.shape[0]
    flat_experts = expert_ids.reshape(N_CTX, ROWS * TOP)
    in_window = flat_experts < EXP_WIN
    one_hot = ((flat_experts[:, :, None] == jnp.arange(EXP_WIN, dtype=jnp.int32)[None, None, :]) & in_window[:, :, None]).astype(jnp.int32)
    earlier = jnp.cumsum(one_hot, axis=1) - one_hot
    rank_in_expert = lax.optimization_barrier(jnp.sum(earlier * one_hot, axis=2)).astype(jnp.int32)
    block_index = jnp.arange(N_CTX, dtype=jnp.int32)[:, None]
    capacity_rows = N_CTX * CAP
    slot_index = jnp.where(in_window, flat_experts * capacity_rows + block_index * CAP + rank_in_expert, EXP_WIN * capacity_rows).reshape(-1).astype(jnp.int32)
    token_index = jnp.repeat(jnp.arange(token_count, dtype=jnp.int32), TOP)
    source_rows = jnp.zeros((EXP_WIN * capacity_rows,), jnp.int32).at[slot_index].set(token_index, mode='drop')
    slot_weights = jnp.zeros((EXP_WIN * capacity_rows,), jnp.float32).at[slot_index].set(expert_weights.reshape(-1), mode='drop')

    def add_expert(total, operands):
        rows_of, weights_of, gate_mat, up_mat, down_mat = operands
        inputs = moe_rows[rows_of]
        gate = jnp.dot(inputs, gate_mat, preferred_element_type=jnp.float32)
        upper = jnp.dot(inputs, up_mat, preferred_element_type=jnp.float32)
        hidden = (jax.nn.silu(gate) * upper).astype(jnp.bfloat16)
        outputs = jnp.dot(hidden, down_mat, preferred_element_type=jnp.float32)
        return (total.at[rows_of].add(weights_of[:, None] * outputs), None)
    total, unused = lax.scan(add_expert, jnp.zeros((token_count, D), jnp.float32), (source_rows.reshape(EXP_WIN, capacity_rows), slot_weights.reshape(EXP_WIN, capacity_rows), w_gate, w_up, w_down))
    return (attention, total.astype(jnp.bfloat16))
```

```python
import math

import jax
import jax.numpy as jnp
from jax import lax
from jax.experimental import pallas as pl
from jax.experimental.pallas import tpu as pltpu
from jax.sharding import PartitionSpec as P

NOPE = 128
ROPE = 64
VDIM = 128
TOP = 8
CAP = 8
HALF = 64
GROUP = 4
MIB = 1 << 20
LIMIT = 52 * MIB
FULL = 60 * MIB

NT = (((1,), (1,)), ((), ()))
TN = (((0,), (0,)), ((), ()))
VMEM = pltpu.VMEM
SMEM_SPEC = pl.BlockSpec(memory_space=pltpu.SMEM)
VMEM_SPEC = pl.BlockSpec(memory_space=pltpu.VMEM)
HBM_SPEC = pl.BlockSpec(memory_space=pltpu.HBM)


def route_kernel(
    ep_ref,
    ids_ref,
    weights_ref,
    rope_ref,
    rows_ref,
    latent_ref,
    sent_ref,
    high_ref,
    low_ref,
    packed_ref,
):
    quarter = packed_ref.shape[0]
    latent_width = latent_ref.shape[1]
    place = pl.multiple_of(ep_ref[0] * quarter, quarter)
    row_count = ids_ref.shape[1]
    slots = sent_ref.shape[0] * CAP
    slot = lax.broadcasted_iota(jnp.int32, (slots, row_count), 0)
    expert = slot // CAP
    named = jnp.zeros((slots, row_count), jnp.float32)
    gate = jnp.zeros((slots, row_count), jnp.float32)
    for choice in range(TOP):
        match = ids_ref[choice : choice + 1, :] == expert
        named = jnp.where(match, 1.0, named)
        gate = jnp.where(match, weights_ref[choice : choice + 1, :], gate)
    row = lax.broadcasted_iota(jnp.int32, (row_count, row_count), 0)
    other = lax.broadcasted_iota(jnp.int32, (row_count, row_count), 1)
    before = jnp.where(row < other, 1.0, 0.0).astype(jnp.bfloat16)
    rank = jnp.dot(named.astype(jnp.bfloat16), before, preferred_element_type=jnp.float32)
    taken = (named > 0.0) & (rank == (slot % CAP).astype(jnp.float32))
    select = jnp.where(taken, 1.0, 0.0).astype(jnp.bfloat16)
    gate = jnp.where(taken, gate, 0.0)
    high = gate.astype(jnp.bfloat16)
    high_ref[...] = high
    low_ref[...] = (gate - high.astype(jnp.float32)).astype(jnp.bfloat16)
    rope = rope_ref[...].astype(jnp.float32).T
    packed_ref[:, :latent_width] = latent_ref[pl.ds(place, quarter), :]
    for part in range(row_count // quarter):

        @pl.when(ep_ref[0] == part)
        def _():
            packed_ref[:, latent_width:] = rope[part * quarter : (part + 1) * quarter].astype(
                jnp.bfloat16
            )

    sent = jnp.dot(select, rows_ref[...], preferred_element_type=jnp.float32)
    for index in range(slots // CAP):
        sent_ref[index] = sent[index * CAP : (index + 1) * CAP].astype(jnp.bfloat16)


def route(ep, expert_ids, expert_weights, k_rope, moe_rows, latent, ctx):
    row_count, features = moe_rows.shape
    quarter = row_count // 4
    latent_width = latent.shape[1]
    slots = ctx * CAP
    return pl.pallas_call(
        route_kernel,
        out_shape=[
            jax.ShapeDtypeStruct((ctx, CAP, features), jnp.bfloat16),
            jax.ShapeDtypeStruct((slots, row_count), jnp.bfloat16),
            jax.ShapeDtypeStruct((slots, row_count), jnp.bfloat16),
            jax.ShapeDtypeStruct((quarter, latent_width + ROPE), jnp.bfloat16),
        ],
        in_specs=[SMEM_SPEC] + [VMEM_SPEC] * 5,
        out_specs=[VMEM_SPEC] * 4,
        compiler_params=pltpu.CompilerParams(vmem_limit_bytes=FULL),
        cost_estimate=pl.CostEstimate(
            flops=2 * row_count * slots * features, bytes_accessed=1 * MIB, transcendentals=0
        ),
        name="route",
    )(ep, expert_ids.T, expert_weights.T, k_rope.T, moe_rows, latent)


def weight_copies(ep_ref, flips, gate_hbm, up_hbm, gate, up, semaphores):
    features = gate.shape[1]
    copies = []
    for index, flip in enumerate(flips):
        place = pl.multiple_of((ep_ref[0] ^ flip) * features, features)
        for which, (source, target) in enumerate(((gate_hbm, gate), (up_hbm, up))):
            copy = pltpu.make_async_copy(
                source.at[0, pl.ds(place, features)], target.at[index], semaphores.at[index, which]
            )
            copy.start()
            copies.append(copy)
    return copies


def near_kernel(
    ep_ref, own_ref, core_ref, gate_hbm, up_hbm, gate_out, up_out, gate, up, semaphores
):
    copies = weight_copies(ep_ref, (0, 1), gate_hbm, up_hbm, gate, up, semaphores)
    gate_sum, up_sum = None, None
    for index, x_ref in enumerate((own_ref, core_ref)):
        rows = x_ref[...]
        copies[2 * index].wait()
        part = jnp.dot(rows, gate[index], preferred_element_type=jnp.float32)
        gate_sum = part if gate_sum is None else gate_sum + part
        copies[2 * index + 1].wait()
        part = jnp.dot(rows, up[index], preferred_element_type=jnp.float32)
        up_sum = part if up_sum is None else up_sum + part
    gate_out[...] = gate_sum
    up_out[...] = up_sum


def near_experts(ep, own, core, w_gate, w_up):
    slots, features = own.shape
    units = w_gate.shape[2]
    return pl.pallas_call(
        near_kernel,
        out_shape=[jax.ShapeDtypeStruct((slots, units), jnp.float32)] * 2,
        in_specs=[SMEM_SPEC] + [VMEM_SPEC] * 2 + [HBM_SPEC] * 2,
        out_specs=[VMEM_SPEC] * 2,
        scratch_shapes=[
            VMEM((2, features, units), jnp.bfloat16),
            VMEM((2, features, units), jnp.bfloat16),
            pltpu.SemaphoreType.DMA((2, 2)),
        ],
        compiler_params=pltpu.CompilerParams(vmem_limit_bytes=LIMIT),
        cost_estimate=pl.CostEstimate(
            flops=8 * slots * features * units,
            bytes_accessed=8 * features * units,
            transcendentals=0,
        ),
        name="near_experts",
    )(ep, own, core, w_gate, w_up)


def far_kernel(
    ep_ref,
    far_ref,
    core_far_ref,
    gate_part,
    up_part,
    gate_hbm,
    up_hbm,
    down_hbm,
    own_out,
    core_out,
    far_out,
    core_far_out,
    gate,
    up,
    down,
    semaphores,
    down_semaphores,
):
    features = gate.shape[1]
    copies = weight_copies(ep_ref, (2, 3), gate_hbm, up_hbm, gate, up, semaphores)
    down_copies = []
    for flip in (3, 1, 2, 0):
        place = pl.multiple_of((ep_ref[0] ^ flip) * features, features)
        copy = pltpu.make_async_copy(
            down_hbm.at[0, :, pl.ds(place, features)], down.at[flip], down_semaphores.at[flip]
        )
        copy.start()
        down_copies.append(copy)
    gate_sum, up_sum = gate_part[...], up_part[...]
    for index, x_ref in enumerate((far_ref, core_far_ref)):
        rows = x_ref[...]
        copies[2 * index].wait()
        gate_sum = gate_sum + jnp.dot(rows, gate[index], preferred_element_type=jnp.float32)
        copies[2 * index + 1].wait()
        up_sum = up_sum + jnp.dot(rows, up[index], preferred_element_type=jnp.float32)
    hidden = (gate_sum / (1.0 + jnp.exp(-gate_sum)) * up_sum).astype(jnp.bfloat16)
    outs = (own_out, core_out, far_out, core_far_out)
    for copy, flip in zip(down_copies, (3, 1, 2, 0)):
        copy.wait()
        outs[flip][...] = jnp.dot(
            hidden, down[flip], preferred_element_type=jnp.float32
        ).astype(jnp.bfloat16)


def far_experts(ep, far, core_far, gate_part, up_part, w_gate, w_up, w_down):
    slots, features = far.shape
    units = w_gate.shape[2]
    return pl.pallas_call(
        far_kernel,
        out_shape=[jax.ShapeDtypeStruct((slots, features), jnp.bfloat16)] * 4,
        in_specs=[SMEM_SPEC] + [VMEM_SPEC] * 4 + [HBM_SPEC] * 3,
        out_specs=[VMEM_SPEC] * 4,
        scratch_shapes=[
            VMEM((2, features, units), jnp.bfloat16),
            VMEM((2, features, units), jnp.bfloat16),
            VMEM((4, units, features), jnp.bfloat16),
            pltpu.SemaphoreType.DMA((2, 2)),
            pltpu.SemaphoreType.DMA((4,)),
        ],
        compiler_params=pltpu.CompilerParams(vmem_limit_bytes=LIMIT),
        cost_estimate=pl.CostEstimate(
            flops=16 * slots * features * units,
            bytes_accessed=16 * features * units,
            transcendentals=slots * units,
        ),
        name="far_experts",
    )(ep, far, core_far, gate_part, up_part, w_gate, w_up, w_down)


def add_kernel(*refs):
    total = refs[0][...].astype(jnp.float32)
    for ref in refs[1:-1]:
        total = total + ref[...].astype(jnp.float32)
    refs[-1][...] = total.astype(jnp.bfloat16)


def add(*parts):
    return pl.pallas_call(
        add_kernel,
        out_shape=jax.ShapeDtypeStruct(parts[0].shape, jnp.bfloat16),
        in_specs=[VMEM_SPEC] * len(parts),
        out_specs=VMEM_SPEC,
        compiler_params=pltpu.CompilerParams(vmem_limit_bytes=8 * MIB),
        cost_estimate=pl.CostEstimate(flops=0, bytes_accessed=MIB, transcendentals=0),
        name="add",
    )(*parts)


def combine_kernel(high_ref, low_ref, returned_ref, out_ref):
    returned = returned_ref[...]
    total = lax.dot_general(high_ref[...], returned, TN, preferred_element_type=jnp.float32)
    total = total + lax.dot_general(
        low_ref[...], returned, TN, preferred_element_type=jnp.float32
    )
    out_ref[...] = total.astype(jnp.bfloat16)


def combine(high, low, returned):
    slots, row_count = high.shape
    features = returned.shape[1]
    return pl.pallas_call(
        combine_kernel,
        out_shape=jax.ShapeDtypeStruct((row_count, features), jnp.bfloat16),
        in_specs=[VMEM_SPEC] * 3,
        out_specs=VMEM_SPEC,
        compiler_params=pltpu.CompilerParams(vmem_limit_bytes=LIMIT),
        cost_estimate=pl.CostEstimate(
            flops=4 * row_count * slots * features, bytes_accessed=MIB, transcendentals=0
        ),
        name="combine",
    )(high, low, returned)


def fold_kernel(q_nope_ref, q_rope_ref, w_uk_ref, out_ref):
    latent_width = w_uk_ref.shape[0]
    for head in range(GROUP):
        columns = slice(head * NOPE, (head + 1) * NOPE)
        folded = lax.dot_general(
            q_nope_ref[:, columns], w_uk_ref[:, columns], NT, preferred_element_type=jnp.float32
        ).astype(jnp.bfloat16)
        rotated = q_rope_ref[:, head * ROPE : (head + 1) * ROPE]
        for run in range(2):
            rows = slice(run * HALF, (run + 1) * HALF)
            place = slice(head * HALF, (head + 1) * HALF)
            out_ref[run, place, :latent_width] = folded[rows]
            out_ref[run, place, latent_width:] = rotated[rows]


def fold(q_nope, q_rope, w_uk):
    query_count, columns = q_nope.shape
    heads = columns // NOPE
    latent_width = w_uk.shape[0]
    width = latent_width + ROPE
    return pl.pallas_call(
        fold_kernel,
        out_shape=jax.ShapeDtypeStruct((2, heads * HALF, width), jnp.bfloat16),
        grid=(heads // GROUP,),
        in_specs=[
            pl.BlockSpec((query_count, GROUP * NOPE), lambda step: (0, step)),
            pl.BlockSpec((query_count, GROUP * ROPE), lambda step: (0, step)),
            pl.BlockSpec((latent_width, GROUP * NOPE), lambda step: (0, step)),
        ],
        out_specs=pl.BlockSpec((2, GROUP * HALF, width), lambda step: (0, step, 0)),
        compiler_params=pltpu.CompilerParams(vmem_limit_bytes=FULL),
        cost_estimate=pl.CostEstimate(
            flops=2 * query_count * columns * latent_width,
            bytes_accessed=6 * MIB,
            transcendentals=0,
        ),
        name="fold",
    )(q_nope, q_rope, w_uk)


def attend_run(run, base, seen, queries_ref, keys_ref, w_uv_ref, w_uv_copy, store):
    latent_width = w_uv_ref.shape[0]
    heads = w_uv_ref.shape[1] // VDIM
    count = GROUP * HALF
    factor = math.log2(math.e) / math.sqrt(NOPE + ROPE)
    query_position = base + lax.rem(lax.broadcasted_iota(jnp.int32, (count, seen), 0), HALF)
    visible = lax.broadcasted_iota(jnp.int32, (count, seen), 1) <= query_position
    for group in range(heads // GROUP):
        scores = lax.dot_general(
            queries_ref[run, group * count : (group + 1) * count, :],
            keys_ref[:seen, :],
            NT,
            preferred_element_type=jnp.float32,
        )
        scores = jnp.where(visible, scores, -jnp.inf)
        top = jnp.max(scores, axis=1, keepdims=True)
        part = jnp.exp2((scores - top) * factor)
        total = jnp.sum(part, axis=1, keepdims=True)
        summed = jnp.dot(
            part.astype(jnp.bfloat16),
            keys_ref[:seen, :latent_width],
            preferred_element_type=jnp.float32,
        )
        mixed = (summed / total).astype(jnp.bfloat16)
        if not group:
            w_uv_copy.wait()
        for index in range(GROUP):
            head = group * GROUP + index
            columns = slice(head * VDIM, (head + 1) * VDIM)
            store(
                columns,
                jnp.dot(
                    mixed[index * HALF : (index + 1) * HALF],
                    w_uv_ref[:, columns],
                    preferred_element_type=jnp.float32,
                ).astype(jnp.bfloat16),
            )


def runs_of(my_ctx, positions_ref):
    first = my_ctx * (2 * HALF)
    low = jnp.where(positions_ref[first] < positions_ref[first + HALF], 0, 1)
    return low, positions_ref[first + low * HALF], positions_ref[first + (1 - low) * HALF]


def low_kernel(
    own_ref,
    positions_ref,
    queries_ref,
    w_uv_hbm,
    own_keys,
    core_own_keys,
    far_keys,
    core_far_keys,
    keys_ref,
    out_ref,
    w_uv_ref,
    semaphore,
):
    w_uv_copy = pltpu.make_async_copy(w_uv_hbm, w_uv_ref, semaphore)
    w_uv_copy.start()
    blocks, block_rows, width = own_keys.shape
    my_ctx, my_ep = own_ref[0], own_ref[1]
    for flip, source in enumerate((own_keys, core_own_keys, far_keys, core_far_keys)):
        for index in range(blocks):
            start = (index ^ my_ctx) * (4 * block_rows) + (my_ep ^ flip) * block_rows
            place = pl.multiple_of(positions_ref[start], block_rows)
            keys_ref[pl.ds(place, block_rows), :] = source[index]
    run, base, _ = runs_of(my_ctx, positions_ref)

    def store(columns, value):
        out_ref[:, columns] = value

    seen = keys_ref.shape[0] // 2
    attend_run(run, base, seen, queries_ref, keys_ref, w_uv_ref, w_uv_copy, store)


def high_kernel(
    own_ref,
    positions_ref,
    queries_ref,
    w_uv_hbm,
    keys_ref,
    low_ref,
    out_ref,
    w_uv_ref,
    semaphore,
):
    w_uv_copy = pltpu.make_async_copy(w_uv_hbm, w_uv_ref, semaphore)
    w_uv_copy.start()
    low, _, base = runs_of(own_ref[0], positions_ref)
    run = 1 - low
    out_ref[pl.ds(pl.multiple_of(low * HALF, HALF), HALF), :] = low_ref[...]
    rows = pl.ds(pl.multiple_of(run * HALF, HALF), HALF)

    def store(columns, value):
        out_ref[rows, columns] = value

    seen = keys_ref.shape[0]
    attend_run(run, base, seen, queries_ref, keys_ref, w_uv_ref, w_uv_copy, store)


def attend_low(own, positions, queries, w_uv, pieces):
    columns = w_uv.shape[1]
    key_count = positions.shape[0]
    width = pieces[0].shape[-1]
    count = queries.shape[1]
    return pl.pallas_call(
        low_kernel,
        out_shape=[
            jax.ShapeDtypeStruct((key_count, width), jnp.bfloat16),
            jax.ShapeDtypeStruct((HALF, columns), jnp.bfloat16),
        ],
        in_specs=[SMEM_SPEC] * 2 + [VMEM_SPEC, HBM_SPEC] + [VMEM_SPEC] * 4,
        out_specs=[VMEM_SPEC] * 2,
        scratch_shapes=[VMEM(w_uv.shape, jnp.bfloat16), pltpu.SemaphoreType.DMA(())],
        compiler_params=pltpu.CompilerParams(vmem_limit_bytes=LIMIT),
        cost_estimate=pl.CostEstimate(
            flops=2 * count * key_count * width,
            bytes_accessed=6 * MIB,
            transcendentals=count * key_count // 2,
        ),
        name="attention_low",
    )(own, positions, queries, w_uv, *pieces)


def attend_high(own, positions, queries, w_uv, keys, low):
    columns = w_uv.shape[1]
    key_count = positions.shape[0]
    width = keys.shape[1]
    count = queries.shape[1]
    return pl.pallas_call(
        high_kernel,
        out_shape=jax.ShapeDtypeStruct((2 * HALF, columns), jnp.bfloat16),
        in_specs=[SMEM_SPEC] * 2 + [VMEM_SPEC, HBM_SPEC] + [VMEM_SPEC] * 2,
        out_specs=VMEM_SPEC,
        scratch_shapes=[VMEM(w_uv.shape, jnp.bfloat16), pltpu.SemaphoreType.DMA(())],
        compiler_params=pltpu.CompilerParams(vmem_limit_bytes=LIMIT),
        cost_estimate=pl.CostEstimate(
            flops=4 * count * key_count * width,
            bytes_accessed=6 * MIB,
            transcendentals=count * key_count,
        ),
        name="attention_high",
    )(own, positions, queries, w_uv, keys, low)


def shards(
    q_nope,
    q_rope,
    latent,
    k_rope,
    w_uk,
    w_uv,
    positions,
    moe_rows,
    expert_ids,
    expert_weights,
    w_gate,
    w_up,
    w_down,
):
    ctx = lax.axis_size("ctx")
    me = lax.axis_index("ctx").astype(jnp.int32).reshape(1)
    ep = lax.axis_index("ep").astype(jnp.int32).reshape(1)

    def over_ctx(value, flip):
        return lax.ppermute(value, "ctx", [(i, i ^ flip) for i in range(ctx)])

    def over_ep(value, flip):
        return lax.ppermute(value, "ep", [(i, i ^ flip) for i in range(4)])

    def exchange(value):
        return lax.all_to_all(value, "ctx", split_axis=0, concat_axis=0, tiled=True)

    outgoing, high, low, packed = route(
        ep, expert_ids, expert_weights, k_rope, moe_rows, latent, ctx
    )
    arrived = exchange(outgoing)
    packed, q_nope = lax.optimization_barrier((packed, q_nope))
    queries = fold(q_nope, q_rope, w_uk)
    own_keys = packed[None]
    step = 1
    while step < ctx // 2:
        own_keys = jnp.concatenate([own_keys, over_ctx(own_keys, step)], axis=0)
        step *= 2
    arrived, queries, own_keys = lax.optimization_barrier((arrived, queries, own_keys))

    own = arrived.reshape(ctx * CAP, arrived.shape[2])
    far = over_ep(own, 2)
    core = over_ep(own, 1)
    gate_part, up_part = near_experts(ep, own, core, w_gate, w_up)
    received = over_ctx(own_keys, step)
    received, far, gate_part = lax.optimization_barrier((received, far, gate_part))
    core_far = over_ep(far, 1)
    own_keys = jnp.concatenate([own_keys, received], axis=0)
    far_keys = over_ep(own_keys, 2)
    own_out, core_out, far_out, core_far_out = far_experts(
        ep, far, core_far, gate_part, up_part, w_gate, w_up, w_down
    )
    from_core_far = over_ep(core_far_out, 1)
    from_core = over_ep(core_out, 1)
    core_own_keys = over_ep(own_keys, 1)
    from_core_far, far_keys = lax.optimization_barrier((from_core_far, far_keys))
    to_far = add(far_out, from_core_far)
    from_far = over_ep(to_far, 2)
    core_far_keys = over_ep(far_keys, 1)
    place = jnp.concatenate([me, ep])
    keys, low_out = attend_low(
        place, positions, queries, w_uv, (own_keys, core_own_keys, far_keys, core_far_keys)
    )
    from_far, keys, low_out = lax.optimization_barrier((from_far, keys, low_out))
    returning = add(own_out, from_core, from_far)
    returned = exchange(returning.reshape(arrived.shape))
    attention = attend_high(place, positions, queries, w_uv, keys, low_out)
    moe_out = combine(high, low, returned.reshape(own.shape))
    return (attention, moe_out)


def solution(mesh):
    return jax.shard_map(
        shards,
        mesh=mesh,
        in_specs=(
            P("ctx", "ep"),
            P("ctx", "ep"),
            P("ctx", None),
            P("ctx", None),
            P(None, "ep"),
            P(None, "ep"),
            P(),
            P("ctx", "ep"),
            P("ctx", None),
            P("ctx", None),
            P("ctx", None, "ep"),
            P("ctx", None, "ep"),
            P("ctx", "ep", None),
        ),
        out_specs=(P("ctx", "ep"), P("ctx", "ep")),
        check_vma=False,
    )
```

```python
import math

import jax
import jax.numpy as jnp
from jax import lax
from jax.experimental import pallas as pl
from jax.experimental.pallas import tpu as pltpu
from jax.sharding import PartitionSpec as P

NOPE = 128
ROPE = 64
VDIM = 128
TOP = 8
CAP = 8
HALF = 64
GROUP = 4
MIB = 1 << 20
LIMIT = 52 * MIB
FULL = 60 * MIB

NT = (((1,), (1,)), ((), ()))
TN = (((0,), (0,)), ((), ()))
VMEM = pltpu.VMEM
SMEM_SPEC = pl.BlockSpec(memory_space=pltpu.SMEM)
VMEM_SPEC = pl.BlockSpec(memory_space=pltpu.VMEM)
HBM_SPEC = pl.BlockSpec(memory_space=pltpu.HBM)


def gather_order(ctx):
    bits = ctx.bit_length() - 1
    return [1 << (bits - 1)] + [1 << bit for bit in range(bits - 1)]


def pack_kernel(ep_ref, latent_ref, rope_ref, packed_ref):
    latent_width = latent_ref.shape[1]
    rope = rope_ref[...].astype(jnp.float32).T
    for core in range(2):

        @pl.when(ep_ref[0] % 2 == core)
        def _():
            rows = slice(core * HALF, (core + 1) * HALF)
            packed_ref[:, :latent_width] = latent_ref[rows, :]
            packed_ref[:, latent_width:] = rope[rows].astype(jnp.bfloat16)


def pack(ep, latent, k_rope):
    return pl.pallas_call(
        pack_kernel,
        out_shape=jax.ShapeDtypeStruct((HALF, latent.shape[1] + ROPE), jnp.bfloat16),
        in_specs=[SMEM_SPEC] + [VMEM_SPEC] * 2,
        out_specs=VMEM_SPEC,
        compiler_params=pltpu.CompilerParams(vmem_limit_bytes=FULL),
        cost_estimate=pl.CostEstimate(flops=0, bytes_accessed=MIB // 4, transcendentals=0),
        name="pack",
    )(ep, latent, k_rope.T)


def route_kernel(ids_ref, weights_ref, rows_ref, sent_ref, high_ref, low_ref):
    row_count = ids_ref.shape[1]
    slots = sent_ref.shape[0] * CAP
    slot = lax.broadcasted_iota(jnp.int32, (slots, row_count), 0)
    expert = slot // CAP
    named = jnp.zeros((slots, row_count), jnp.float32)
    gate = jnp.zeros((slots, row_count), jnp.float32)
    for choice in range(TOP):
        match = ids_ref[choice : choice + 1, :] == expert
        named = jnp.where(match, 1.0, named)
        gate = jnp.where(match, weights_ref[choice : choice + 1, :], gate)
    row = lax.broadcasted_iota(jnp.int32, (row_count, row_count), 0)
    other = lax.broadcasted_iota(jnp.int32, (row_count, row_count), 1)
    before = jnp.where(row < other, 1.0, 0.0).astype(jnp.bfloat16)
    rank = jnp.dot(named.astype(jnp.bfloat16), before, preferred_element_type=jnp.float32)
    taken = (named > 0.0) & (rank == (slot % CAP).astype(jnp.float32))
    select = jnp.where(taken, 1.0, 0.0).astype(jnp.bfloat16)
    gate = jnp.where(taken, gate, 0.0)
    high = gate.astype(jnp.bfloat16)
    high_ref[...] = high
    low_ref[...] = (gate - high.astype(jnp.float32)).astype(jnp.bfloat16)
    sent = jnp.dot(select, rows_ref[...], preferred_element_type=jnp.float32)
    for index in range(slots // CAP):
        sent_ref[index] = sent[index * CAP : (index + 1) * CAP].astype(jnp.bfloat16)


def route(expert_ids, expert_weights, moe_rows, ctx):
    row_count, features = moe_rows.shape
    slots = ctx * CAP
    return pl.pallas_call(
        route_kernel,
        out_shape=[
            jax.ShapeDtypeStruct((ctx, CAP, features), jnp.bfloat16),
            jax.ShapeDtypeStruct((slots, row_count), jnp.bfloat16),
            jax.ShapeDtypeStruct((slots, row_count), jnp.bfloat16),
        ],
        in_specs=[VMEM_SPEC] * 3,
        out_specs=[VMEM_SPEC] * 3,
        compiler_params=pltpu.CompilerParams(vmem_limit_bytes=FULL),
        cost_estimate=pl.CostEstimate(
            flops=2 * row_count * slots * features, bytes_accessed=1 * MIB, transcendentals=0
        ),
        name="route",
    )(expert_ids.T, expert_weights.T, moe_rows)


def weight_copies(ep_ref, flips, gate_hbm, up_hbm, gate, up, semaphores):
    features = gate.shape[1]
    copies = []
    for index, flip in enumerate(flips):
        place = pl.multiple_of((ep_ref[0] ^ flip) * features, features)
        for which, (source, target) in enumerate(((gate_hbm, gate), (up_hbm, up))):
            copy = pltpu.make_async_copy(
                source.at[0, pl.ds(place, features)], target.at[index], semaphores.at[index, which]
            )
            copy.start()
            copies.append(copy)
    return copies


def near_kernel(
    ep_ref, own_ref, core_ref, gate_hbm, up_hbm, gate_out, up_out, gate, up, semaphores
):
    copies = weight_copies(ep_ref, (0, 1), gate_hbm, up_hbm, gate, up, semaphores)
    gate_sum, up_sum = None, None
    for index, x_ref in enumerate((own_ref, core_ref)):
        rows = x_ref[...]
        copies[2 * index].wait()
        part = jnp.dot(rows, gate[index], preferred_element_type=jnp.float32)
        gate_sum = part if gate_sum is None else gate_sum + part
        copies[2 * index + 1].wait()
        part = jnp.dot(rows, up[index], preferred_element_type=jnp.float32)
        up_sum = part if up_sum is None else up_sum + part
    gate_out[...] = gate_sum
    up_out[...] = up_sum


def near_experts(ep, own, core, w_gate, w_up):
    slots, features = own.shape
    units = w_gate.shape[2]
    return pl.pallas_call(
        near_kernel,
        out_shape=[jax.ShapeDtypeStruct((slots, units), jnp.float32)] * 2,
        in_specs=[SMEM_SPEC] + [VMEM_SPEC] * 2 + [HBM_SPEC] * 2,
        out_specs=[VMEM_SPEC] * 2,
        scratch_shapes=[
            VMEM((2, features, units), jnp.bfloat16),
            VMEM((2, features, units), jnp.bfloat16),
            pltpu.SemaphoreType.DMA((2, 2)),
        ],
        compiler_params=pltpu.CompilerParams(vmem_limit_bytes=LIMIT),
        cost_estimate=pl.CostEstimate(
            flops=8 * slots * features * units,
            bytes_accessed=8 * features * units,
            transcendentals=0,
        ),
        name="near_experts",
    )(ep, own, core, w_gate, w_up)


def far_kernel(
    ep_ref,
    far_ref,
    core_far_ref,
    gate_part,
    up_part,
    gate_hbm,
    up_hbm,
    down_hbm,
    own_out,
    core_out,
    far_out,
    core_far_out,
    gate,
    up,
    down,
    semaphores,
    down_semaphores,
):
    features = gate.shape[1]
    copies = weight_copies(ep_ref, (2, 3), gate_hbm, up_hbm, gate, up, semaphores)
    down_copies = []
    for flip in (3, 1, 2, 0):
        place = pl.multiple_of((ep_ref[0] ^ flip) * features, features)
        copy = pltpu.make_async_copy(
            down_hbm.at[0, :, pl.ds(place, features)], down.at[flip], down_semaphores.at[flip]
        )
        copy.start()
        down_copies.append(copy)
    gate_sum, up_sum = gate_part[...], up_part[...]
    for index, x_ref in enumerate((far_ref, core_far_ref)):
        rows = x_ref[...]
        copies[2 * index].wait()
        gate_sum = gate_sum + jnp.dot(rows, gate[index], preferred_element_type=jnp.float32)
        copies[2 * index + 1].wait()
        up_sum = up_sum + jnp.dot(rows, up[index], preferred_element_type=jnp.float32)
    hidden = (gate_sum / (1.0 + jnp.exp(-gate_sum)) * up_sum).astype(jnp.bfloat16)
    outs = (own_out, core_out, far_out, core_far_out)
    for copy, flip in zip(down_copies, (3, 1, 2, 0)):
        copy.wait()
        outs[flip][...] = jnp.dot(
            hidden, down[flip], preferred_element_type=jnp.float32
        ).astype(jnp.bfloat16)


def far_experts(ep, far, core_far, gate_part, up_part, w_gate, w_up, w_down):
    slots, features = far.shape
    units = w_gate.shape[2]
    return pl.pallas_call(
        far_kernel,
        out_shape=[jax.ShapeDtypeStruct((slots, features), jnp.bfloat16)] * 4,
        in_specs=[SMEM_SPEC] + [VMEM_SPEC] * 4 + [HBM_SPEC] * 3,
        out_specs=[VMEM_SPEC] * 4,
        scratch_shapes=[
            VMEM((2, features, units), jnp.bfloat16),
            VMEM((2, features, units), jnp.bfloat16),
            VMEM((4, units, features), jnp.bfloat16),
            pltpu.SemaphoreType.DMA((2, 2)),
            pltpu.SemaphoreType.DMA((4,)),
        ],
        compiler_params=pltpu.CompilerParams(vmem_limit_bytes=LIMIT),
        cost_estimate=pl.CostEstimate(
            flops=16 * slots * features * units,
            bytes_accessed=16 * features * units,
            transcendentals=slots * units,
        ),
        name="far_experts",
    )(ep, far, core_far, gate_part, up_part, w_gate, w_up, w_down)


def add_kernel(*refs):
    total = refs[0][...].astype(jnp.float32)
    for ref in refs[1:-1]:
        total = total + ref[...].astype(jnp.float32)
    refs[-1][...] = total.astype(jnp.bfloat16)


def add(*parts):
    return pl.pallas_call(
        add_kernel,
        out_shape=jax.ShapeDtypeStruct(parts[0].shape, jnp.bfloat16),
        in_specs=[VMEM_SPEC] * len(parts),
        out_specs=VMEM_SPEC,
        compiler_params=pltpu.CompilerParams(vmem_limit_bytes=8 * MIB),
        cost_estimate=pl.CostEstimate(flops=0, bytes_accessed=MIB, transcendentals=0),
        name="add",
    )(*parts)


def combine_kernel(high_ref, low_ref, returned_ref, out_ref):
    returned = returned_ref[...]
    total = lax.dot_general(high_ref[...], returned, TN, preferred_element_type=jnp.float32)
    total = total + lax.dot_general(
        low_ref[...], returned, TN, preferred_element_type=jnp.float32
    )
    out_ref[...] = total.astype(jnp.bfloat16)


def combine(high, low, returned):
    slots, row_count = high.shape
    features = returned.shape[1]
    return pl.pallas_call(
        combine_kernel,
        out_shape=jax.ShapeDtypeStruct((row_count, features), jnp.bfloat16),
        in_specs=[VMEM_SPEC] * 3,
        out_specs=VMEM_SPEC,
        compiler_params=pltpu.CompilerParams(vmem_limit_bytes=LIMIT),
        cost_estimate=pl.CostEstimate(
            flops=4 * row_count * slots * features, bytes_accessed=MIB, transcendentals=0
        ),
        name="combine",
    )(high, low, returned)


def fold_kernel(q_nope_ref, q_rope_ref, w_uk_ref, out_ref):
    latent_width = w_uk_ref.shape[0]
    for head in range(GROUP):
        columns = slice(head * NOPE, (head + 1) * NOPE)
        folded = lax.dot_general(
            q_nope_ref[:, columns], w_uk_ref[:, columns], NT, preferred_element_type=jnp.float32
        ).astype(jnp.bfloat16)
        rotated = q_rope_ref[:, head * ROPE : (head + 1) * ROPE]
        for run in range(2):
            rows = slice(run * HALF, (run + 1) * HALF)
            place = slice(head * HALF, (head + 1) * HALF)
            out_ref[run, place, :latent_width] = folded[rows]
            out_ref[run, place, latent_width:] = rotated[rows]


def fold(q_nope, q_rope, w_uk):
    query_count, columns = q_nope.shape
    heads = columns // NOPE
    latent_width = w_uk.shape[0]
    width = latent_width + ROPE
    return pl.pallas_call(
        fold_kernel,
        out_shape=jax.ShapeDtypeStruct((2, heads * HALF, width), jnp.bfloat16),
        grid=(heads // GROUP,),
        in_specs=[
            pl.BlockSpec((query_count, GROUP * NOPE), lambda step: (0, step)),
            pl.BlockSpec((query_count, GROUP * ROPE), lambda step: (0, step)),
            pl.BlockSpec((latent_width, GROUP * NOPE), lambda step: (0, step)),
        ],
        out_specs=pl.BlockSpec((2, GROUP * HALF, width), lambda step: (0, step, 0)),
        compiler_params=pltpu.CompilerParams(vmem_limit_bytes=FULL),
        cost_estimate=pl.CostEstimate(
            flops=2 * query_count * columns * latent_width,
            bytes_accessed=6 * MIB,
            transcendentals=0,
        ),
        name="fold",
    )(q_nope, q_rope, w_uk)


def attend_run(run, base, seen, queries_ref, keys_ref, w_uv_ref, w_uv_copy, store):
    latent_width = w_uv_ref.shape[0]
    heads = w_uv_ref.shape[1] // VDIM
    count = GROUP * HALF
    factor = math.log2(math.e) / math.sqrt(NOPE + ROPE)
    query_position = base + lax.rem(lax.broadcasted_iota(jnp.int32, (count, seen), 0), HALF)
    visible = lax.broadcasted_iota(jnp.int32, (count, seen), 1) <= query_position
    for group in range(heads // GROUP):
        scores = lax.dot_general(
            queries_ref[run, group * count : (group + 1) * count, :],
            keys_ref[:seen, :],
            NT,
            preferred_element_type=jnp.float32,
        )
        scores = jnp.where(visible, scores, -jnp.inf)
        top = jnp.max(scores, axis=1, keepdims=True)
        part = jnp.exp2((scores - top) * factor)
        total = jnp.sum(part, axis=1, keepdims=True)
        summed = jnp.dot(
            part.astype(jnp.bfloat16),
            keys_ref[:seen, :latent_width],
            preferred_element_type=jnp.float32,
        )
        mixed = (summed / total).astype(jnp.bfloat16)
        if not group:
            w_uv_copy.wait()
        for index in range(GROUP):
            head = group * GROUP + index
            columns = slice(head * VDIM, (head + 1) * VDIM)
            store(
                columns,
                jnp.dot(
                    mixed[index * HALF : (index + 1) * HALF],
                    w_uv_ref[:, columns],
                    preferred_element_type=jnp.float32,
                ).astype(jnp.bfloat16),
            )


def runs_of(my_ctx, positions_ref):
    first = my_ctx * (2 * HALF)
    low = jnp.where(positions_ref[first] < positions_ref[first + HALF], 0, 1)
    return low, positions_ref[first + low * HALF], positions_ref[first + (1 - low) * HALF]


def low_kernel(
    own_ref,
    positions_ref,
    queries_ref,
    w_uv_hbm,
    own_keys,
    core_keys,
    keys_ref,
    out_ref,
    w_uv_ref,
    semaphore,
):
    w_uv_copy = pltpu.make_async_copy(w_uv_hbm, w_uv_ref, semaphore)
    w_uv_copy.start()
    blocks, block_rows, width = own_keys.shape
    my_ctx, my_ep = own_ref[0], own_ref[1]
    for flip, source in enumerate((own_keys, core_keys)):
        for index in range(blocks):
            source_ctx = my_ctx
            for bit, step in enumerate(gather_order(blocks)):
                if index >> bit & 1:
                    source_ctx = source_ctx ^ step
            start = source_ctx * (2 * HALF) + ((my_ep % 2) ^ flip) * HALF
            place = pl.multiple_of(positions_ref[start], block_rows)
            keys_ref[pl.ds(place, block_rows), :] = source[index]
    run, base, _ = runs_of(my_ctx, positions_ref)

    def store(columns, value):
        out_ref[:, columns] = value

    seen = keys_ref.shape[0] // 2
    attend_run(run, base, seen, queries_ref, keys_ref, w_uv_ref, w_uv_copy, store)


def high_kernel(
    own_ref,
    positions_ref,
    queries_ref,
    w_uv_hbm,
    keys_ref,
    low_ref,
    out_ref,
    w_uv_ref,
    semaphore,
):
    w_uv_copy = pltpu.make_async_copy(w_uv_hbm, w_uv_ref, semaphore)
    w_uv_copy.start()
    low, _, base = runs_of(own_ref[0], positions_ref)
    run = 1 - low
    out_ref[pl.ds(pl.multiple_of(low * HALF, HALF), HALF), :] = low_ref[...]
    rows = pl.ds(pl.multiple_of(run * HALF, HALF), HALF)

    def store(columns, value):
        out_ref[rows, columns] = value

    seen = keys_ref.shape[0]
    attend_run(run, base, seen, queries_ref, keys_ref, w_uv_ref, w_uv_copy, store)


def attend_low(own, positions, queries, w_uv, pieces):
    columns = w_uv.shape[1]
    key_count = positions.shape[0]
    width = pieces[0].shape[-1]
    count = queries.shape[1]
    return pl.pallas_call(
        low_kernel,
        out_shape=[
            jax.ShapeDtypeStruct((key_count, width), jnp.bfloat16),
            jax.ShapeDtypeStruct((HALF, columns), jnp.bfloat16),
        ],
        in_specs=[SMEM_SPEC] * 2 + [VMEM_SPEC, HBM_SPEC] + [VMEM_SPEC] * 2,
        out_specs=[VMEM_SPEC] * 2,
        scratch_shapes=[VMEM(w_uv.shape, jnp.bfloat16), pltpu.SemaphoreType.DMA(())],
        compiler_params=pltpu.CompilerParams(vmem_limit_bytes=LIMIT),
        cost_estimate=pl.CostEstimate(
            flops=2 * count * key_count * width,
            bytes_accessed=6 * MIB,
            transcendentals=count * key_count // 2,
        ),
        name="attention_low",
    )(own, positions, queries, w_uv, *pieces)


def attend_high(own, positions, queries, w_uv, keys, low):
    columns = w_uv.shape[1]
    key_count = positions.shape[0]
    width = keys.shape[1]
    count = queries.shape[1]
    return pl.pallas_call(
        high_kernel,
        out_shape=jax.ShapeDtypeStruct((2 * HALF, columns), jnp.bfloat16),
        in_specs=[SMEM_SPEC] * 2 + [VMEM_SPEC, HBM_SPEC] + [VMEM_SPEC] * 2,
        out_specs=VMEM_SPEC,
        scratch_shapes=[VMEM(w_uv.shape, jnp.bfloat16), pltpu.SemaphoreType.DMA(())],
        compiler_params=pltpu.CompilerParams(vmem_limit_bytes=LIMIT),
        cost_estimate=pl.CostEstimate(
            flops=4 * count * key_count * width,
            bytes_accessed=6 * MIB,
            transcendentals=count * key_count,
        ),
        name="attention_high",
    )(own, positions, queries, w_uv, keys, low)


def shards(
    q_nope,
    q_rope,
    latent,
    k_rope,
    w_uk,
    w_uv,
    positions,
    moe_rows,
    expert_ids,
    expert_weights,
    w_gate,
    w_up,
    w_down,
):
    ctx = lax.axis_size("ctx")
    me = lax.axis_index("ctx").astype(jnp.int32).reshape(1)
    ep = lax.axis_index("ep").astype(jnp.int32).reshape(1)

    def over_ctx(value, flip):
        return lax.ppermute(value, "ctx", [(i, i ^ flip) for i in range(ctx)])

    def over_ep(value, flip):
        return lax.ppermute(value, "ep", [(i, i ^ flip) for i in range(4)])

    def exchange(value):
        return lax.all_to_all(value, "ctx", split_axis=0, concat_axis=0, tiled=True)

    packed = pack(ep, latent, k_rope)
    packed, moe_rows = lax.optimization_barrier((packed, moe_rows))
    outgoing, high, low = route(expert_ids, expert_weights, moe_rows, ctx)
    arrived = exchange(outgoing)
    high, q_nope = lax.optimization_barrier((high, q_nope))
    queries = fold(q_nope, q_rope, w_uk)
    own_keys = packed[None]
    flips = gather_order(ctx)
    for flip in flips[:-1]:
        own_keys = jnp.concatenate([own_keys, over_ctx(own_keys, flip)], axis=0)
    arrived, queries, own_keys = lax.optimization_barrier((arrived, queries, own_keys))

    own = arrived.reshape(ctx * CAP, arrived.shape[2])
    far = over_ep(own, 2)
    core = over_ep(own, 1)
    received = over_ctx(own_keys, flips[-1])
    gate_part, up_part = near_experts(ep, own, core, w_gate, w_up)
    far, gate_part = lax.optimization_barrier((far, gate_part))
    core_far = over_ep(far, 1)
    core_far, received = lax.optimization_barrier((core_far, received))
    own_out, core_out, far_out, core_far_out = far_experts(
        ep, far, core_far, gate_part, up_part, w_gate, w_up, w_down
    )
    from_core_far = over_ep(core_far_out, 1)
    from_core = over_ep(core_out, 1)
    own_keys = jnp.concatenate([own_keys, received], axis=0)
    core_keys = over_ep(own_keys, 1)
    to_far = add(far_out, from_core_far)
    from_far = over_ep(to_far, 2)
    place = jnp.concatenate([me, ep])
    keys, low_out = attend_low(place, positions, queries, w_uv, (own_keys, core_keys))
    from_far, keys, low_out = lax.optimization_barrier((from_far, keys, low_out))
    returning = add(own_out, from_core, from_far)
    returned = exchange(returning.reshape(arrived.shape))
    attention = attend_high(place, positions, queries, w_uv, keys, low_out)
    moe_out = combine(high, low, returned.reshape(own.shape))
    return (attention, moe_out)


def solution(mesh):
    return jax.shard_map(
        shards,
        mesh=mesh,
        in_specs=(
            P("ctx", "ep"),
            P("ctx", "ep"),
            P("ctx", None),
            P("ctx", None),
            P(None, "ep"),
            P(None, "ep"),
            P(),
            P("ctx", "ep"),
            P("ctx", None),
            P("ctx", None),
            P("ctx", None, "ep"),
            P("ctx", None, "ep"),
            P("ctx", "ep", None),
        ),
        out_specs=(P("ctx", "ep"), P("ctx", "ep")),
        check_vma=False,
    )
```

```python
import functools
import math

import jax
import jax.numpy as jnp
from jax import lax
from jax.experimental import pallas as pl
from jax.experimental.pallas import tpu as pltpu
from jax.sharding import PartitionSpec as P

NOPE = 128
ROPE = 64
VDIM = 128
TOP = 8
CAP = 8
HALF = 64
GROUP = 4
MIB = 1 << 20
LIMIT = 52 * MIB
FULL = 60 * MIB
SMALL = 24 * MIB
CHUNK = 256

NT = (((1,), (1,)), ((), ()))
TN = (((0,), (0,)), ((), ()))
VMEM = pltpu.VMEM
SMEM_SPEC = pl.BlockSpec(memory_space=pltpu.SMEM)
VMEM_SPEC = pl.BlockSpec(memory_space=pltpu.VMEM)
HBM_SPEC = pl.BlockSpec(memory_space=pltpu.HBM)


def gather_order(ctx):
    bits = ctx.bit_length() - 1
    return [1 << (bits - 1)] + [1 << bit for bit in range(bits - 1)]


def pack_kernel(ep_ref, latent_ref, rope_ref, packed_ref):
    latent_width = latent_ref.shape[1]
    rope = rope_ref[...].astype(jnp.float32).T
    for core in range(2):

        @pl.when(ep_ref[0] % 2 == core)
        def _():
            rows = slice(core * HALF, (core + 1) * HALF)
            packed_ref[:, :latent_width] = latent_ref[rows, :]
            packed_ref[:, latent_width:] = rope[rows].astype(jnp.bfloat16)


def pack(ep, latent, k_rope):
    return pl.pallas_call(
        pack_kernel,
        out_shape=jax.ShapeDtypeStruct((HALF, latent.shape[1] + ROPE), jnp.bfloat16),
        in_specs=[SMEM_SPEC] + [VMEM_SPEC] * 2,
        out_specs=VMEM_SPEC,
        compiler_params=pltpu.CompilerParams(vmem_limit_bytes=FULL),
        cost_estimate=pl.CostEstimate(flops=0, bytes_accessed=MIB // 4, transcendentals=0),
        name="pack",
    )(ep, latent, k_rope.T)


def route_kernel(ids_ref, weights_ref, rows_ref, sent_ref, high_ref, low_ref):
    row_count = ids_ref.shape[1]
    slots = sent_ref.shape[0] * CAP
    slot = lax.broadcasted_iota(jnp.int32, (slots, row_count), 0)
    expert = slot // CAP
    named = jnp.zeros((slots, row_count), jnp.float32)
    gate = jnp.zeros((slots, row_count), jnp.float32)
    for choice in range(TOP):
        match = ids_ref[choice : choice + 1, :] == expert
        named = jnp.where(match, 1.0, named)
        gate = jnp.where(match, weights_ref[choice : choice + 1, :], gate)
    row = lax.broadcasted_iota(jnp.int32, (row_count, row_count), 0)
    other = lax.broadcasted_iota(jnp.int32, (row_count, row_count), 1)
    before = jnp.where(row < other, 1.0, 0.0).astype(jnp.bfloat16)
    rank = jnp.dot(named.astype(jnp.bfloat16), before, preferred_element_type=jnp.float32)
    taken = (named > 0.0) & (rank == (slot % CAP).astype(jnp.float32))
    select = jnp.where(taken, 1.0, 0.0).astype(jnp.bfloat16)
    gate = jnp.where(taken, gate, 0.0)
    high = gate.astype(jnp.bfloat16)
    high_ref[...] = high
    low_ref[...] = (gate - high.astype(jnp.float32)).astype(jnp.bfloat16)
    sent = jnp.dot(select, rows_ref[...], preferred_element_type=jnp.float32)
    for index in range(slots // CAP):
        sent_ref[index] = sent[index * CAP : (index + 1) * CAP].astype(jnp.bfloat16)


def route(expert_ids, expert_weights, moe_rows, ctx):
    row_count, features = moe_rows.shape
    slots = ctx * CAP
    return pl.pallas_call(
        route_kernel,
        out_shape=[
            jax.ShapeDtypeStruct((ctx, CAP, features), jnp.bfloat16),
            jax.ShapeDtypeStruct((slots, row_count), jnp.bfloat16),
            jax.ShapeDtypeStruct((slots, row_count), jnp.bfloat16),
        ],
        in_specs=[VMEM_SPEC] * 3,
        out_specs=[VMEM_SPEC] * 3,
        compiler_params=pltpu.CompilerParams(vmem_limit_bytes=FULL),
        cost_estimate=pl.CostEstimate(
            flops=2 * row_count * slots * features, bytes_accessed=1 * MIB, transcendentals=0
        ),
        name="route",
    )(expert_ids.T, expert_weights.T, moe_rows)


def weight_copies(ep_ref, flips, gate_hbm, up_hbm, gate, up, semaphores):
    features = gate.shape[1]
    copies = []
    for index, flip in enumerate(flips):
        place = pl.multiple_of((ep_ref[0] ^ flip) * features, features)
        for which, (source, target) in enumerate(((gate_hbm, gate), (up_hbm, up))):
            copy = pltpu.make_async_copy(
                source.at[0, pl.ds(place, features)], target.at[index], semaphores.at[index, which]
            )
            copy.start()
            copies.append(copy)
    return copies


def near_kernel(
    ep_ref,
    own_ref,
    core_ref,
    gate_hbm,
    up_hbm,
    down_hbm,
    sums_out,
    far_gate,
    far_up,
    down,
    gate,
    up,
    semaphores,
    far_semaphores,
    down_semaphores,
):
    units = gate.shape[2]
    features = gate.shape[1]
    copies = weight_copies(ep_ref, (0, 1), gate_hbm, up_hbm, gate, up, semaphores)
    later = weight_copies(ep_ref, (2, 3), gate_hbm, up_hbm, far_gate, far_up, far_semaphores)
    for flip in (3, 1, 2, 0):
        place = pl.multiple_of((ep_ref[0] ^ flip) * features, features)
        copy = pltpu.make_async_copy(
            down_hbm.at[0, :, pl.ds(place, features)], down.at[flip], down_semaphores.at[flip]
        )
        copy.start()
        later.append(copy)
    gate_sum, up_sum = None, None
    for index, x_ref in enumerate((own_ref, core_ref)):
        rows = x_ref[...]
        copies[2 * index].wait()
        part = jnp.dot(rows, gate[index], preferred_element_type=jnp.float32)
        gate_sum = part if gate_sum is None else gate_sum + part
        copies[2 * index + 1].wait()
        part = jnp.dot(rows, up[index], preferred_element_type=jnp.float32)
        up_sum = part if up_sum is None else up_sum + part
    sums_out[:, :units] = gate_sum
    sums_out[:, units:] = up_sum
    for copy in later:
        copy.wait()


def near_experts(ep, own, core, w_gate, w_up, w_down):
    slots, features = own.shape
    units = w_gate.shape[2]
    return pl.pallas_call(
        near_kernel,
        out_shape=[
            jax.ShapeDtypeStruct((slots, 2 * units), jnp.float32),
            jax.ShapeDtypeStruct((2, features, units), jnp.bfloat16),
            jax.ShapeDtypeStruct((2, features, units), jnp.bfloat16),
            jax.ShapeDtypeStruct((4, units, features), jnp.bfloat16),
        ],
        in_specs=[SMEM_SPEC] + [VMEM_SPEC] * 2 + [HBM_SPEC] * 3,
        out_specs=[VMEM_SPEC] * 4,
        scratch_shapes=[
            VMEM((2, features, units), jnp.bfloat16),
            VMEM((2, features, units), jnp.bfloat16),
            pltpu.SemaphoreType.DMA((2, 2)),
            pltpu.SemaphoreType.DMA((2, 2)),
            pltpu.SemaphoreType.DMA((4,)),
        ],
        compiler_params=pltpu.CompilerParams(vmem_limit_bytes=46 * MIB),
        cost_estimate=pl.CostEstimate(
            flops=8 * slots * features * units,
            bytes_accessed=24 * features * units,
            transcendentals=0,
        ),
        name="near_experts",
    )(ep, own, core, w_gate, w_up, w_down)


def far_kernel(
    far_ref, core_far_ref, sums_ref, gate, up, down, own_out, core_out, far_out, core_far_out
):
    units = gate.shape[2]
    gate_sum, up_sum = sums_ref[:, :units], sums_ref[:, units:]
    for index, x_ref in enumerate((far_ref, core_far_ref)):
        rows = x_ref[...]
        gate_sum = gate_sum + jnp.dot(rows, gate[index], preferred_element_type=jnp.float32)
        up_sum = up_sum + jnp.dot(rows, up[index], preferred_element_type=jnp.float32)
    hidden = (gate_sum / (1.0 + jnp.exp(-gate_sum)) * up_sum).astype(jnp.bfloat16)
    outs = (own_out, core_out, far_out, core_far_out)
    for flip in (3, 1, 2, 0):
        outs[flip][...] = jnp.dot(
            hidden, down[flip], preferred_element_type=jnp.float32
        ).astype(jnp.bfloat16)


def far_experts(far, core_far, sums, gate, up, down):
    slots, features = far.shape
    units = gate.shape[2]
    return pl.pallas_call(
        far_kernel,
        out_shape=[jax.ShapeDtypeStruct((slots, features), jnp.bfloat16)] * 4,
        in_specs=[VMEM_SPEC] * 6,
        out_specs=[VMEM_SPEC] * 4,
        compiler_params=pltpu.CompilerParams(vmem_limit_bytes=SMALL),
        cost_estimate=pl.CostEstimate(flops=0, bytes_accessed=0, transcendentals=0),
        name="far_experts",
    )(far, core_far, sums, gate, up, down)


def add_kernel(*refs):
    total = refs[0][...].astype(jnp.float32)
    for ref in refs[1:-1]:
        total = total + ref[...].astype(jnp.float32)
    refs[-1][...] = total.astype(jnp.bfloat16)


def add(*parts):
    return pl.pallas_call(
        add_kernel,
        out_shape=jax.ShapeDtypeStruct(parts[0].shape, jnp.bfloat16),
        in_specs=[VMEM_SPEC] * len(parts),
        out_specs=VMEM_SPEC,
        compiler_params=pltpu.CompilerParams(vmem_limit_bytes=8 * MIB),
        cost_estimate=pl.CostEstimate(flops=0, bytes_accessed=MIB, transcendentals=0),
        name="add",
    )(*parts)


def combine_kernel(high_ref, low_ref, returned_ref, out_ref):
    returned = returned_ref[...]
    total = lax.dot_general(high_ref[...], returned, TN, preferred_element_type=jnp.float32)
    total = total + lax.dot_general(
        low_ref[...], returned, TN, preferred_element_type=jnp.float32
    )
    out_ref[...] = total.astype(jnp.bfloat16)


def combine(high, low, returned):
    slots, row_count = high.shape
    features = returned.shape[1]
    return pl.pallas_call(
        combine_kernel,
        out_shape=jax.ShapeDtypeStruct((row_count, features), jnp.bfloat16),
        in_specs=[VMEM_SPEC] * 3,
        out_specs=VMEM_SPEC,
        compiler_params=pltpu.CompilerParams(vmem_limit_bytes=LIMIT),
        cost_estimate=pl.CostEstimate(
            flops=4 * row_count * slots * features, bytes_accessed=MIB, transcendentals=0
        ),
        name="combine",
    )(high, low, returned)


def fold_kernel(q_nope_ref, q_rope_ref, w_uk_ref, out_ref):
    latent_width = w_uk_ref.shape[0]
    for head in range(GROUP):
        columns = slice(head * NOPE, (head + 1) * NOPE)
        folded = lax.dot_general(
            q_nope_ref[:, columns], w_uk_ref[:, columns], NT, preferred_element_type=jnp.float32
        ).astype(jnp.bfloat16)
        rotated = q_rope_ref[:, head * ROPE : (head + 1) * ROPE]
        for run in range(2):
            rows = slice(run * HALF, (run + 1) * HALF)
            place = slice(head * HALF, (head + 1) * HALF)
            out_ref[run, place, :latent_width] = folded[rows]
            out_ref[run, place, latent_width:] = rotated[rows]


def fold(q_nope, q_rope, w_uk):
    query_count, columns = q_nope.shape
    heads = columns // NOPE
    latent_width = w_uk.shape[0]
    width = latent_width + ROPE
    return pl.pallas_call(
        fold_kernel,
        out_shape=jax.ShapeDtypeStruct((2, heads * HALF, width), jnp.bfloat16),
        grid=(heads // GROUP,),
        in_specs=[
            pl.BlockSpec((query_count, GROUP * NOPE), lambda step: (0, step)),
            pl.BlockSpec((query_count, GROUP * ROPE), lambda step: (0, step)),
            pl.BlockSpec((latent_width, GROUP * NOPE), lambda step: (0, step)),
        ],
        out_specs=pl.BlockSpec((2, GROUP * HALF, width), lambda step: (0, step, 0)),
        compiler_params=pltpu.CompilerParams(vmem_limit_bytes=FULL),
        cost_estimate=pl.CostEstimate(
            flops=2 * query_count * columns * latent_width,
            bytes_accessed=6 * MIB,
            transcendentals=0,
        ),
        name="fold",
    )(q_nope, q_rope, w_uk)


def attention_kernel(
    first,
    last,
    own_ref,
    positions_ref,
    queries_hbm,
    w_uv_hbm,
    own_keys,
    core_keys,
    *refs,
):
    done_ref = None
    if first:
        done_ref, *refs = refs
    out_ref, keys, queries, w_uv, scores, tops, mixed, semaphores = refs
    latent_width = w_uv.shape[0]
    count = (last - first) * HALF
    blocks = own_keys.shape[0]
    my_ctx, my_ep = own_ref[0], own_ref[1]
    mine = my_ctx * (2 * HALF)
    low = jnp.where(positions_ref[mine] < positions_ref[mine + HALF], 0, 1)
    high = 1 - low
    low_base = positions_ref[mine + low * HALF]
    high_base = positions_ref[mine + high * HALF]
    copies = []

    def copy(source, target):
        copies.append(pltpu.make_async_copy(source, target, semaphores.at[len(copies)]))
        copies[-1].start()

    copy(queries_hbm.at[high, pl.ds(first * HALF, count)], queries.at[pl.ds(0, count)])
    copy(queries_hbm.at[low, pl.ds(first * HALF, count)], queries.at[pl.ds(count, count)])
    for flip, source in enumerate((own_keys, core_keys)):
        for index in range(blocks):
            source_ctx = my_ctx
            for bit, step in enumerate(gather_order(blocks)):
                if index >> bit & 1:
                    source_ctx = source_ctx ^ step
            start = source_ctx * (2 * HALF) + ((my_ep % 2) ^ flip) * HALF
            place = pl.multiple_of(positions_ref[start], HALF)
            copy(source.at[index], keys.at[pl.ds(place, HALF)])
    copy(w_uv_hbm.at[:, pl.ds(first * VDIM, (last - first) * VDIM)], w_uv)
    tops[...] = jnp.full(tops.shape, -jnp.inf, jnp.float32)
    offset = lax.broadcasted_iota(jnp.int32, (HALF, CHUNK), 1) - lax.broadcasted_iota(
        jnp.int32, (HALF, CHUNK), 0
    )
    for pending in copies[:-1]:
        pending.wait()
    low_chunks = (low_base + HALF + CHUNK - 1) // CHUNK
    high_chunks = (high_base + HALF + CHUNK - 1) // CHUNK

    def score(chunk, bases):
        start = pl.multiple_of(chunk * CHUNK, CHUNK)
        part = lax.dot_general(
            queries[: len(bases) * count, :],
            keys[pl.ds(start, CHUNK), :],
            NT,
            preferred_element_type=jnp.float32,
        )
        for index, base in enumerate(bases):
            visible = offset <= base - start
            for head in range(last - first):
                rows = slice(index * count + head * HALF, index * count + (head + 1) * HALF)
                seen = jnp.where(visible, part[rows], -jnp.inf)
                scores[chunk, rows, :] = seen
                top = tops[rows, :]
                for lane in range(0, CHUNK, 128):
                    top = jnp.maximum(top, seen[:, lane : lane + 128])
                tops[rows, :] = top
        return 0

    lax.fori_loop(0, low_chunks, lambda c, _: score(c, (high_base, low_base)), 0)
    lax.fori_loop(low_chunks, high_chunks, lambda c, _: score(c, (high_base,)), 0)
    factor = math.log2(math.e) / math.sqrt(NOPE + ROPE)

    def mix(rows, chunks):
        top = jnp.max(tops[rows, :], axis=1, keepdims=True) * factor
        total = jnp.zeros((count, 128), jnp.float32)
        parts = []
        for chunk in range(chunks):
            part = jnp.exp2(scores[chunk, rows, :] * factor - top)
            for lane in range(0, CHUNK, 128):
                total = total + part[:, lane : lane + 128]
            parts.append(part.astype(jnp.bfloat16))
        summed = jnp.dot(
            jnp.concatenate(parts, axis=1),
            keys[: chunks * CHUNK, :latent_width],
            preferred_element_type=jnp.float32,
        )
        share = 1.0 / jnp.sum(total, axis=1, keepdims=True)
        mixed[rows, :] = (summed * share).astype(jnp.bfloat16)

    most = keys.shape[0] // CHUNK
    for chunks in range(1, most + 1):

        @pl.when(high_chunks == chunks)
        def _():
            mix(slice(0, count), chunks)

        @pl.when(low_chunks == chunks)
        def _():
            mix(slice(count, 2 * count), chunks)

    copies[-1].wait()
    high_rows = pl.ds(pl.multiple_of(high * HALF, HALF), HALF)
    low_rows = pl.ds(pl.multiple_of(low * HALF, HALF), HALF)
    if first:
        out_ref[:, : first * VDIM] = done_ref[...]
    skipped = first * VDIM
    for head in range(last - first):
        both = jnp.concatenate(
            [
                mixed[head * HALF : (head + 1) * HALF, :],
                mixed[count + head * HALF : count + (head + 1) * HALF, :],
            ],
            axis=0,
        )
        value = jnp.dot(
            both, w_uv[:, head * VDIM : (head + 1) * VDIM], preferred_element_type=jnp.float32
        ).astype(jnp.bfloat16)
        columns = slice(skipped + head * VDIM, skipped + (head + 1) * VDIM)
        out_ref[high_rows, columns] = value[:HALF]
        out_ref[low_rows, columns] = value[HALF:]


def attend(first, last, own, positions, queries, w_uv, own_keys, core_keys, *done):
    latent_width = w_uv.shape[0]
    key_count = positions.shape[0]
    width = own_keys.shape[-1]
    count = (last - first) * HALF
    return pl.pallas_call(
        functools.partial(attention_kernel, first, last),
        out_shape=jax.ShapeDtypeStruct((2 * HALF, last * VDIM), jnp.bfloat16),
        in_specs=[SMEM_SPEC] * 2 + [HBM_SPEC] * 4 + [VMEM_SPEC] * len(done),
        out_specs=VMEM_SPEC,
        scratch_shapes=[
            VMEM((key_count, width), jnp.bfloat16),
            VMEM((2 * count, width), jnp.bfloat16),
            VMEM((latent_width, (last - first) * VDIM), jnp.bfloat16),
            VMEM((key_count // CHUNK, 2 * count, CHUNK), jnp.float32),
            VMEM((2 * count, 128), jnp.float32),
            VMEM((2 * count, latent_width), jnp.bfloat16),
            pltpu.SemaphoreType.DMA((2 * own_keys.shape[0] + 3,)),
        ],
        compiler_params=pltpu.CompilerParams(vmem_limit_bytes=LIMIT),
        cost_estimate=pl.CostEstimate(
            flops=3 * count * key_count * width,
            bytes_accessed=4 * MIB,
            transcendentals=count * key_count,
        ),
        name="attention",
    )(own, positions, queries, w_uv, own_keys, core_keys, *done)


def shards(
    q_nope,
    q_rope,
    latent,
    k_rope,
    w_uk,
    w_uv,
    positions,
    moe_rows,
    expert_ids,
    expert_weights,
    w_gate,
    w_up,
    w_down,
):
    ctx = lax.axis_size("ctx")
    me = lax.axis_index("ctx").astype(jnp.int32).reshape(1)
    ep = lax.axis_index("ep").astype(jnp.int32).reshape(1)

    def over_ctx(value, flip):
        return lax.ppermute(value, "ctx", [(i, i ^ flip) for i in range(ctx)])

    def over_ep(value, flip):
        return lax.ppermute(value, "ep", [(i, i ^ flip) for i in range(4)])

    def exchange(value):
        return lax.all_to_all(value, "ctx", split_axis=0, concat_axis=0, tiled=True)

    packed = pack(ep, latent, k_rope)
    packed, moe_rows = lax.optimization_barrier((packed, moe_rows))
    outgoing, high, low = route(expert_ids, expert_weights, moe_rows, ctx)
    arrived = exchange(outgoing)
    high, q_nope = lax.optimization_barrier((high, q_nope))
    queries = fold(q_nope, q_rope, w_uk)
    flips = gather_order(ctx)
    own_keys = packed[None]
    for flip in flips[:-1]:
        own_keys = jnp.concatenate([own_keys, over_ctx(own_keys, flip)], axis=0)
    arrived, queries, own_keys = lax.optimization_barrier((arrived, queries, own_keys))

    own = arrived.reshape(ctx * CAP, arrived.shape[2])
    far = over_ep(own, 2)
    core = over_ep(own, 1)
    received = over_ctx(own_keys, flips[-1])
    sums, far_gate, far_up, down = near_experts(ep, own, core, w_gate, w_up, w_down)
    far, sums = lax.optimization_barrier((far, sums))
    core_far = over_ep(far, 1)
    own_out, core_out, far_out, core_far_out = far_experts(
        far, core_far, sums, far_gate, far_up, down
    )
    core_far_out, received = lax.optimization_barrier((core_far_out, received))
    from_core_far = over_ep(core_far_out, 1)
    from_core = over_ep(core_out, 1)
    to_far = add(far_out, from_core_far)
    from_far = over_ep(to_far, 2)
    own_keys = jnp.concatenate([own_keys, received], axis=0)
    core_keys = over_ep(own_keys, 1)
    place = jnp.concatenate([me, ep])
    heads = q_nope.shape[1] // NOPE
    split = heads // 2
    half = attend(0, split, place, positions, queries, w_uv, own_keys, core_keys)
    from_far, half = lax.optimization_barrier((from_far, half))
    returning = add(own_out, from_core, from_far)
    returned = exchange(returning.reshape(arrived.shape))
    attention = attend(
        split, heads, place, positions, queries, w_uv, own_keys, core_keys, half
    )
    moe_out = combine(high, low, returned.reshape(own.shape))
    return (attention, moe_out)


def solution(mesh):
    return jax.shard_map(
        shards,
        mesh=mesh,
        in_specs=(
            P("ctx", "ep"),
            P("ctx", "ep"),
            P("ctx", None),
            P("ctx", None),
            P(None, "ep"),
            P(None, "ep"),
            P(),
            P("ctx", "ep"),
            P("ctx", None),
            P("ctx", None),
            P("ctx", None, "ep"),
            P("ctx", None, "ep"),
            P("ctx", "ep", None),
        ),
        out_specs=(P("ctx", "ep"), P("ctx", "ep")),
        check_vma=False,
    )
```

```python
import functools
import math

import jax
import jax.numpy as jnp
from jax import lax
from jax.experimental import pallas as pl
from jax.experimental.pallas import tpu as pltpu
from jax.sharding import PartitionSpec as P

NOPE = 128
ROPE = 64
VDIM = 128
TOP = 8
CAP = 8
HALF = 64
GROUP = 4
MIB = 1 << 20
LIMIT = 52 * MIB
FULL = 60 * MIB
SMALL = 24 * MIB
CHUNK = 256

NT = (((1,), (1,)), ((), ()))
TN = (((0,), (0,)), ((), ()))
VMEM = pltpu.VMEM
SMEM_SPEC = pl.BlockSpec(memory_space=pltpu.SMEM)
VMEM_SPEC = pl.BlockSpec(memory_space=pltpu.VMEM)
HBM_SPEC = pl.BlockSpec(memory_space=pltpu.HBM)


def gather_order(ctx):
    bits = ctx.bit_length() - 1
    return [1 << (bits - 1)] + [1 << bit for bit in range(bits - 1)]


def route_kernel(
    ep_ref,
    ids_ref,
    weights_ref,
    rope_ref,
    rows_ref,
    latent_ref,
    sent_ref,
    high_ref,
    low_ref,
    packed_ref,
):
    latent_width = latent_ref.shape[1]
    rope = rope_ref[...].astype(jnp.float32).T
    for core in range(2):

        @pl.when(ep_ref[0] % 2 == core)
        def _():
            rows = slice(core * HALF, (core + 1) * HALF)
            packed_ref[:, :latent_width] = latent_ref[rows, :]
            packed_ref[:, latent_width:] = rope[rows].astype(jnp.bfloat16)

    row_count = ids_ref.shape[1]
    slots = sent_ref.shape[0] * CAP
    slot = lax.broadcasted_iota(jnp.int32, (slots, row_count), 0)
    expert = slot // CAP
    named = jnp.zeros((slots, row_count), jnp.float32)
    gate = jnp.zeros((slots, row_count), jnp.float32)
    for choice in range(TOP):
        match = ids_ref[choice : choice + 1, :] == expert
        named = jnp.where(match, 1.0, named)
        gate = jnp.where(match, weights_ref[choice : choice + 1, :], gate)
    row = lax.broadcasted_iota(jnp.int32, (row_count, row_count), 0)
    other = lax.broadcasted_iota(jnp.int32, (row_count, row_count), 1)
    before = jnp.where(row < other, 1.0, 0.0).astype(jnp.bfloat16)
    rank = jnp.dot(named.astype(jnp.bfloat16), before, preferred_element_type=jnp.float32)
    taken = (named > 0.0) & (rank == (slot % CAP).astype(jnp.float32))
    select = jnp.where(taken, 1.0, 0.0).astype(jnp.bfloat16)
    gate = jnp.where(taken, gate, 0.0)
    high = gate.astype(jnp.bfloat16)
    high_ref[...] = high
    low_ref[...] = (gate - high.astype(jnp.float32)).astype(jnp.bfloat16)
    sent = jnp.dot(select, rows_ref[...], preferred_element_type=jnp.float32)
    for index in range(slots // CAP):
        sent_ref[index] = sent[index * CAP : (index + 1) * CAP].astype(jnp.bfloat16)


def route(ep, expert_ids, expert_weights, k_rope, moe_rows, latent, ctx):
    row_count, features = moe_rows.shape
    slots = ctx * CAP
    return pl.pallas_call(
        route_kernel,
        out_shape=[
            jax.ShapeDtypeStruct((ctx, CAP, features), jnp.bfloat16),
            jax.ShapeDtypeStruct((slots, row_count), jnp.bfloat16),
            jax.ShapeDtypeStruct((slots, row_count), jnp.bfloat16),
            jax.ShapeDtypeStruct((HALF, latent.shape[1] + ROPE), jnp.bfloat16),
        ],
        in_specs=[SMEM_SPEC] + [VMEM_SPEC] * 5,
        out_specs=[VMEM_SPEC] * 4,
        compiler_params=pltpu.CompilerParams(vmem_limit_bytes=FULL),
        cost_estimate=pl.CostEstimate(
            flops=2 * row_count * slots * features, bytes_accessed=1 * MIB, transcendentals=0
        ),
        name="route",
    )(ep, expert_ids.T, expert_weights.T, k_rope.T, moe_rows, latent)


def weight_copies(ep_ref, flips, gate_hbm, up_hbm, gate, up, semaphores):
    features = gate.shape[1]
    copies = []
    for index, flip in enumerate(flips):
        place = pl.multiple_of((ep_ref[0] ^ flip) * features, features)
        for which, (source, target) in enumerate(((gate_hbm, gate), (up_hbm, up))):
            copy = pltpu.make_async_copy(
                source.at[0, pl.ds(place, features)], target.at[index], semaphores.at[index, which]
            )
            copy.start()
            copies.append(copy)
    return copies


def near_kernel(
    ep_ref,
    own_ref,
    core_ref,
    gate_hbm,
    up_hbm,
    down_hbm,
    sums_out,
    far_gate,
    far_up,
    down,
    gate,
    up,
    semaphores,
    far_semaphores,
    down_semaphores,
):
    units = gate.shape[2]
    features = gate.shape[1]
    copies = weight_copies(ep_ref, (0, 1), gate_hbm, up_hbm, gate, up, semaphores)
    later = weight_copies(ep_ref, (2, 3), gate_hbm, up_hbm, far_gate, far_up, far_semaphores)
    for flip in (3, 1, 2, 0):
        place = pl.multiple_of((ep_ref[0] ^ flip) * features, features)
        copy = pltpu.make_async_copy(
            down_hbm.at[0, :, pl.ds(place, features)], down.at[flip], down_semaphores.at[flip]
        )
        copy.start()
        later.append(copy)
    gate_sum, up_sum = None, None
    for index, x_ref in enumerate((own_ref, core_ref)):
        rows = x_ref[...]
        copies[2 * index].wait()
        part = jnp.dot(rows, gate[index], preferred_element_type=jnp.float32)
        gate_sum = part if gate_sum is None else gate_sum + part
        copies[2 * index + 1].wait()
        part = jnp.dot(rows, up[index], preferred_element_type=jnp.float32)
        up_sum = part if up_sum is None else up_sum + part
    sums_out[:, :units] = gate_sum
    sums_out[:, units:] = up_sum
    for copy in later:
        copy.wait()


def near_experts(ep, own, core, w_gate, w_up, w_down):
    slots, features = own.shape
    units = w_gate.shape[2]
    return pl.pallas_call(
        near_kernel,
        out_shape=[
            jax.ShapeDtypeStruct((slots, 2 * units), jnp.float32),
            jax.ShapeDtypeStruct((2, features, units), jnp.bfloat16),
            jax.ShapeDtypeStruct((2, features, units), jnp.bfloat16),
            jax.ShapeDtypeStruct((4, units, features), jnp.bfloat16),
        ],
        in_specs=[SMEM_SPEC] + [VMEM_SPEC] * 2 + [HBM_SPEC] * 3,
        out_specs=[VMEM_SPEC] * 4,
        scratch_shapes=[
            VMEM((2, features, units), jnp.bfloat16),
            VMEM((2, features, units), jnp.bfloat16),
            pltpu.SemaphoreType.DMA((2, 2)),
            pltpu.SemaphoreType.DMA((2, 2)),
            pltpu.SemaphoreType.DMA((4,)),
        ],
        compiler_params=pltpu.CompilerParams(vmem_limit_bytes=46 * MIB),
        cost_estimate=pl.CostEstimate(
            flops=8 * slots * features * units,
            bytes_accessed=24 * features * units,
            transcendentals=0,
        ),
        name="near_experts",
    )(ep, own, core, w_gate, w_up, w_down)


def far_kernel(
    far_ref, core_far_ref, sums_ref, gate, up, down, own_out, core_out, far_out, core_far_out
):
    units = gate.shape[2]
    gate_sum, up_sum = sums_ref[:, :units], sums_ref[:, units:]
    for index, x_ref in enumerate((far_ref, core_far_ref)):
        rows = x_ref[...]
        gate_sum = gate_sum + jnp.dot(rows, gate[index], preferred_element_type=jnp.float32)
        up_sum = up_sum + jnp.dot(rows, up[index], preferred_element_type=jnp.float32)
    hidden = (gate_sum / (1.0 + jnp.exp(-gate_sum)) * up_sum).astype(jnp.bfloat16)
    outs = (own_out, core_out, far_out, core_far_out)
    for flip in (3, 1, 2, 0):
        outs[flip][...] = jnp.dot(
            hidden, down[flip], preferred_element_type=jnp.float32
        ).astype(jnp.bfloat16)


def far_experts(far, core_far, sums, gate, up, down):
    slots, features = far.shape
    units = gate.shape[2]
    return pl.pallas_call(
        far_kernel,
        out_shape=[jax.ShapeDtypeStruct((slots, features), jnp.bfloat16)] * 4,
        in_specs=[VMEM_SPEC] * 6,
        out_specs=[VMEM_SPEC] * 4,
        compiler_params=pltpu.CompilerParams(vmem_limit_bytes=24 * MIB),
        cost_estimate=pl.CostEstimate(flops=0, bytes_accessed=0, transcendentals=0),
        name="far_experts",
    )(far, core_far, sums, gate, up, down)


def add_kernel(*refs):
    total = refs[0][...].astype(jnp.float32)
    for ref in refs[1:-1]:
        total = total + ref[...].astype(jnp.float32)
    refs[-1][...] = total.astype(jnp.bfloat16)


def add(*parts):
    return pl.pallas_call(
        add_kernel,
        out_shape=jax.ShapeDtypeStruct(parts[0].shape, jnp.bfloat16),
        in_specs=[VMEM_SPEC] * len(parts),
        out_specs=VMEM_SPEC,
        compiler_params=pltpu.CompilerParams(vmem_limit_bytes=8 * MIB),
        cost_estimate=pl.CostEstimate(flops=0, bytes_accessed=MIB, transcendentals=0),
        name="add",
    )(*parts)


def combine_kernel(high_ref, low_ref, returned_ref, out_ref):
    returned = returned_ref[...]
    total = lax.dot_general(high_ref[...], returned, TN, preferred_element_type=jnp.float32)
    total = total + lax.dot_general(
        low_ref[...], returned, TN, preferred_element_type=jnp.float32
    )
    out_ref[...] = total.astype(jnp.bfloat16)


def combine(high, low, returned):
    slots, row_count = high.shape
    features = returned.shape[1]
    return pl.pallas_call(
        combine_kernel,
        out_shape=jax.ShapeDtypeStruct((row_count, features), jnp.bfloat16),
        in_specs=[VMEM_SPEC] * 3,
        out_specs=VMEM_SPEC,
        compiler_params=pltpu.CompilerParams(vmem_limit_bytes=LIMIT),
        cost_estimate=pl.CostEstimate(
            flops=4 * row_count * slots * features, bytes_accessed=MIB, transcendentals=0
        ),
        name="combine",
    )(high, low, returned)


def low_run(my_ctx, positions_ref):
    mine = my_ctx * (2 * HALF)
    return jnp.where(positions_ref[mine] < positions_ref[mine + HALF], 0, 1)


def fold_kernel(own_ref, positions_ref, q_nope_ref, q_rope_ref, w_uk_ref, out_ref):
    latent_width = w_uk_ref.shape[0]
    low = low_run(own_ref[0], positions_ref)
    for head in range(GROUP):
        columns = slice(head * NOPE, (head + 1) * NOPE)
        folded = lax.dot_general(
            q_nope_ref[:, columns], w_uk_ref[:, columns], NT, preferred_element_type=jnp.float32
        ).astype(jnp.bfloat16)
        rotated = q_rope_ref[:, head * ROPE : (head + 1) * ROPE]
        for run in range(2):
            rows = slice(run * HALF, (run + 1) * HALF)
            place = slice(head * HALF, (head + 1) * HALF)
            slot = 1 - (low ^ run)
            out_ref[0, slot, place, :latent_width] = folded[rows]
            out_ref[0, slot, place, latent_width:] = rotated[rows]


def fold(own, positions, q_nope, q_rope, w_uk):
    query_count, columns = q_nope.shape
    heads = columns // NOPE
    latent_width = w_uk.shape[0]
    width = latent_width + ROPE
    steps = heads // GROUP // 2
    queries = pl.pallas_call(
        fold_kernel,
        out_shape=jax.ShapeDtypeStruct((2, 2, heads // 2 * HALF, width), jnp.bfloat16),
        grid=(2 * steps,),
        in_specs=[
            SMEM_SPEC,
            SMEM_SPEC,
            pl.BlockSpec((query_count, GROUP * NOPE), lambda step: (0, step)),
            pl.BlockSpec((query_count, GROUP * ROPE), lambda step: (0, step)),
            pl.BlockSpec((latent_width, GROUP * NOPE), lambda step: (0, step)),
        ],
        out_specs=pl.BlockSpec(
            (1, 2, GROUP * HALF, width), lambda step: (step // steps, 0, step % steps, 0)
        ),
        compiler_params=pltpu.CompilerParams(vmem_limit_bytes=FULL),
        cost_estimate=pl.CostEstimate(
            flops=2 * query_count * columns * latent_width,
            bytes_accessed=6 * MIB,
            transcendentals=0,
        ),
        name="fold",
    )(own, positions, q_nope, q_rope, w_uk)
    return queries.reshape(2, heads * HALF, width)


def first_kernel(
    own_ref,
    positions_ref,
    queries,
    w_uv_hbm,
    own_keys,
    core_keys,
    out_ref,
    keys,
    later_w_uv,
    w_uv,
    *scratch,
):
    semaphores = scratch[-1]
    copies = []
    for index, target in enumerate((w_uv, later_w_uv)):
        width = target.shape[1]
        source = w_uv_hbm.at[:, pl.ds(index * width, width)]
        copies.append(pltpu.make_async_copy(source, target, semaphores.at[index]))
        copies[-1].start()
    blocks = own_keys.shape[0]
    my_ctx, my_ep = own_ref[0], own_ref[1]
    for flip, source in enumerate((own_keys, core_keys)):
        for index in range(blocks):
            source_ctx = my_ctx
            for bit, step in enumerate(gather_order(blocks)):
                if index >> bit & 1:
                    source_ctx = source_ctx ^ step
            start = source_ctx * (2 * HALF) + ((my_ep % 2) ^ flip) * HALF
            place = pl.multiple_of(positions_ref[start], HALF)
            keys[pl.ds(place, HALF), :] = source[index]
    attend_heads(
        own_ref, positions_ref, queries.at[0], w_uv, keys, out_ref, 0, copies[0].wait, *scratch[:-1]
    )
    copies[1].wait()


def second_kernel(own_ref, positions_ref, queries, w_uv, keys, done_ref, out_ref, *scratch):
    skipped = done_ref.shape[1]
    out_ref[:, :skipped] = done_ref[...]
    attend_heads(
        own_ref, positions_ref, queries.at[1], w_uv, keys, out_ref, skipped, lambda: None, *scratch
    )


def attend_heads(
    own_ref, positions_ref, queries, w_uv, keys, out_ref, skipped, wait, scores, tops, mixed
):
    latent_width = w_uv.shape[0]
    count = queries.shape[0] // 2
    heads = count // HALF
    mine = own_ref[0] * (2 * HALF)
    low = low_run(own_ref[0], positions_ref)
    high = 1 - low
    low_base = positions_ref[mine + low * HALF]
    high_base = positions_ref[mine + high * HALF]
    tops[...] = jnp.full(tops.shape, -jnp.inf, jnp.float32)
    offset = lax.broadcasted_iota(jnp.int32, (HALF, CHUNK), 1) - lax.broadcasted_iota(
        jnp.int32, (HALF, CHUNK), 0
    )
    low_chunks = (low_base + HALF + CHUNK - 1) // CHUNK
    high_chunks = (high_base + HALF + CHUNK - 1) // CHUNK

    def score(chunk, bases):
        start = pl.multiple_of(chunk * CHUNK, CHUNK)
        part = lax.dot_general(
            queries[: len(bases) * count, :],
            keys[pl.ds(start, CHUNK), :],
            NT,
            preferred_element_type=jnp.float32,
        )
        for index, base in enumerate(bases):
            visible = offset <= base - start
            for head in range(heads):
                rows = slice(index * count + head * HALF, index * count + (head + 1) * HALF)
                seen = jnp.where(visible, part[rows], -jnp.inf)
                scores[chunk, rows, :] = seen
                top = tops[rows, :]
                for lane in range(0, CHUNK, 128):
                    top = jnp.maximum(top, seen[:, lane : lane + 128])
                tops[rows, :] = top
        return 0

    lax.fori_loop(0, low_chunks, lambda c, _: score(c, (high_base, low_base)), 0)
    lax.fori_loop(low_chunks, high_chunks, lambda c, _: score(c, (high_base,)), 0)
    factor = math.log2(math.e) / math.sqrt(NOPE + ROPE)

    def mix(rows, chunks):
        top = jnp.max(tops[rows, :], axis=1, keepdims=True) * factor
        total = jnp.zeros((count, 128), jnp.float32)
        parts = []
        for chunk in range(chunks):
            part = jnp.exp2(scores[chunk, rows, :] * factor - top)
            for lane in range(0, CHUNK, 128):
                total = total + part[:, lane : lane + 128]
            parts.append(part.astype(jnp.bfloat16))
        summed = jnp.dot(
            jnp.concatenate(parts, axis=1),
            keys[: chunks * CHUNK, :latent_width],
            preferred_element_type=jnp.float32,
        )
        share = 1.0 / jnp.sum(total, axis=1, keepdims=True)
        mixed[rows, :] = (summed * share).astype(jnp.bfloat16)

    most = keys.shape[0] // CHUNK
    for chunks in range(1, most + 1):

        @pl.when(high_chunks == chunks)
        def _():
            mix(slice(0, count), chunks)

        @pl.when(low_chunks == chunks)
        def _():
            mix(slice(count, 2 * count), chunks)

    wait()
    high_rows = pl.ds(pl.multiple_of(high * HALF, HALF), HALF)
    low_rows = pl.ds(pl.multiple_of(low * HALF, HALF), HALF)
    for head in range(heads):
        both = jnp.concatenate(
            [
                mixed[head * HALF : (head + 1) * HALF, :],
                mixed[count + head * HALF : count + (head + 1) * HALF, :],
            ],
            axis=0,
        )
        value = jnp.dot(
            both, w_uv[:, head * VDIM : (head + 1) * VDIM], preferred_element_type=jnp.float32
        ).astype(jnp.bfloat16)
        columns = slice(skipped + head * VDIM, skipped + (head + 1) * VDIM)
        out_ref[high_rows, columns] = value[:HALF]
        out_ref[low_rows, columns] = value[HALF:]


def attend_scratch(count, key_count, latent_width):
    return [
        VMEM((key_count // CHUNK, 2 * count, CHUNK), jnp.float32),
        VMEM((2 * count, 128), jnp.float32),
        VMEM((2 * count, latent_width), jnp.bfloat16),
    ]


def attend_cost(count, key_count, width):
    return pl.CostEstimate(
        flops=3 * count * key_count * width,
        bytes_accessed=4 * MIB,
        transcendentals=count * key_count,
    )


def attend_first(own, positions, queries, w_uv, own_keys, core_keys):
    latent_width, columns = w_uv.shape
    key_count = positions.shape[0]
    width = own_keys.shape[-1]
    count = queries.shape[1] // 2
    half = (latent_width, columns // 2)
    return pl.pallas_call(
        first_kernel,
        out_shape=[
            jax.ShapeDtypeStruct((2 * HALF, columns // 2), jnp.bfloat16),
            jax.ShapeDtypeStruct((key_count, width), jnp.bfloat16),
            jax.ShapeDtypeStruct(half, jnp.bfloat16),
        ],
        in_specs=[SMEM_SPEC] * 2 + [VMEM_SPEC, HBM_SPEC] + [VMEM_SPEC] * 2,
        out_specs=[VMEM_SPEC] * 3,
        scratch_shapes=[VMEM(half, jnp.bfloat16)]
        + attend_scratch(count, key_count, latent_width)
        + [pltpu.SemaphoreType.DMA((2,))],
        compiler_params=pltpu.CompilerParams(vmem_limit_bytes=48 * MIB),
        cost_estimate=attend_cost(count, key_count, width),
        name="attention_first",
    )(own, positions, queries, w_uv, own_keys, core_keys)


def attend_second(own, positions, queries, w_uv, keys, done):
    latent_width, columns = w_uv.shape
    key_count, width = keys.shape
    count = queries.shape[1] // 2
    return pl.pallas_call(
        second_kernel,
        out_shape=jax.ShapeDtypeStruct((2 * HALF, 2 * columns), jnp.bfloat16),
        in_specs=[SMEM_SPEC] * 2 + [VMEM_SPEC] * 4,
        out_specs=VMEM_SPEC,
        scratch_shapes=attend_scratch(count, key_count, latent_width),
        compiler_params=pltpu.CompilerParams(vmem_limit_bytes=48 * MIB),
        cost_estimate=attend_cost(count, key_count, width),
        name="attention_second",
    )(own, positions, queries, w_uv, keys, done)


def shards(
    q_nope,
    q_rope,
    latent,
    k_rope,
    w_uk,
    w_uv,
    positions,
    moe_rows,
    expert_ids,
    expert_weights,
    w_gate,
    w_up,
    w_down,
):
    ctx = lax.axis_size("ctx")
    me = lax.axis_index("ctx").astype(jnp.int32).reshape(1)
    ep = lax.axis_index("ep").astype(jnp.int32).reshape(1)

    def over_ctx(value, flip):
        return lax.ppermute(value, "ctx", [(i, i ^ flip) for i in range(ctx)])

    def over_ep(value, flip):
        return lax.ppermute(value, "ep", [(i, i ^ flip) for i in range(4)])

    def exchange(value):
        return lax.all_to_all(value, "ctx", split_axis=0, concat_axis=0, tiled=True)

    place = jnp.concatenate([me, ep])
    outgoing, high, low, packed = route(
        ep, expert_ids, expert_weights, k_rope, moe_rows, latent, ctx
    )
    arrived = exchange(outgoing)
    flips = gather_order(ctx)
    received = over_ctx(packed[None], flips[0])
    high, q_nope, received = lax.optimization_barrier((high, q_nope, received))
    queries = fold(place, positions, q_nope, q_rope, w_uk)
    own_keys = jnp.concatenate([packed[None], received], axis=0)
    for flip in flips[1:-1]:
        own_keys = jnp.concatenate([own_keys, over_ctx(own_keys, flip)], axis=0)
    arrived, queries, own_keys = lax.optimization_barrier((arrived, queries, own_keys))

    own = arrived.reshape(ctx * CAP, arrived.shape[2])
    far = over_ep(own, 2)
    core = over_ep(own, 1)
    received = over_ctx(own_keys, flips[-1])
    sums, far_gate, far_up, down = near_experts(ep, own, core, w_gate, w_up, w_down)
    far, sums = lax.optimization_barrier((far, sums))
    core_far = over_ep(far, 1)
    own_out, core_out, far_out, core_far_out = far_experts(
        far, core_far, sums, far_gate, far_up, down
    )
    core_far_out, received = lax.optimization_barrier((core_far_out, received))
    from_core_far = over_ep(core_far_out, 1)
    from_core = over_ep(core_out, 1)
    own_keys = jnp.concatenate([own_keys, received], axis=0)
    own_keys, from_core_far = lax.optimization_barrier((own_keys, from_core_far))
    to_far = add(far_out, from_core_far)
    from_far = over_ep(to_far, 2)
    core_keys = over_ep(own_keys, 1)
    half, keys, later_w_uv = attend_first(
        place, positions, queries, w_uv, own_keys, core_keys
    )
    from_far, half = lax.optimization_barrier((from_far, half))
    returning = add(own_out, from_core, from_far)
    returned = exchange(returning.reshape(arrived.shape))
    attention = attend_second(place, positions, queries, later_w_uv, keys, half)
    moe_out = combine(high, low, returned.reshape(own.shape))
    return (attention, moe_out)


def solution(mesh):
    return jax.shard_map(
        shards,
        mesh=mesh,
        in_specs=(
            P("ctx", "ep"),
            P("ctx", "ep"),
            P("ctx", None),
            P("ctx", None),
            P(None, "ep"),
            P(None, "ep"),
            P(),
            P("ctx", "ep"),
            P("ctx", None),
            P("ctx", None),
            P("ctx", None, "ep"),
            P("ctx", None, "ep"),
            P("ctx", "ep", None),
        ),
        out_specs=(P("ctx", "ep"), P("ctx", "ep")),
        check_vma=False,
    )
```

```python
import functools
import math

import jax
import jax.numpy as jnp
from jax import lax
from jax.experimental import pallas as pl
from jax.experimental.pallas import tpu as pltpu
from jax.sharding import PartitionSpec as P

NOPE = 128
ROPE = 64
VDIM = 128
TOP = 8
CAP = 8
HALF = 64
GROUP = 4
MIB = 1 << 20
LIMIT = 52 * MIB
FULL = 60 * MIB
SMALL = 24 * MIB
CHUNK = 256

NT = (((1,), (1,)), ((), ()))
TN = (((0,), (0,)), ((), ()))
VMEM = pltpu.VMEM
SMEM_SPEC = pl.BlockSpec(memory_space=pltpu.SMEM)
VMEM_SPEC = pl.BlockSpec(memory_space=pltpu.VMEM)
HBM_SPEC = pl.BlockSpec(memory_space=pltpu.HBM)


def gather_order(ctx):
    bits = ctx.bit_length() - 1
    return [1 << (bits - 1)] + [1 << bit for bit in range(bits - 1)]


def route_kernel(
    ep_ref,
    ids_ref,
    weights_ref,
    rope_ref,
    rows_ref,
    latent_ref,
    sent_ref,
    high_ref,
    low_ref,
    packed_ref,
):
    latent_width = latent_ref.shape[1]
    rope = rope_ref[...].astype(jnp.float32).T
    for core in range(2):

        @pl.when(ep_ref[0] % 2 == core)
        def _():
            rows = slice(core * HALF, (core + 1) * HALF)
            packed_ref[:, :latent_width] = latent_ref[rows, :]
            packed_ref[:, latent_width:] = rope[rows].astype(jnp.bfloat16)

    row_count = ids_ref.shape[1]
    slots = sent_ref.shape[0] * CAP
    slot = lax.broadcasted_iota(jnp.int32, (slots, row_count), 0)
    expert = slot // CAP
    named = jnp.zeros((slots, row_count), jnp.float32)
    gate = jnp.zeros((slots, row_count), jnp.float32)
    for choice in range(TOP):
        match = ids_ref[choice : choice + 1, :] == expert
        named = jnp.where(match, 1.0, named)
        gate = jnp.where(match, weights_ref[choice : choice + 1, :], gate)
    row = lax.broadcasted_iota(jnp.int32, (row_count, row_count), 0)
    other = lax.broadcasted_iota(jnp.int32, (row_count, row_count), 1)
    before = jnp.where(row < other, 1.0, 0.0).astype(jnp.bfloat16)
    rank = jnp.dot(named.astype(jnp.bfloat16), before, preferred_element_type=jnp.float32)
    taken = (named > 0.0) & (rank == (slot % CAP).astype(jnp.float32))
    select = jnp.where(taken, 1.0, 0.0).astype(jnp.bfloat16)
    gate = jnp.where(taken, gate, 0.0)
    high = gate.astype(jnp.bfloat16)
    high_ref[...] = high
    low_ref[...] = (gate - high.astype(jnp.float32)).astype(jnp.bfloat16)
    sent = jnp.dot(select, rows_ref[...], preferred_element_type=jnp.float32)
    for index in range(slots // CAP):
        sent_ref[index] = sent[index * CAP : (index + 1) * CAP].astype(jnp.bfloat16)


def route(ep, expert_ids, expert_weights, k_rope, moe_rows, latent, ctx):
    row_count, features = moe_rows.shape
    slots = ctx * CAP
    return pl.pallas_call(
        route_kernel,
        out_shape=[
            jax.ShapeDtypeStruct((ctx, CAP, features), jnp.bfloat16),
            jax.ShapeDtypeStruct((slots, row_count), jnp.bfloat16),
            jax.ShapeDtypeStruct((slots, row_count), jnp.bfloat16),
            jax.ShapeDtypeStruct((HALF, latent.shape[1] + ROPE), jnp.bfloat16),
        ],
        in_specs=[SMEM_SPEC] + [VMEM_SPEC] * 5,
        out_specs=[VMEM_SPEC] * 4,
        compiler_params=pltpu.CompilerParams(vmem_limit_bytes=FULL),
        cost_estimate=pl.CostEstimate(
            flops=2 * row_count * slots * features, bytes_accessed=1 * MIB, transcendentals=0
        ),
        name="route",
    )(ep, expert_ids.T, expert_weights.T, k_rope.T, moe_rows, latent)


def weight_copies(ep_ref, flips, gate_hbm, up_hbm, gate, up, semaphores):
    features = gate.shape[1]
    copies = []
    for index, flip in enumerate(flips):
        place = pl.multiple_of((ep_ref[0] ^ flip) * features, features)
        for which, (source, target) in enumerate(((gate_hbm, gate), (up_hbm, up))):
            copy = pltpu.make_async_copy(
                source.at[0, pl.ds(place, features)], target.at[index], semaphores.at[index, which]
            )
            copy.start()
            copies.append(copy)
    return copies


def near_kernel(
    ep_ref,
    own_ref,
    core_ref,
    gate_hbm,
    up_hbm,
    down_hbm,
    sums_out,
    far_gate,
    far_up,
    down,
    gate,
    up,
    semaphores,
    far_semaphores,
    down_semaphores,
):
    units = gate.shape[2]
    features = gate.shape[1]
    copies = weight_copies(ep_ref, (0, 1), gate_hbm, up_hbm, gate, up, semaphores)
    later = weight_copies(ep_ref, (2, 3), gate_hbm, up_hbm, far_gate, far_up, far_semaphores)
    for flip in (3, 1, 2, 0):
        place = pl.multiple_of((ep_ref[0] ^ flip) * features, features)
        copy = pltpu.make_async_copy(
            down_hbm.at[0, :, pl.ds(place, features)], down.at[flip], down_semaphores.at[flip]
        )
        copy.start()
        later.append(copy)
    gate_sum, up_sum = None, None
    for index, x_ref in enumerate((own_ref, core_ref)):
        rows = x_ref[...]
        copies[2 * index].wait()
        part = jnp.dot(rows, gate[index], preferred_element_type=jnp.float32)
        gate_sum = part if gate_sum is None else gate_sum + part
        copies[2 * index + 1].wait()
        part = jnp.dot(rows, up[index], preferred_element_type=jnp.float32)
        up_sum = part if up_sum is None else up_sum + part
    sums_out[:, :units] = gate_sum
    sums_out[:, units:] = up_sum
    for copy in later:
        copy.wait()


def near_experts(ep, own, core, w_gate, w_up, w_down):
    slots, features = own.shape
    units = w_gate.shape[2]
    return pl.pallas_call(
        near_kernel,
        out_shape=[
            jax.ShapeDtypeStruct((slots, 2 * units), jnp.float32),
            jax.ShapeDtypeStruct((2, features, units), jnp.bfloat16),
            jax.ShapeDtypeStruct((2, features, units), jnp.bfloat16),
            jax.ShapeDtypeStruct((4, units, features), jnp.bfloat16),
        ],
        in_specs=[SMEM_SPEC] + [VMEM_SPEC] * 2 + [HBM_SPEC] * 3,
        out_specs=[VMEM_SPEC] * 4,
        scratch_shapes=[
            VMEM((2, features, units), jnp.bfloat16),
            VMEM((2, features, units), jnp.bfloat16),
            pltpu.SemaphoreType.DMA((2, 2)),
            pltpu.SemaphoreType.DMA((2, 2)),
            pltpu.SemaphoreType.DMA((4,)),
        ],
        compiler_params=pltpu.CompilerParams(vmem_limit_bytes=46 * MIB),
        cost_estimate=pl.CostEstimate(
            flops=8 * slots * features * units,
            bytes_accessed=24 * features * units,
            transcendentals=0,
        ),
        name="near_experts",
    )(ep, own, core, w_gate, w_up, w_down)


def far_kernel(
    far_ref, core_far_ref, sums_ref, gate, up, down, own_out, core_out, far_out, core_far_out
):
    units = gate.shape[2]
    gate_sum, up_sum = sums_ref[:, :units], sums_ref[:, units:]
    for index, x_ref in enumerate((far_ref, core_far_ref)):
        rows = x_ref[...]
        gate_sum = gate_sum + jnp.dot(rows, gate[index], preferred_element_type=jnp.float32)
        up_sum = up_sum + jnp.dot(rows, up[index], preferred_element_type=jnp.float32)
    hidden = (gate_sum / (1.0 + jnp.exp(-gate_sum)) * up_sum).astype(jnp.bfloat16)
    outs = (own_out, core_out, far_out, core_far_out)
    for flip in (3, 1, 2, 0):
        outs[flip][...] = jnp.dot(
            hidden, down[flip], preferred_element_type=jnp.float32
        ).astype(jnp.bfloat16)


def far_experts(far, core_far, sums, gate, up, down):
    slots, features = far.shape
    units = gate.shape[2]
    return pl.pallas_call(
        far_kernel,
        out_shape=[jax.ShapeDtypeStruct((slots, features), jnp.bfloat16)] * 4,
        in_specs=[VMEM_SPEC] * 6,
        out_specs=[VMEM_SPEC] * 4,
        compiler_params=pltpu.CompilerParams(vmem_limit_bytes=24 * MIB),
        cost_estimate=pl.CostEstimate(flops=0, bytes_accessed=0, transcendentals=0),
        name="far_experts",
    )(far, core_far, sums, gate, up, down)


def add_kernel(*refs):
    total = refs[0][...].astype(jnp.float32)
    for ref in refs[1:-1]:
        total = total + ref[...].astype(jnp.float32)
    refs[-1][...] = total.astype(jnp.bfloat16)


def add(*parts):
    return pl.pallas_call(
        add_kernel,
        out_shape=jax.ShapeDtypeStruct(parts[0].shape, jnp.bfloat16),
        in_specs=[VMEM_SPEC] * len(parts),
        out_specs=VMEM_SPEC,
        compiler_params=pltpu.CompilerParams(vmem_limit_bytes=8 * MIB),
        cost_estimate=pl.CostEstimate(flops=0, bytes_accessed=MIB, transcendentals=0),
        name="add",
    )(*parts)


def combine_kernel(high_ref, low_ref, returned_ref, out_ref):
    returned = returned_ref[...]
    total = lax.dot_general(high_ref[...], returned, TN, preferred_element_type=jnp.float32)
    total = total + lax.dot_general(
        low_ref[...], returned, TN, preferred_element_type=jnp.float32
    )
    out_ref[...] = total.astype(jnp.bfloat16)


def combine(high, low, returned):
    slots, row_count = high.shape
    features = returned.shape[1]
    return pl.pallas_call(
        combine_kernel,
        out_shape=jax.ShapeDtypeStruct((row_count, features), jnp.bfloat16),
        in_specs=[VMEM_SPEC] * 3,
        out_specs=VMEM_SPEC,
        compiler_params=pltpu.CompilerParams(vmem_limit_bytes=LIMIT),
        cost_estimate=pl.CostEstimate(
            flops=4 * row_count * slots * features, bytes_accessed=MIB, transcendentals=0
        ),
        name="combine",
    )(high, low, returned)


def low_run(my_ctx, positions_ref):
    mine = my_ctx * (2 * HALF)
    return jnp.where(positions_ref[mine] < positions_ref[mine + HALF], 0, 1)


def fold_kernel(own_ref, positions_ref, q_nope_ref, q_rope_ref, w_uk_ref, out_ref):
    latent_width = w_uk_ref.shape[0]
    low = low_run(own_ref[0], positions_ref)
    for head in range(GROUP):
        columns = slice(head * NOPE, (head + 1) * NOPE)
        folded = lax.dot_general(
            q_nope_ref[:, columns], w_uk_ref[:, columns], NT, preferred_element_type=jnp.float32
        ).astype(jnp.bfloat16)
        rotated = q_rope_ref[:, head * ROPE : (head + 1) * ROPE]
        for run in range(2):
            rows = slice(run * HALF, (run + 1) * HALF)
            place = slice(head * HALF, (head + 1) * HALF)
            slot = 1 - (low ^ run)
            out_ref[0, slot, place, :latent_width] = folded[rows]
            out_ref[0, slot, place, latent_width:] = rotated[rows]


def fold(own, positions, q_nope, q_rope, w_uk):
    query_count, columns = q_nope.shape
    heads = columns // NOPE
    latent_width = w_uk.shape[0]
    width = latent_width + ROPE
    steps = heads // GROUP // 2
    queries = pl.pallas_call(
        fold_kernel,
        out_shape=jax.ShapeDtypeStruct((2, 2, heads // 2 * HALF, width), jnp.bfloat16),
        grid=(2 * steps,),
        in_specs=[
            SMEM_SPEC,
            SMEM_SPEC,
            pl.BlockSpec((query_count, GROUP * NOPE), lambda step: (0, step)),
            pl.BlockSpec((query_count, GROUP * ROPE), lambda step: (0, step)),
            pl.BlockSpec((latent_width, GROUP * NOPE), lambda step: (0, step)),
        ],
        out_specs=pl.BlockSpec(
            (1, 2, GROUP * HALF, width), lambda step: (step // steps, 0, step % steps, 0)
        ),
        compiler_params=pltpu.CompilerParams(vmem_limit_bytes=FULL),
        cost_estimate=pl.CostEstimate(
            flops=2 * query_count * columns * latent_width,
            bytes_accessed=6 * MIB,
            transcendentals=0,
        ),
        name="fold",
    )(own, positions, q_nope, q_rope, w_uk)
    return queries.reshape(2, heads * HALF, width)


def first_kernel(
    own_ref,
    ep_ref,
    positions_ref,
    queries_hbm,
    w_uv_hbm,
    own_keys,
    core_keys,
    out_ref,
    keys,
    later_w_uv,
    w_uv,
    queries,
    *scratch,
):
    semaphores = scratch[-1]
    copies = [pltpu.make_async_copy(queries_hbm.at[0], queries, semaphores.at[2])]
    copies[0].start()
    for index, target in enumerate((w_uv, later_w_uv)):
        width = target.shape[1]
        source = w_uv_hbm.at[:, pl.ds(index * width, width)]
        copies.append(pltpu.make_async_copy(source, target, semaphores.at[index]))
        copies[-1].start()
    blocks = own_keys.shape[0]
    my_ctx, my_ep = own_ref[0], ep_ref[0]
    for flip, source in enumerate((own_keys, core_keys)):
        for index in range(blocks):
            source_ctx = my_ctx
            for bit, step in enumerate(gather_order(blocks)):
                if index >> bit & 1:
                    source_ctx = source_ctx ^ step
            start = source_ctx * (2 * HALF) + ((my_ep % 2) ^ flip) * HALF
            place = pl.multiple_of(positions_ref[start], HALF)
            keys[pl.ds(place, HALF), :] = source[index]
    copies[0].wait()
    attend_heads(
        own_ref, positions_ref, queries, w_uv, keys, out_ref, 0, copies[1].wait, *scratch[:-1]
    )
    copies[2].wait()


def second_kernel(own_ref, positions_ref, queries, w_uv, keys, done_ref, out_ref, *scratch):
    skipped = done_ref.shape[1]
    out_ref[:, :skipped] = done_ref[...]
    attend_heads(
        own_ref, positions_ref, queries.at[1], w_uv, keys, out_ref, skipped, lambda: None, *scratch
    )


def attend_heads(
    own_ref, positions_ref, queries, w_uv, keys, out_ref, skipped, wait, scores, tops, mixed
):
    latent_width = w_uv.shape[0]
    count = queries.shape[0] // 2
    heads = count // HALF
    mine = own_ref[0] * (2 * HALF)
    low = low_run(own_ref[0], positions_ref)
    high = 1 - low
    low_base = positions_ref[mine + low * HALF]
    high_base = positions_ref[mine + high * HALF]
    tops[...] = jnp.full(tops.shape, -jnp.inf, jnp.float32)
    offset = lax.broadcasted_iota(jnp.int32, (HALF, CHUNK), 1) - lax.broadcasted_iota(
        jnp.int32, (HALF, CHUNK), 0
    )
    low_chunks = (low_base + HALF + CHUNK - 1) // CHUNK
    high_chunks = (high_base + HALF + CHUNK - 1) // CHUNK

    def score(chunk, bases):
        start = pl.multiple_of(chunk * CHUNK, CHUNK)
        part = lax.dot_general(
            queries[: len(bases) * count, :],
            keys[pl.ds(start, CHUNK), :],
            NT,
            preferred_element_type=jnp.float32,
        )
        for index, base in enumerate(bases):
            visible = offset <= base - start
            for head in range(heads):
                rows = slice(index * count + head * HALF, index * count + (head + 1) * HALF)
                seen = jnp.where(visible, part[rows], -jnp.inf)
                scores[chunk, rows, :] = seen
                top = tops[rows, :]
                for lane in range(0, CHUNK, 128):
                    top = jnp.maximum(top, seen[:, lane : lane + 128])
                tops[rows, :] = top
        return 0

    lax.fori_loop(0, low_chunks, lambda c, _: score(c, (high_base, low_base)), 0)
    lax.fori_loop(low_chunks, high_chunks, lambda c, _: score(c, (high_base,)), 0)
    factor = math.log2(math.e) / math.sqrt(NOPE + ROPE)

    def mix(rows, chunks):
        top = jnp.max(tops[rows, :], axis=1, keepdims=True) * factor
        total = jnp.zeros((count, 128), jnp.float32)
        parts = []
        for chunk in range(chunks):
            part = jnp.exp2(scores[chunk, rows, :] * factor - top)
            for lane in range(0, CHUNK, 128):
                total = total + part[:, lane : lane + 128]
            parts.append(part.astype(jnp.bfloat16))
        summed = jnp.dot(
            jnp.concatenate(parts, axis=1),
            keys[: chunks * CHUNK, :latent_width],
            preferred_element_type=jnp.float32,
        )
        share = 1.0 / jnp.sum(total, axis=1, keepdims=True)
        mixed[rows, :] = (summed * share).astype(jnp.bfloat16)

    most = keys.shape[0] // CHUNK
    for chunks in range(1, most + 1):

        @pl.when(high_chunks == chunks)
        def _():
            mix(slice(0, count), chunks)

        @pl.when(low_chunks == chunks)
        def _():
            mix(slice(count, 2 * count), chunks)

    wait()
    high_rows = pl.ds(pl.multiple_of(high * HALF, HALF), HALF)
    low_rows = pl.ds(pl.multiple_of(low * HALF, HALF), HALF)
    for head in range(heads):
        both = jnp.concatenate(
            [
                mixed[head * HALF : (head + 1) * HALF, :],
                mixed[count + head * HALF : count + (head + 1) * HALF, :],
            ],
            axis=0,
        )
        value = jnp.dot(
            both, w_uv[:, head * VDIM : (head + 1) * VDIM], preferred_element_type=jnp.float32
        ).astype(jnp.bfloat16)
        columns = slice(skipped + head * VDIM, skipped + (head + 1) * VDIM)
        out_ref[high_rows, columns] = value[:HALF]
        out_ref[low_rows, columns] = value[HALF:]


def attend_scratch(count, key_count, latent_width):
    return [
        VMEM((key_count // CHUNK, 2 * count, CHUNK), jnp.float32),
        VMEM((2 * count, 128), jnp.float32),
        VMEM((2 * count, latent_width), jnp.bfloat16),
    ]


def attend_limit(key_count):
    return (12 + -(-9 * key_count // 1024)) * MIB


def attend_cost(count, key_count, width):
    return pl.CostEstimate(
        flops=3 * count * key_count * width,
        bytes_accessed=4 * MIB,
        transcendentals=count * key_count,
    )


def attend_first(own, ep, positions, queries, w_uv, own_keys, core_keys):
    latent_width, columns = w_uv.shape
    key_count = positions.shape[0]
    width = own_keys.shape[-1]
    count = queries.shape[1] // 2
    half = (latent_width, columns // 2)
    return pl.pallas_call(
        first_kernel,
        out_shape=[
            jax.ShapeDtypeStruct((2 * HALF, columns // 2), jnp.bfloat16),
            jax.ShapeDtypeStruct((key_count, width), jnp.bfloat16),
            jax.ShapeDtypeStruct(half, jnp.bfloat16),
        ],
        in_specs=[SMEM_SPEC] * 3 + [HBM_SPEC] * 2 + [VMEM_SPEC] * 2,
        out_specs=[VMEM_SPEC] * 3,
        scratch_shapes=[VMEM(half, jnp.bfloat16), VMEM(queries.shape[1:], jnp.bfloat16)]
        + attend_scratch(count, key_count, latent_width)
        + [pltpu.SemaphoreType.DMA((3,))],
        compiler_params=pltpu.CompilerParams(vmem_limit_bytes=attend_limit(key_count)),
        cost_estimate=attend_cost(count, key_count, width),
        name="attention_first",
    )(own, ep, positions, queries, w_uv, own_keys, core_keys)


def attend_second(own, positions, queries, w_uv, keys, done):
    latent_width, columns = w_uv.shape
    key_count, width = keys.shape
    count = queries.shape[1] // 2
    return pl.pallas_call(
        second_kernel,
        out_shape=jax.ShapeDtypeStruct((2 * HALF, 2 * columns), jnp.bfloat16),
        in_specs=[SMEM_SPEC] * 2 + [VMEM_SPEC] * 4,
        out_specs=VMEM_SPEC,
        scratch_shapes=attend_scratch(count, key_count, latent_width),
        compiler_params=pltpu.CompilerParams(vmem_limit_bytes=attend_limit(key_count)),
        cost_estimate=attend_cost(count, key_count, width),
        name="attention_second",
    )(own, positions, queries, w_uv, keys, done)


def shards(
    q_nope,
    q_rope,
    latent,
    k_rope,
    w_uk,
    w_uv,
    positions,
    moe_rows,
    expert_ids,
    expert_weights,
    w_gate,
    w_up,
    w_down,
):
    ctx = lax.axis_size("ctx")
    me = lax.axis_index("ctx").astype(jnp.int32).reshape(1)
    ep = lax.axis_index("ep").astype(jnp.int32).reshape(1)

    def over_ctx(value, flip):
        return lax.ppermute(value, "ctx", [(i, i ^ flip) for i in range(ctx)])

    def over_ep(value, flip):
        return lax.ppermute(value, "ep", [(i, i ^ flip) for i in range(4)])

    def exchange(value):
        return lax.all_to_all(value, "ctx", split_axis=0, concat_axis=0, tiled=True)

    outgoing, high, low, packed = route(
        ep, expert_ids, expert_weights, k_rope, moe_rows, latent, ctx
    )
    arrived = exchange(outgoing)
    flips = gather_order(ctx)
    received = over_ctx(packed[None], flips[0])
    high, q_nope, received = lax.optimization_barrier((high, q_nope, received))
    queries = fold(me, positions, q_nope, q_rope, w_uk)
    own_keys = jnp.concatenate([packed[None], received], axis=0)
    for flip in flips[1:-1]:
        own_keys = jnp.concatenate([own_keys, over_ctx(own_keys, flip)], axis=0)
    arrived, queries, own_keys = lax.optimization_barrier((arrived, queries, own_keys))

    own = arrived.reshape(ctx * CAP, arrived.shape[2])
    far = over_ep(own, 2)
    core = over_ep(own, 1)
    received = over_ctx(own_keys, flips[-1])
    sums, far_gate, far_up, down = near_experts(ep, own, core, w_gate, w_up, w_down)
    far, sums = lax.optimization_barrier((far, sums))
    core_far = over_ep(far, 1)
    own_out, core_out, far_out, core_far_out = far_experts(
        far, core_far, sums, far_gate, far_up, down
    )
    core_far_out, received = lax.optimization_barrier((core_far_out, received))
    from_core_far = over_ep(core_far_out, 1)
    from_core = over_ep(core_out, 1)
    own_keys = jnp.concatenate([own_keys, received], axis=0)
    own_keys, from_core_far = lax.optimization_barrier((own_keys, from_core_far))
    to_far = add(far_out, from_core_far)
    from_far = over_ep(to_far, 2)
    core_keys = over_ep(own_keys, 1)
    half, keys, later_w_uv = attend_first(
        me, ep, positions, queries, w_uv, own_keys, core_keys
    )
    from_far, half = lax.optimization_barrier((from_far, half))
    returning = add(own_out, from_core, from_far)
    returned = exchange(returning.reshape(arrived.shape))
    attention = attend_second(me, positions, queries, later_w_uv, keys, half)
    moe_out = combine(high, low, returned.reshape(own.shape))
    return (attention, moe_out)


def solution(mesh):
    return jax.shard_map(
        shards,
        mesh=mesh,
        in_specs=(
            P("ctx", "ep"),
            P("ctx", "ep"),
            P("ctx", None),
            P("ctx", None),
            P(None, "ep"),
            P(None, "ep"),
            P(),
            P("ctx", "ep"),
            P("ctx", None),
            P("ctx", None),
            P("ctx", None, "ep"),
            P("ctx", None, "ep"),
            P("ctx", "ep", None),
        ),
        out_specs=(P("ctx", "ep"), P("ctx", "ep")),
        check_vma=False,
    )
```

```python
import functools
import math

import jax
import jax.numpy as jnp
from jax import lax
from jax.experimental import pallas as pl
from jax.experimental.pallas import tpu as pltpu
from jax.sharding import PartitionSpec as P

NOPE = 128
ROPE = 64
VDIM = 128
TOP = 8
CAP = 8
HALF = 64
GROUP = 4
MIB = 1 << 20
LIMIT = 52 * MIB
FULL = 60 * MIB
SMALL = 24 * MIB
CHUNK = 256

NT = (((1,), (1,)), ((), ()))
TN = (((0,), (0,)), ((), ()))
VMEM = pltpu.VMEM
SMEM_SPEC = pl.BlockSpec(memory_space=pltpu.SMEM)
VMEM_SPEC = pl.BlockSpec(memory_space=pltpu.VMEM)
HBM_SPEC = pl.BlockSpec(memory_space=pltpu.HBM)


def gather_order(ctx):
    bits = ctx.bit_length() - 1
    return [1 << (bits - 1)] + [1 << bit for bit in range(bits - 1)]


def route_kernel(
    ep_ref,
    ids_ref,
    weights_ref,
    rope_ref,
    rows_ref,
    latent_ref,
    sent_ref,
    high_ref,
    low_ref,
    packed_ref,
):
    latent_width = latent_ref.shape[1]
    rope = rope_ref[...].astype(jnp.float32).T
    for core in range(2):

        @pl.when(ep_ref[0] % 2 == core)
        def _():
            rows = slice(core * HALF, (core + 1) * HALF)
            packed_ref[:, :latent_width] = latent_ref[rows, :]
            packed_ref[:, latent_width:] = rope[rows].astype(jnp.bfloat16)

    row_count = ids_ref.shape[1]
    slots = sent_ref.shape[0] * CAP
    slot = lax.broadcasted_iota(jnp.int32, (slots, row_count), 0)
    expert = slot // CAP
    named = jnp.zeros((slots, row_count), jnp.float32)
    gate = jnp.zeros((slots, row_count), jnp.float32)
    for choice in range(TOP):
        match = ids_ref[choice : choice + 1, :] == expert
        named = jnp.where(match, 1.0, named)
        gate = jnp.where(match, weights_ref[choice : choice + 1, :], gate)
    row = lax.broadcasted_iota(jnp.int32, (row_count, row_count), 0)
    other = lax.broadcasted_iota(jnp.int32, (row_count, row_count), 1)
    before = jnp.where(row < other, 1.0, 0.0).astype(jnp.bfloat16)
    rank = jnp.dot(named.astype(jnp.bfloat16), before, preferred_element_type=jnp.float32)
    taken = (named > 0.0) & (rank == (slot % CAP).astype(jnp.float32))
    select = jnp.where(taken, 1.0, 0.0).astype(jnp.bfloat16)
    gate = jnp.where(taken, gate, 0.0)
    high = gate.astype(jnp.bfloat16)
    high_ref[...] = high
    low_ref[...] = (gate - high.astype(jnp.float32)).astype(jnp.bfloat16)
    sent = jnp.dot(select, rows_ref[...], preferred_element_type=jnp.float32)
    for index in range(slots // CAP):
        sent_ref[index] = sent[index * CAP : (index + 1) * CAP].astype(jnp.bfloat16)


def route(ep, expert_ids, expert_weights, k_rope, moe_rows, latent, ctx):
    row_count, features = moe_rows.shape
    slots = ctx * CAP
    return pl.pallas_call(
        route_kernel,
        out_shape=[
            jax.ShapeDtypeStruct((ctx, CAP, features), jnp.bfloat16),
            jax.ShapeDtypeStruct((slots, row_count), jnp.bfloat16),
            jax.ShapeDtypeStruct((slots, row_count), jnp.bfloat16),
            jax.ShapeDtypeStruct((HALF, latent.shape[1] + ROPE), jnp.bfloat16),
        ],
        in_specs=[SMEM_SPEC] + [VMEM_SPEC] * 5,
        out_specs=[VMEM_SPEC] * 4,
        compiler_params=pltpu.CompilerParams(vmem_limit_bytes=FULL),
        cost_estimate=pl.CostEstimate(
            flops=2 * row_count * slots * features, bytes_accessed=1 * MIB, transcendentals=0
        ),
        name="route",
    )(ep, expert_ids.T, expert_weights.T, k_rope.T, moe_rows, latent)


def weight_copies(ep_ref, flips, gate_hbm, up_hbm, gate, up, semaphores):
    features = gate.shape[1]
    copies = []
    for index, flip in enumerate(flips):
        place = pl.multiple_of((ep_ref[0] ^ flip) * features, features)
        for which, (source, target) in enumerate(((gate_hbm, gate), (up_hbm, up))):
            copy = pltpu.make_async_copy(
                source.at[0, pl.ds(place, features)], target.at[index], semaphores.at[index, which]
            )
            copy.start()
            copies.append(copy)
    return copies


def near_kernel(
    ep_ref,
    own_ref,
    core_ref,
    gate_hbm,
    up_hbm,
    down_hbm,
    sums_out,
    far_gate,
    far_up,
    down,
    gate,
    up,
    semaphores,
    far_semaphores,
    down_semaphores,
):
    units = gate.shape[2]
    features = gate.shape[1]
    copies = weight_copies(ep_ref, (0, 1), gate_hbm, up_hbm, gate, up, semaphores)
    later = weight_copies(ep_ref, (2, 3), gate_hbm, up_hbm, far_gate, far_up, far_semaphores)
    for flip in (3, 1, 2, 0):
        place = pl.multiple_of((ep_ref[0] ^ flip) * features, features)
        copy = pltpu.make_async_copy(
            down_hbm.at[0, :, pl.ds(place, features)], down.at[flip], down_semaphores.at[flip]
        )
        copy.start()
        later.append(copy)
    gate_sum, up_sum = None, None
    for index, x_ref in enumerate((own_ref, core_ref)):
        rows = x_ref[...]
        copies[2 * index].wait()
        part = jnp.dot(rows, gate[index], preferred_element_type=jnp.float32)
        gate_sum = part if gate_sum is None else gate_sum + part
        copies[2 * index + 1].wait()
        part = jnp.dot(rows, up[index], preferred_element_type=jnp.float32)
        up_sum = part if up_sum is None else up_sum + part
    sums_out[:, :units] = gate_sum
    sums_out[:, units:] = up_sum
    for copy in later:
        copy.wait()


def near_experts(ep, own, core, w_gate, w_up, w_down):
    slots, features = own.shape
    units = w_gate.shape[2]
    return pl.pallas_call(
        near_kernel,
        out_shape=[
            jax.ShapeDtypeStruct((slots, 2 * units), jnp.float32),
            jax.ShapeDtypeStruct((2, features, units), jnp.bfloat16),
            jax.ShapeDtypeStruct((2, features, units), jnp.bfloat16),
            jax.ShapeDtypeStruct((4, units, features), jnp.bfloat16),
        ],
        in_specs=[SMEM_SPEC] + [VMEM_SPEC] * 2 + [HBM_SPEC] * 3,
        out_specs=[VMEM_SPEC] * 4,
        scratch_shapes=[
            VMEM((2, features, units), jnp.bfloat16),
            VMEM((2, features, units), jnp.bfloat16),
            pltpu.SemaphoreType.DMA((2, 2)),
            pltpu.SemaphoreType.DMA((2, 2)),
            pltpu.SemaphoreType.DMA((4,)),
        ],
        compiler_params=pltpu.CompilerParams(vmem_limit_bytes=46 * MIB),
        cost_estimate=pl.CostEstimate(
            flops=8 * slots * features * units,
            bytes_accessed=24 * features * units,
            transcendentals=0,
        ),
        name="near_experts",
    )(ep, own, core, w_gate, w_up, w_down)


def far_kernel(
    far_ref, core_far_ref, sums_ref, gate, up, down, own_out, core_out, far_out, core_far_out
):
    units = gate.shape[2]
    gate_sum, up_sum = sums_ref[:, :units], sums_ref[:, units:]
    for index, x_ref in enumerate((far_ref, core_far_ref)):
        rows = x_ref[...]
        gate_sum = gate_sum + jnp.dot(rows, gate[index], preferred_element_type=jnp.float32)
        up_sum = up_sum + jnp.dot(rows, up[index], preferred_element_type=jnp.float32)
    hidden = (gate_sum / (1.0 + jnp.exp(-gate_sum)) * up_sum).astype(jnp.bfloat16)
    outs = (own_out, core_out, far_out, core_far_out)
    for flip in (3, 1, 2, 0):
        outs[flip][...] = jnp.dot(
            hidden, down[flip], preferred_element_type=jnp.float32
        ).astype(jnp.bfloat16)


def far_experts(far, core_far, sums, gate, up, down):
    slots, features = far.shape
    units = gate.shape[2]
    return pl.pallas_call(
        far_kernel,
        out_shape=[jax.ShapeDtypeStruct((slots, features), jnp.bfloat16)] * 4,
        in_specs=[VMEM_SPEC] * 6,
        out_specs=[VMEM_SPEC] * 4,
        compiler_params=pltpu.CompilerParams(vmem_limit_bytes=24 * MIB),
        cost_estimate=pl.CostEstimate(flops=0, bytes_accessed=0, transcendentals=0),
        name="far_experts",
    )(far, core_far, sums, gate, up, down)


def add_kernel(*refs):
    total = refs[0][...].astype(jnp.float32)
    for ref in refs[1:-1]:
        total = total + ref[...].astype(jnp.float32)
    refs[-1][...] = total.astype(jnp.bfloat16)


def add(*parts):
    return pl.pallas_call(
        add_kernel,
        out_shape=jax.ShapeDtypeStruct(parts[0].shape, jnp.bfloat16),
        in_specs=[VMEM_SPEC] * len(parts),
        out_specs=VMEM_SPEC,
        compiler_params=pltpu.CompilerParams(vmem_limit_bytes=8 * MIB),
        cost_estimate=pl.CostEstimate(flops=0, bytes_accessed=MIB, transcendentals=0),
        name="add",
    )(*parts)


def combine_kernel(high_ref, low_ref, returned_ref, out_ref):
    returned = returned_ref[...]
    total = lax.dot_general(high_ref[...], returned, TN, preferred_element_type=jnp.float32)
    total = total + lax.dot_general(
        low_ref[...], returned, TN, preferred_element_type=jnp.float32
    )
    out_ref[...] = total.astype(jnp.bfloat16)


def combine(high, low, returned):
    slots, row_count = high.shape
    features = returned.shape[1]
    return pl.pallas_call(
        combine_kernel,
        out_shape=jax.ShapeDtypeStruct((row_count, features), jnp.bfloat16),
        in_specs=[VMEM_SPEC] * 3,
        out_specs=VMEM_SPEC,
        compiler_params=pltpu.CompilerParams(vmem_limit_bytes=LIMIT),
        cost_estimate=pl.CostEstimate(
            flops=4 * row_count * slots * features, bytes_accessed=MIB, transcendentals=0
        ),
        name="combine",
    )(high, low, returned)


def low_run(my_ctx, positions_ref):
    mine = my_ctx * (2 * HALF)
    return jnp.where(positions_ref[mine] < positions_ref[mine + HALF], 0, 1)


def fold_kernel(own_ref, positions_ref, q_nope_ref, q_rope_ref, w_uk_ref, out_ref):
    latent_width = w_uk_ref.shape[0]
    low = low_run(own_ref[0], positions_ref)
    for head in range(GROUP):
        columns = slice(head * NOPE, (head + 1) * NOPE)
        folded = lax.dot_general(
            q_nope_ref[:, columns], w_uk_ref[:, columns], NT, preferred_element_type=jnp.float32
        ).astype(jnp.bfloat16)
        rotated = q_rope_ref[:, head * ROPE : (head + 1) * ROPE]
        for run in range(2):
            rows = slice(run * HALF, (run + 1) * HALF)
            place = slice(head * HALF, (head + 1) * HALF)
            slot = 1 - (low ^ run)
            out_ref[0, slot, place, :latent_width] = folded[rows]
            out_ref[0, slot, place, latent_width:] = rotated[rows]


def fold(own, positions, q_nope, q_rope, w_uk):
    query_count, columns = q_nope.shape
    heads = columns // NOPE
    latent_width = w_uk.shape[0]
    width = latent_width + ROPE
    steps = heads // GROUP // 2
    queries = pl.pallas_call(
        fold_kernel,
        out_shape=jax.ShapeDtypeStruct((2, 2, heads // 2 * HALF, width), jnp.bfloat16),
        grid=(2 * steps,),
        in_specs=[
            SMEM_SPEC,
            SMEM_SPEC,
            pl.BlockSpec((query_count, GROUP * NOPE), lambda step: (0, step)),
            pl.BlockSpec((query_count, GROUP * ROPE), lambda step: (0, step)),
            pl.BlockSpec((latent_width, GROUP * NOPE), lambda step: (0, step)),
        ],
        out_specs=pl.BlockSpec(
            (1, 2, GROUP * HALF, width), lambda step: (step // steps, 0, step % steps, 0)
        ),
        compiler_params=pltpu.CompilerParams(vmem_limit_bytes=FULL),
        cost_estimate=pl.CostEstimate(
            flops=2 * query_count * columns * latent_width,
            bytes_accessed=6 * MIB,
            transcendentals=0,
        ),
        name="fold",
    )(own, positions, q_nope, q_rope, w_uk)
    return queries.reshape(2, heads * HALF, width)


def attention_kernel(
    index,
    own_ref,
    ep_ref,
    positions_ref,
    queries_ref,
    w_uv_ref,
    own_keys,
    core_keys,
    *refs,
):
    done_ref = None
    if index:
        done_ref, *refs = refs
    out_ref, keys, *scratch = refs
    columns = w_uv_ref.shape[1] // 2
    blocks = own_keys.shape[0]
    my_ctx, my_ep = own_ref[0], ep_ref[0]
    for flip, source in enumerate((own_keys, core_keys)):
        for block in range(blocks):
            source_ctx = my_ctx
            for bit, step in enumerate(gather_order(blocks)):
                if block >> bit & 1:
                    source_ctx = source_ctx ^ step
            start = source_ctx * (2 * HALF) + ((my_ep % 2) ^ flip) * HALF
            place = pl.multiple_of(positions_ref[start], HALF)
            keys[pl.ds(place, HALF), :] = source[block]
    skipped = 0
    if index:
        skipped = columns
        out_ref[:, :columns] = done_ref[...]
    attend_heads(
        own_ref,
        positions_ref,
        queries_ref.at[index],
        w_uv_ref.at[:, pl.ds(index * columns, columns)],
        keys,
        out_ref,
        skipped,
        *scratch,
    )


def attend_heads(
    own_ref, positions_ref, queries, w_uv, keys, out_ref, skipped, scores, tops, mixed
):
    latent_width = w_uv.shape[0]
    count = queries.shape[0] // 2
    heads = count // HALF
    mine = own_ref[0] * (2 * HALF)
    low = low_run(own_ref[0], positions_ref)
    high = 1 - low
    low_base = positions_ref[mine + low * HALF]
    high_base = positions_ref[mine + high * HALF]
    tops[...] = jnp.full(tops.shape, -jnp.inf, jnp.float32)
    offset = lax.broadcasted_iota(jnp.int32, (HALF, CHUNK), 1) - lax.broadcasted_iota(
        jnp.int32, (HALF, CHUNK), 0
    )
    low_chunks = (low_base + HALF + CHUNK - 1) // CHUNK
    high_chunks = (high_base + HALF + CHUNK - 1) // CHUNK

    def score(chunk, bases):
        start = pl.multiple_of(chunk * CHUNK, CHUNK)
        part = lax.dot_general(
            queries[: len(bases) * count, :],
            keys[pl.ds(start, CHUNK), :],
            NT,
            preferred_element_type=jnp.float32,
        )
        for index, base in enumerate(bases):
            visible = offset <= base - start
            for head in range(heads):
                rows = slice(index * count + head * HALF, index * count + (head + 1) * HALF)
                seen = jnp.where(visible, part[rows], -jnp.inf)
                scores[chunk, rows, :] = seen
                top = tops[rows, :]
                for lane in range(0, CHUNK, 128):
                    top = jnp.maximum(top, seen[:, lane : lane + 128])
                tops[rows, :] = top
        return 0

    lax.fori_loop(0, low_chunks, lambda c, _: score(c, (high_base, low_base)), 0)
    lax.fori_loop(low_chunks, high_chunks, lambda c, _: score(c, (high_base,)), 0)
    factor = math.log2(math.e) / math.sqrt(NOPE + ROPE)

    def mix(rows, chunks):
        top = jnp.max(tops[rows, :], axis=1, keepdims=True) * factor
        total = jnp.zeros((count, 128), jnp.float32)
        parts = []
        for chunk in range(chunks):
            part = jnp.exp2(scores[chunk, rows, :] * factor - top)
            for lane in range(0, CHUNK, 128):
                total = total + part[:, lane : lane + 128]
            parts.append(part.astype(jnp.bfloat16))
        summed = jnp.dot(
            jnp.concatenate(parts, axis=1),
            keys[: chunks * CHUNK, :latent_width],
            preferred_element_type=jnp.float32,
        )
        share = 1.0 / jnp.sum(total, axis=1, keepdims=True)
        mixed[rows, :] = (summed * share).astype(jnp.bfloat16)

    most = keys.shape[0] // CHUNK
    for chunks in range(1, most + 1):

        @pl.when(high_chunks == chunks)
        def _():
            mix(slice(0, count), chunks)

        @pl.when(low_chunks == chunks)
        def _():
            mix(slice(count, 2 * count), chunks)

    high_rows = pl.ds(pl.multiple_of(high * HALF, HALF), HALF)
    low_rows = pl.ds(pl.multiple_of(low * HALF, HALF), HALF)
    for head in range(heads):
        both = jnp.concatenate(
            [
                mixed[head * HALF : (head + 1) * HALF, :],
                mixed[count + head * HALF : count + (head + 1) * HALF, :],
            ],
            axis=0,
        )
        value = jnp.dot(
            both, w_uv[:, head * VDIM : (head + 1) * VDIM], preferred_element_type=jnp.float32
        ).astype(jnp.bfloat16)
        columns = slice(skipped + head * VDIM, skipped + (head + 1) * VDIM)
        out_ref[high_rows, columns] = value[:HALF]
        out_ref[low_rows, columns] = value[HALF:]


def attend_scratch(count, key_count, latent_width):
    return [
        VMEM((key_count // CHUNK, 2 * count, CHUNK), jnp.float32),
        VMEM((2 * count, 128), jnp.float32),
        VMEM((2 * count, latent_width), jnp.bfloat16),
    ]


def attend_limit(key_count):
    return (12 + -(-9 * key_count // 1024)) * MIB


def attend_cost(count, key_count, width):
    return pl.CostEstimate(
        flops=3 * count * key_count * width,
        bytes_accessed=4 * MIB,
        transcendentals=count * key_count,
    )


def attend(index, own, ep, positions, queries, w_uv, own_keys, core_keys, *done):
    latent_width, columns = w_uv.shape
    key_count = positions.shape[0]
    width = own_keys.shape[-1]
    count = queries.shape[1] // 2
    return pl.pallas_call(
        functools.partial(attention_kernel, index),
        out_shape=jax.ShapeDtypeStruct((2 * HALF, (1 + index) * columns // 2), jnp.bfloat16),
        in_specs=[SMEM_SPEC] * 3 + [VMEM_SPEC] * (4 + len(done)),
        out_specs=VMEM_SPEC,
        scratch_shapes=[VMEM((key_count, width), jnp.bfloat16)]
        + attend_scratch(count, key_count, latent_width),
        compiler_params=pltpu.CompilerParams(vmem_limit_bytes=attend_limit(key_count)),
        cost_estimate=attend_cost(count, key_count, width),
        name="attention",
    )(own, ep, positions, queries, w_uv, own_keys, core_keys, *done)


def shards(
    q_nope,
    q_rope,
    latent,
    k_rope,
    w_uk,
    w_uv,
    positions,
    moe_rows,
    expert_ids,
    expert_weights,
    w_gate,
    w_up,
    w_down,
):
    ctx = lax.axis_size("ctx")
    me = lax.axis_index("ctx").astype(jnp.int32).reshape(1)
    ep = lax.axis_index("ep").astype(jnp.int32).reshape(1)

    def over_ctx(value, flip):
        return lax.ppermute(value, "ctx", [(i, i ^ flip) for i in range(ctx)])

    def over_ep(value, flip):
        return lax.ppermute(value, "ep", [(i, i ^ flip) for i in range(4)])

    def exchange(value):
        return lax.all_to_all(value, "ctx", split_axis=0, concat_axis=0, tiled=True)

    outgoing, high, low, packed = route(
        ep, expert_ids, expert_weights, k_rope, moe_rows, latent, ctx
    )
    arrived = exchange(outgoing)
    flips = gather_order(ctx)
    received = over_ctx(packed[None], flips[0])
    high, q_nope, received = lax.optimization_barrier((high, q_nope, received))
    queries = fold(me, positions, q_nope, q_rope, w_uk)
    own_keys = jnp.concatenate([packed[None], received], axis=0)
    for flip in flips[1:-1]:
        own_keys = jnp.concatenate([own_keys, over_ctx(own_keys, flip)], axis=0)
    arrived, queries, own_keys = lax.optimization_barrier((arrived, queries, own_keys))

    own = arrived.reshape(ctx * CAP, arrived.shape[2])
    far = over_ep(own, 2)
    core = over_ep(own, 1)
    received = over_ctx(own_keys, flips[-1])
    sums, far_gate, far_up, down = near_experts(ep, own, core, w_gate, w_up, w_down)
    far, sums = lax.optimization_barrier((far, sums))
    core_far = over_ep(far, 1)
    own_out, core_out, far_out, core_far_out = far_experts(
        far, core_far, sums, far_gate, far_up, down
    )
    core_far_out, received = lax.optimization_barrier((core_far_out, received))
    from_core_far = over_ep(core_far_out, 1)
    from_core = over_ep(core_out, 1)
    own_keys = jnp.concatenate([own_keys, received], axis=0)
    own_keys, from_core_far = lax.optimization_barrier((own_keys, from_core_far))
    to_far = add(far_out, from_core_far)
    from_far = over_ep(to_far, 2)
    core_keys = over_ep(own_keys, 1)
    half = attend(0, me, ep, positions, queries, w_uv, own_keys, core_keys)
    from_far, half = lax.optimization_barrier((from_far, half))
    returning = add(own_out, from_core, from_far)
    returned = exchange(returning.reshape(arrived.shape))
    attention = attend(1, me, ep, positions, queries, w_uv, own_keys, core_keys, half)
    moe_out = combine(high, low, returned.reshape(own.shape))
    return (attention, moe_out)


def solution(mesh):
    return jax.shard_map(
        shards,
        mesh=mesh,
        in_specs=(
            P("ctx", "ep"),
            P("ctx", "ep"),
            P("ctx", None),
            P("ctx", None),
            P(None, "ep"),
            P(None, "ep"),
            P(),
            P("ctx", "ep"),
            P("ctx", None),
            P("ctx", None),
            P("ctx", None, "ep"),
            P("ctx", None, "ep"),
            P("ctx", "ep", None),
        ),
        out_specs=(P("ctx", "ep"), P("ctx", "ep")),
        check_vma=False,
    )
```

```python
import math

import jax
import jax.numpy as jnp
from jax import lax
from jax.experimental import pallas as pl
from jax.experimental.pallas import tpu as pltpu
from jax.sharding import PartitionSpec as P

NOPE = 128
ROPE = 64
VDIM = 128
TOP = 8
CAP = 8
HALF = 64
GROUP = 4
MIB = 1 << 20
LIMIT = 52 * MIB
FULL = 60 * MIB
SMALL = 24 * MIB
CHUNK = 256

NT = (((1,), (1,)), ((), ()))
TN = (((0,), (0,)), ((), ()))
VMEM = pltpu.VMEM
SMEM_SPEC = pl.BlockSpec(memory_space=pltpu.SMEM)
VMEM_SPEC = pl.BlockSpec(memory_space=pltpu.VMEM)
HBM_SPEC = pl.BlockSpec(memory_space=pltpu.HBM)


def gather_order(ctx):
    bits = ctx.bit_length() - 1
    return [1 << (bits - 1)] + [1 << bit for bit in range(bits - 1)]


def route_kernel(
    ep_ref,
    ids_ref,
    weights_ref,
    rope_ref,
    rows_ref,
    latent_ref,
    sent_ref,
    high_ref,
    low_ref,
    packed_ref,
):
    latent_width = latent_ref.shape[1]
    rope = rope_ref[...].astype(jnp.float32).T
    for core in range(2):

        @pl.when(ep_ref[0] % 2 == core)
        def _():
            rows = slice(core * HALF, (core + 1) * HALF)
            packed_ref[:, :latent_width] = latent_ref[rows, :]
            packed_ref[:, latent_width:] = rope[rows].astype(jnp.bfloat16)

    row_count = ids_ref.shape[1]
    slots = sent_ref.shape[0] * CAP
    slot = lax.broadcasted_iota(jnp.int32, (slots, row_count), 0)
    expert = slot // CAP
    named = jnp.zeros((slots, row_count), jnp.float32)
    gate = jnp.zeros((slots, row_count), jnp.float32)
    for choice in range(TOP):
        match = ids_ref[choice : choice + 1, :] == expert
        named = jnp.where(match, 1.0, named)
        gate = jnp.where(match, weights_ref[choice : choice + 1, :], gate)
    row = lax.broadcasted_iota(jnp.int32, (row_count, row_count), 0)
    other = lax.broadcasted_iota(jnp.int32, (row_count, row_count), 1)
    before = jnp.where(row < other, 1.0, 0.0).astype(jnp.bfloat16)
    rank = jnp.dot(named.astype(jnp.bfloat16), before, preferred_element_type=jnp.float32)
    taken = (named > 0.0) & (rank == (slot % CAP).astype(jnp.float32))
    select = jnp.where(taken, 1.0, 0.0).astype(jnp.bfloat16)
    gate = jnp.where(taken, gate, 0.0)
    blocks = [gate[index * CAP : (index + 1) * CAP] for index in range(slots // CAP)]
    gate = jnp.concatenate([block for block in blocks for _ in range(2)], axis=0)
    high = gate.astype(jnp.bfloat16)
    high_ref[...] = high
    low_ref[...] = (gate - high.astype(jnp.float32)).astype(jnp.bfloat16)
    sent = jnp.dot(select, rows_ref[...], preferred_element_type=jnp.float32)
    for index in range(slots // CAP):
        sent_ref[index] = sent[index * CAP : (index + 1) * CAP].astype(jnp.bfloat16)


def route(ep, expert_ids, expert_weights, k_rope, moe_rows, latent, ctx):
    row_count, features = moe_rows.shape
    slots = ctx * CAP
    return pl.pallas_call(
        route_kernel,
        out_shape=[
            jax.ShapeDtypeStruct((ctx, CAP, features), jnp.bfloat16),
            jax.ShapeDtypeStruct((2 * slots, row_count), jnp.bfloat16),
            jax.ShapeDtypeStruct((2 * slots, row_count), jnp.bfloat16),
            jax.ShapeDtypeStruct((HALF, latent.shape[1] + ROPE), jnp.bfloat16),
        ],
        in_specs=[SMEM_SPEC] + [VMEM_SPEC] * 5,
        out_specs=[VMEM_SPEC] * 4,
        compiler_params=pltpu.CompilerParams(vmem_limit_bytes=FULL),
        cost_estimate=pl.CostEstimate(
            flops=2 * row_count * slots * features, bytes_accessed=1 * MIB, transcendentals=0
        ),
        name="route",
    )(ep, expert_ids.T, expert_weights.T, k_rope.T, moe_rows, latent)


def weight_copies(ep_ref, flips, gate_hbm, up_hbm, gate, up, semaphores):
    features = gate.shape[1]
    copies = []
    for index, flip in enumerate(flips):
        place = pl.multiple_of((ep_ref[0] ^ flip) * features, features)
        for which, (source, target) in enumerate(((gate_hbm, gate), (up_hbm, up))):
            copy = pltpu.make_async_copy(
                source.at[0, pl.ds(place, features)], target.at[index], semaphores.at[index, which]
            )
            copy.start()
            copies.append(copy)
    return copies


def near_kernel(
    ep_ref,
    own_ref,
    core_ref,
    gate_hbm,
    up_hbm,
    down_hbm,
    sums_out,
    far_gate,
    far_up,
    down,
    gate,
    up,
    semaphores,
    far_semaphores,
    down_semaphores,
):
    units = gate.shape[2]
    features = gate.shape[1]
    copies = weight_copies(ep_ref, (0, 1), gate_hbm, up_hbm, gate, up, semaphores)
    later = weight_copies(ep_ref, (2, 3), gate_hbm, up_hbm, far_gate, far_up, far_semaphores)
    for flip in (3, 1, 2, 0):
        place = pl.multiple_of((ep_ref[0] ^ flip) * features, features)
        copy = pltpu.make_async_copy(
            down_hbm.at[0, :, pl.ds(place, features)], down.at[flip], down_semaphores.at[flip]
        )
        copy.start()
        later.append(copy)
    gate_sum, up_sum = None, None
    for index, x_ref in enumerate((own_ref, core_ref)):
        rows = x_ref[...]
        copies[2 * index].wait()
        part = jnp.dot(rows, gate[index], preferred_element_type=jnp.float32)
        gate_sum = part if gate_sum is None else gate_sum + part
        copies[2 * index + 1].wait()
        part = jnp.dot(rows, up[index], preferred_element_type=jnp.float32)
        up_sum = part if up_sum is None else up_sum + part
    sums_out[:, :units] = gate_sum
    sums_out[:, units:] = up_sum
    for copy in later:
        copy.wait()


def near_experts(ep, own, core, w_gate, w_up, w_down):
    slots, features = own.shape
    units = w_gate.shape[2]
    return pl.pallas_call(
        near_kernel,
        out_shape=[
            jax.ShapeDtypeStruct((slots, 2 * units), jnp.float32),
            jax.ShapeDtypeStruct((2, features, units), jnp.bfloat16),
            jax.ShapeDtypeStruct((2, features, units), jnp.bfloat16),
            jax.ShapeDtypeStruct((4, units, features), jnp.bfloat16),
        ],
        in_specs=[SMEM_SPEC] + [VMEM_SPEC] * 2 + [HBM_SPEC] * 3,
        out_specs=[VMEM_SPEC] * 4,
        scratch_shapes=[
            VMEM((2, features, units), jnp.bfloat16),
            VMEM((2, features, units), jnp.bfloat16),
            pltpu.SemaphoreType.DMA((2, 2)),
            pltpu.SemaphoreType.DMA((2, 2)),
            pltpu.SemaphoreType.DMA((4,)),
        ],
        compiler_params=pltpu.CompilerParams(vmem_limit_bytes=46 * MIB),
        cost_estimate=pl.CostEstimate(
            flops=8 * slots * features * units,
            bytes_accessed=24 * features * units,
            transcendentals=0,
        ),
        name="near_experts",
    )(ep, own, core, w_gate, w_up, w_down)


def far_kernel(
    far_ref, core_far_ref, sums_ref, gate, up, down, own_out, core_out, far_out, core_far_out
):
    units = gate.shape[2]
    gate_sum, up_sum = sums_ref[:, :units], sums_ref[:, units:]
    for index, x_ref in enumerate((far_ref, core_far_ref)):
        rows = x_ref[...]
        gate_sum = gate_sum + jnp.dot(rows, gate[index], preferred_element_type=jnp.float32)
        up_sum = up_sum + jnp.dot(rows, up[index], preferred_element_type=jnp.float32)
    hidden = (gate_sum / (1.0 + jnp.exp(-gate_sum)) * up_sum).astype(jnp.bfloat16)
    outs = (own_out, core_out, far_out, core_far_out)
    for flip in (3, 1, 2, 0):
        outs[flip][...] = jnp.dot(
            hidden, down[flip], preferred_element_type=jnp.float32
        ).astype(jnp.bfloat16)


def far_experts(far, core_far, sums, gate, up, down):
    slots, features = far.shape
    units = gate.shape[2]
    return pl.pallas_call(
        far_kernel,
        out_shape=[jax.ShapeDtypeStruct((slots, features), jnp.bfloat16)] * 4,
        in_specs=[VMEM_SPEC] * 6,
        out_specs=[VMEM_SPEC] * 4,
        compiler_params=pltpu.CompilerParams(vmem_limit_bytes=24 * MIB),
        cost_estimate=pl.CostEstimate(flops=0, bytes_accessed=0, transcendentals=0),
        name="far_experts",
    )(far, core_far, sums, gate, up, down)


def sum_kernel(ep_ref, own_ref, from_core_ref, far_ref, from_core_far_ref, out_ref):
    my_x = ep_ref[0] // 2
    for flip, (mine, other) in enumerate(
        ((own_ref, from_core_ref), (far_ref, from_core_far_ref))
    ):
        total = mine[...].astype(jnp.float32) + other[...].astype(jnp.float32)
        for index in range(out_ref.shape[0]):
            block = total[index * CAP : (index + 1) * CAP].astype(jnp.bfloat16)
            out_ref[index, my_x ^ flip] = block


def sum_cores(ep, own, from_core, far, from_core_far, ctx):
    features = own.shape[1]
    return pl.pallas_call(
        sum_kernel,
        out_shape=jax.ShapeDtypeStruct((ctx, 2, CAP, features), jnp.bfloat16),
        in_specs=[SMEM_SPEC] + [VMEM_SPEC] * 4,
        out_specs=VMEM_SPEC,
        compiler_params=pltpu.CompilerParams(vmem_limit_bytes=16 * MIB),
        cost_estimate=pl.CostEstimate(flops=0, bytes_accessed=MIB, transcendentals=0),
        name="sum_cores",
    )(ep, own, from_core, far, from_core_far)


def combine_kernel(high_ref, low_ref, returned_ref, out_ref):
    returned = returned_ref[...]
    total = lax.dot_general(high_ref[...], returned, TN, preferred_element_type=jnp.float32)
    total = total + lax.dot_general(
        low_ref[...], returned, TN, preferred_element_type=jnp.float32
    )
    out_ref[...] = total.astype(jnp.bfloat16)


def combine(high, low, returned):
    slots, row_count = high.shape
    features = returned.shape[1]
    return pl.pallas_call(
        combine_kernel,
        out_shape=jax.ShapeDtypeStruct((row_count, features), jnp.bfloat16),
        in_specs=[VMEM_SPEC] * 3,
        out_specs=VMEM_SPEC,
        compiler_params=pltpu.CompilerParams(vmem_limit_bytes=LIMIT),
        cost_estimate=pl.CostEstimate(
            flops=4 * row_count * slots * features, bytes_accessed=MIB, transcendentals=0
        ),
        name="combine",
    )(high, low, returned)


def low_run(my_ctx, positions_ref):
    mine = my_ctx * (2 * HALF)
    return jnp.where(positions_ref[mine] < positions_ref[mine + HALF], 0, 1)


def fold_kernel(own_ref, positions_ref, q_nope_ref, q_rope_ref, w_uk_ref, out_ref):
    latent_width = w_uk_ref.shape[0]
    low = low_run(own_ref[0], positions_ref)
    for head in range(GROUP):
        columns = slice(head * NOPE, (head + 1) * NOPE)
        folded = lax.dot_general(
            q_nope_ref[:, columns], w_uk_ref[:, columns], NT, preferred_element_type=jnp.float32
        ).astype(jnp.bfloat16)
        rotated = q_rope_ref[:, head * ROPE : (head + 1) * ROPE]
        for run in range(2):
            rows = slice(run * HALF, (run + 1) * HALF)
            place = slice(head * HALF, (head + 1) * HALF)
            slot = 1 - (low ^ run)
            out_ref[0, slot, place, :latent_width] = folded[rows]
            out_ref[0, slot, place, latent_width:] = rotated[rows]


def fold(own, positions, q_nope, q_rope, w_uk):
    query_count, columns = q_nope.shape
    heads = columns // NOPE
    latent_width = w_uk.shape[0]
    width = latent_width + ROPE
    steps = heads // GROUP // 2
    queries = pl.pallas_call(
        fold_kernel,
        out_shape=jax.ShapeDtypeStruct((2, 2, heads // 2 * HALF, width), jnp.bfloat16),
        grid=(2 * steps,),
        in_specs=[
            SMEM_SPEC,
            SMEM_SPEC,
            pl.BlockSpec((query_count, GROUP * NOPE), lambda step: (0, step)),
            pl.BlockSpec((query_count, GROUP * ROPE), lambda step: (0, step)),
            pl.BlockSpec((latent_width, GROUP * NOPE), lambda step: (0, step)),
        ],
        out_specs=pl.BlockSpec(
            (1, 2, GROUP * HALF, width), lambda step: (step // steps, 0, step % steps, 0)
        ),
        compiler_params=pltpu.CompilerParams(vmem_limit_bytes=FULL),
        cost_estimate=pl.CostEstimate(
            flops=2 * query_count * columns * latent_width,
            bytes_accessed=6 * MIB,
            transcendentals=0,
        ),
        name="fold",
    )(own, positions, q_nope, q_rope, w_uk)
    return queries.reshape(2, heads * HALF, width)


def attention_kernel(
    own_ref,
    ep_ref,
    positions_ref,
    queries_hbm,
    w_uv_hbm,
    own_keys,
    core_keys,
    out_ref,
    keys,
    queries,
    w_uv,
    scores,
    tops,
    mixed,
    semaphores,
):
    query_copies = [
        pltpu.make_async_copy(queries_hbm.at[part], queries.at[part], semaphores.at[part])
        for part in range(2)
    ]
    w_uv_copy = pltpu.make_async_copy(w_uv_hbm, w_uv, semaphores.at[2])
    for copy in (query_copies[0], w_uv_copy, query_copies[1]):
        copy.start()
    blocks = own_keys.shape[0]
    my_ctx, my_ep = own_ref[0], ep_ref[0]
    for flip, source in enumerate((own_keys, core_keys)):
        for block in range(blocks):
            source_ctx = my_ctx
            for bit, step in enumerate(gather_order(blocks)):
                if block >> bit & 1:
                    source_ctx = source_ctx ^ step
            start = source_ctx * (2 * HALF) + ((my_ep % 2) ^ flip) * HALF
            place = pl.multiple_of(positions_ref[start], HALF)
            keys[pl.ds(place, HALF), :] = source[block]
    for part in range(2):
        query_copies[part].wait()
        attend_heads(
            own_ref,
            positions_ref,
            queries.at[part],
            w_uv,
            keys,
            out_ref,
            part * (w_uv.shape[1] // 2),
            scores,
            tops,
            mixed,
            w_uv_copy.wait if not part else lambda: None,
        )


def attend_heads(
    own_ref, positions_ref, queries, w_uv, keys, out_ref, skipped, scores, tops, mixed, wait
):
    latent_width = w_uv.shape[0]
    count = queries.shape[0] // 2
    heads = count // HALF
    mine = own_ref[0] * (2 * HALF)
    low = low_run(own_ref[0], positions_ref)
    high = 1 - low
    low_base = positions_ref[mine + low * HALF]
    high_base = positions_ref[mine + high * HALF]
    tops[...] = jnp.full(tops.shape, -jnp.inf, jnp.float32)
    offset = lax.broadcasted_iota(jnp.int32, (HALF, CHUNK), 1) - lax.broadcasted_iota(
        jnp.int32, (HALF, CHUNK), 0
    )
    low_chunks = (low_base + HALF + CHUNK - 1) // CHUNK
    high_chunks = (high_base + HALF + CHUNK - 1) // CHUNK

    def score(chunk, bases):
        start = pl.multiple_of(chunk * CHUNK, CHUNK)
        part = lax.dot_general(
            queries[: len(bases) * count, :],
            keys[pl.ds(start, CHUNK), :],
            NT,
            preferred_element_type=jnp.float32,
        )
        for index, base in enumerate(bases):
            visible = offset <= base - start
            for head in range(heads):
                rows = slice(index * count + head * HALF, index * count + (head + 1) * HALF)
                seen = jnp.where(visible, part[rows], -jnp.inf)
                scores[chunk, rows, :] = seen
                top = tops[rows, :]
                for lane in range(0, CHUNK, 128):
                    top = jnp.maximum(top, seen[:, lane : lane + 128])
                tops[rows, :] = top
        return 0

    lax.fori_loop(0, low_chunks, lambda c, _: score(c, (high_base, low_base)), 0)
    lax.fori_loop(low_chunks, high_chunks, lambda c, _: score(c, (high_base,)), 0)
    factor = math.log2(math.e) / math.sqrt(NOPE + ROPE)

    def mix(rows, chunks):
        top = jnp.max(tops[rows, :], axis=1, keepdims=True) * factor
        total = jnp.zeros((count, 128), jnp.float32)
        parts = []
        for chunk in range(chunks):
            part = jnp.exp2(scores[chunk, rows, :] * factor - top)
            for lane in range(0, CHUNK, 128):
                total = total + part[:, lane : lane + 128]
            parts.append(part.astype(jnp.bfloat16))
        summed = jnp.dot(
            jnp.concatenate(parts, axis=1),
            keys[: chunks * CHUNK, :latent_width],
            preferred_element_type=jnp.float32,
        )
        share = 1.0 / jnp.sum(total, axis=1, keepdims=True)
        mixed[rows, :] = (summed * share).astype(jnp.bfloat16)

    most = keys.shape[0] // CHUNK
    for chunks in range(1, most + 1):

        @pl.when(high_chunks == chunks)
        def _():
            mix(slice(0, count), chunks)

        @pl.when(low_chunks == chunks)
        def _():
            mix(slice(count, 2 * count), chunks)

    wait()
    high_rows = pl.ds(pl.multiple_of(high * HALF, HALF), HALF)
    low_rows = pl.ds(pl.multiple_of(low * HALF, HALF), HALF)
    for head in range(heads):
        both = jnp.concatenate(
            [
                mixed[head * HALF : (head + 1) * HALF, :],
                mixed[count + head * HALF : count + (head + 1) * HALF, :],
            ],
            axis=0,
        )
        columns = slice(skipped + head * VDIM, skipped + (head + 1) * VDIM)
        value = jnp.dot(
            both, w_uv[:, columns], preferred_element_type=jnp.float32
        ).astype(jnp.bfloat16)
        out_ref[high_rows, columns] = value[:HALF]
        out_ref[low_rows, columns] = value[HALF:]


def attend(own, ep, positions, queries, w_uv, own_keys, core_keys):
    latent_width, columns = w_uv.shape
    key_count = positions.shape[0]
    width = own_keys.shape[-1]
    rows = queries.shape[1]
    return pl.pallas_call(
        attention_kernel,
        out_shape=jax.ShapeDtypeStruct((2 * HALF, columns), jnp.bfloat16),
        in_specs=[SMEM_SPEC] * 3 + [HBM_SPEC] * 2 + [VMEM_SPEC] * 2,
        out_specs=VMEM_SPEC,
        scratch_shapes=[
            VMEM((key_count, width), jnp.bfloat16),
            VMEM(queries.shape, jnp.bfloat16),
            VMEM(w_uv.shape, jnp.bfloat16),
            VMEM((key_count // CHUNK, rows, CHUNK), jnp.float32),
            VMEM((rows, 128), jnp.float32),
            VMEM((rows, latent_width), jnp.bfloat16),
            pltpu.SemaphoreType.DMA((3,)),
        ],
        compiler_params=pltpu.CompilerParams(vmem_limit_bytes=61 * MIB),
        cost_estimate=pl.CostEstimate(flops=0, bytes_accessed=0, transcendentals=0),
        name="attention",
    )(own, ep, positions, queries, w_uv, own_keys, core_keys)


def shards(
    q_nope,
    q_rope,
    latent,
    k_rope,
    w_uk,
    w_uv,
    positions,
    moe_rows,
    expert_ids,
    expert_weights,
    w_gate,
    w_up,
    w_down,
):
    ctx = lax.axis_size("ctx")
    me = lax.axis_index("ctx").astype(jnp.int32).reshape(1)
    ep = lax.axis_index(("x", "core")).astype(jnp.int32).reshape(1)

    def over_ctx(value, flip):
        return lax.ppermute(value, "ctx", [(i, i ^ flip) for i in range(ctx)])

    def over(value, axis):
        return lax.ppermute(value, axis, [(0, 1), (1, 0)])

    outgoing, high, low, packed = route(
        ep, expert_ids, expert_weights, k_rope, moe_rows, latent, ctx
    )
    arrived = lax.all_to_all(outgoing, "ctx", split_axis=0, concat_axis=0, tiled=True)
    high, q_nope = lax.optimization_barrier((high, q_nope))
    queries = fold(me, positions, q_nope, q_rope, w_uk)
    flips = gather_order(ctx)
    own_keys = packed[None]
    for flip in flips[:-2]:
        own_keys = jnp.concatenate([own_keys, over_ctx(own_keys, flip)], axis=0)
    arrived, queries = lax.optimization_barrier((arrived, queries))

    own = arrived.reshape(ctx * CAP, arrived.shape[2])
    far = over(own, "x")
    core = over(own, "core")
    received = over_ctx(own_keys, flips[-2])
    sums, far_gate, far_up, down = near_experts(ep, own, core, w_gate, w_up, w_down)
    far, sums, received = lax.optimization_barrier((far, sums, received))
    core_far = over(far, "core")
    own_keys = jnp.concatenate([own_keys, received], axis=0)
    received = over_ctx(own_keys, flips[-1])
    own_out, core_out, far_out, core_far_out = far_experts(
        far, core_far, sums, far_gate, far_up, down
    )
    from_core_far = over(core_far_out, "core")
    from_core = over(core_out, "core")
    returning = sum_cores(ep, own_out, from_core, far_out, from_core_far, ctx)
    returning, received = lax.optimization_barrier((returning, received))
    returned = lax.all_to_all(
        returning.reshape(2 * ctx, CAP, returning.shape[3]),
        ("ctx", "x"),
        split_axis=0,
        concat_axis=0,
        tiled=True,
    )
    own_keys = jnp.concatenate([own_keys, received], axis=0)
    core_keys = over(own_keys, "core")
    attention = attend(me, ep, positions, queries, w_uv, own_keys, core_keys)
    moe_out = combine(high, low, returned.reshape(2 * ctx * CAP, returned.shape[2]))
    return (attention, moe_out)


def solution(mesh):
    split = (mesh.shape["ctx"], mesh.shape["ep"] // 2, 2)
    mesh = jax.sharding.Mesh(mesh.devices.reshape(split), ("ctx", "x", "core"))
    ep = ("x", "core")
    return jax.shard_map(
        shards,
        mesh=mesh,
        in_specs=(
            P("ctx", ep),
            P("ctx", ep),
            P("ctx", None),
            P("ctx", None),
            P(None, ep),
            P(None, ep),
            P(),
            P("ctx", ep),
            P("ctx", None),
            P("ctx", None),
            P("ctx", None, ep),
            P("ctx", None, ep),
            P("ctx", ep, None),
        ),
        out_specs=(P("ctx", ep), P("ctx", ep)),
        check_vma=False,
    )
```

```python
import math

import jax
import jax.numpy as jnp
from jax import lax
from jax.experimental import pallas as pl
from jax.experimental.pallas import tpu as pltpu
from jax.sharding import PartitionSpec as P

NOPE = 128
ROPE = 64
VDIM = 128
TOP = 8
CAP = 8
HALF = 64
GROUP = 4
MIB = 1 << 20
LIMIT = 52 * MIB
FULL = 60 * MIB
SMALL = 24 * MIB
CHUNK = 256

NT = (((1,), (1,)), ((), ()))
TN = (((0,), (0,)), ((), ()))
VMEM = pltpu.VMEM
SMEM_SPEC = pl.BlockSpec(memory_space=pltpu.SMEM)
VMEM_SPEC = pl.BlockSpec(memory_space=pltpu.VMEM)
HBM_SPEC = pl.BlockSpec(memory_space=pltpu.HBM)


def gather_order(ctx):
    bits = ctx.bit_length() - 1
    return [1 << (bits - 1)] + [1 << bit for bit in range(bits - 1)]


def route_kernel(
    ep_ref,
    ids_ref,
    weights_ref,
    rope_ref,
    rows_ref,
    latent_ref,
    sent_ref,
    high_ref,
    low_ref,
    packed_ref,
):
    latent_width = latent_ref.shape[1]
    rope = rope_ref[...].astype(jnp.float32).T
    for core in range(2):

        @pl.when(ep_ref[0] % 2 == core)
        def _():
            rows = slice(core * HALF, (core + 1) * HALF)
            packed_ref[:, :latent_width] = latent_ref[rows, :]
            packed_ref[:, latent_width:] = rope[rows].astype(jnp.bfloat16)

    row_count = ids_ref.shape[1]
    slots = sent_ref.shape[0] * CAP
    slot = lax.broadcasted_iota(jnp.int32, (slots, row_count), 0)
    expert = slot // CAP
    named = jnp.zeros((slots, row_count), jnp.float32)
    gate = jnp.zeros((slots, row_count), jnp.float32)
    for choice in range(TOP):
        match = ids_ref[choice : choice + 1, :] == expert
        named = jnp.where(match, 1.0, named)
        gate = jnp.where(match, weights_ref[choice : choice + 1, :], gate)
    row = lax.broadcasted_iota(jnp.int32, (row_count, row_count), 0)
    other = lax.broadcasted_iota(jnp.int32, (row_count, row_count), 1)
    before = jnp.where(row < other, 1.0, 0.0).astype(jnp.bfloat16)
    rank = jnp.dot(named.astype(jnp.bfloat16), before, preferred_element_type=jnp.float32)
    taken = (named > 0.0) & (rank == (slot % CAP).astype(jnp.float32))
    select = jnp.where(taken, 1.0, 0.0).astype(jnp.bfloat16)
    gate = jnp.where(taken, gate, 0.0)
    blocks = [gate[index * CAP : (index + 1) * CAP] for index in range(slots // CAP)]
    gate = jnp.concatenate([block for block in blocks for _ in range(2)], axis=0)
    high = gate.astype(jnp.bfloat16)
    high_ref[...] = high
    low_ref[...] = (gate - high.astype(jnp.float32)).astype(jnp.bfloat16)
    sent = jnp.dot(select, rows_ref[...], preferred_element_type=jnp.float32)
    for index in range(slots // CAP):
        sent_ref[index] = sent[index * CAP : (index + 1) * CAP].astype(jnp.bfloat16)


def route(ep, expert_ids, expert_weights, k_rope, moe_rows, latent, ctx):
    row_count, features = moe_rows.shape
    slots = ctx * CAP
    return pl.pallas_call(
        route_kernel,
        out_shape=[
            jax.ShapeDtypeStruct((ctx, CAP, features), jnp.bfloat16),
            jax.ShapeDtypeStruct((2 * slots, row_count), jnp.bfloat16),
            jax.ShapeDtypeStruct((2 * slots, row_count), jnp.bfloat16),
            jax.ShapeDtypeStruct((HALF, latent.shape[1] + ROPE), jnp.bfloat16),
        ],
        in_specs=[SMEM_SPEC] + [VMEM_SPEC] * 5,
        out_specs=[VMEM_SPEC] * 4,
        compiler_params=pltpu.CompilerParams(vmem_limit_bytes=FULL),
        cost_estimate=pl.CostEstimate(
            flops=2 * row_count * slots * features, bytes_accessed=1 * MIB, transcendentals=0
        ),
        name="route",
    )(ep, expert_ids.T, expert_weights.T, k_rope.T, moe_rows, latent)


def weight_copies(ep_ref, flips, gate_hbm, up_hbm, gate, up, semaphores):
    features = gate.shape[1]
    copies = []
    for index, flip in enumerate(flips):
        place = pl.multiple_of((ep_ref[0] ^ flip) * features, features)
        for which, (source, target) in enumerate(((gate_hbm, gate), (up_hbm, up))):
            copy = pltpu.make_async_copy(
                source.at[0, pl.ds(place, features)], target.at[index], semaphores.at[index, which]
            )
            copy.start()
            copies.append(copy)
    return copies


def near_kernel(
    ep_ref,
    own_ref,
    core_ref,
    gate_hbm,
    up_hbm,
    down_hbm,
    sums_out,
    far_gate,
    far_up,
    down,
    gate,
    up,
    semaphores,
    far_semaphores,
    down_semaphores,
):
    units = gate.shape[2]
    features = gate.shape[1]
    copies = weight_copies(ep_ref, (0, 1), gate_hbm, up_hbm, gate, up, semaphores)
    later = weight_copies(ep_ref, (2, 3), gate_hbm, up_hbm, far_gate, far_up, far_semaphores)
    for flip in (3, 1, 2, 0):
        place = pl.multiple_of((ep_ref[0] ^ flip) * features, features)
        copy = pltpu.make_async_copy(
            down_hbm.at[0, :, pl.ds(place, features)], down.at[flip], down_semaphores.at[flip]
        )
        copy.start()
        later.append(copy)
    gate_sum, up_sum = None, None
    for index, x_ref in enumerate((own_ref, core_ref)):
        rows = x_ref[...]
        copies[2 * index].wait()
        part = jnp.dot(rows, gate[index], preferred_element_type=jnp.float32)
        gate_sum = part if gate_sum is None else gate_sum + part
        copies[2 * index + 1].wait()
        part = jnp.dot(rows, up[index], preferred_element_type=jnp.float32)
        up_sum = part if up_sum is None else up_sum + part
    sums_out[:, :units] = gate_sum
    sums_out[:, units:] = up_sum
    for copy in later:
        copy.wait()


def near_experts(ep, own, core, w_gate, w_up, w_down):
    slots, features = own.shape
    units = w_gate.shape[2]
    return pl.pallas_call(
        near_kernel,
        out_shape=[
            jax.ShapeDtypeStruct((slots, 2 * units), jnp.float32),
            jax.ShapeDtypeStruct((2, features, units), jnp.bfloat16),
            jax.ShapeDtypeStruct((2, features, units), jnp.bfloat16),
            jax.ShapeDtypeStruct((4, units, features), jnp.bfloat16),
        ],
        in_specs=[SMEM_SPEC] + [VMEM_SPEC] * 2 + [HBM_SPEC] * 3,
        out_specs=[VMEM_SPEC] * 4,
        scratch_shapes=[
            VMEM((2, features, units), jnp.bfloat16),
            VMEM((2, features, units), jnp.bfloat16),
            pltpu.SemaphoreType.DMA((2, 2)),
            pltpu.SemaphoreType.DMA((2, 2)),
            pltpu.SemaphoreType.DMA((4,)),
        ],
        compiler_params=pltpu.CompilerParams(vmem_limit_bytes=46 * MIB),
        cost_estimate=pl.CostEstimate(
            flops=8 * slots * features * units,
            bytes_accessed=24 * features * units,
            transcendentals=0,
        ),
        name="near_experts",
    )(ep, own, core, w_gate, w_up, w_down)


def far_kernel(
    far_ref, core_far_ref, sums_ref, gate, up, down, own_out, core_out, far_out, core_far_out
):
    units = gate.shape[2]
    gate_sum, up_sum = sums_ref[:, :units], sums_ref[:, units:]
    for index, x_ref in enumerate((far_ref, core_far_ref)):
        rows = x_ref[...]
        gate_sum = gate_sum + jnp.dot(rows, gate[index], preferred_element_type=jnp.float32)
        up_sum = up_sum + jnp.dot(rows, up[index], preferred_element_type=jnp.float32)
    hidden = (gate_sum / (1.0 + jnp.exp(-gate_sum)) * up_sum).astype(jnp.bfloat16)
    outs = (own_out, core_out, far_out, core_far_out)
    for flip in (3, 1, 2, 0):
        outs[flip][...] = jnp.dot(
            hidden, down[flip], preferred_element_type=jnp.float32
        ).astype(jnp.bfloat16)


def far_experts(far, core_far, sums, gate, up, down):
    slots, features = far.shape
    units = gate.shape[2]
    return pl.pallas_call(
        far_kernel,
        out_shape=[jax.ShapeDtypeStruct((slots, features), jnp.bfloat16)] * 4,
        in_specs=[VMEM_SPEC] * 6,
        out_specs=[VMEM_SPEC] * 4,
        compiler_params=pltpu.CompilerParams(vmem_limit_bytes=24 * MIB),
        cost_estimate=pl.CostEstimate(flops=0, bytes_accessed=0, transcendentals=0),
        name="far_experts",
    )(far, core_far, sums, gate, up, down)


def sum_kernel(ep_ref, own_ref, from_core_ref, far_ref, from_core_far_ref, out_ref):
    my_x = ep_ref[0] // 2
    for flip, (mine, other) in enumerate(
        ((own_ref, from_core_ref), (far_ref, from_core_far_ref))
    ):
        total = mine[...].astype(jnp.float32) + other[...].astype(jnp.float32)
        for index in range(out_ref.shape[0]):
            block = total[index * CAP : (index + 1) * CAP].astype(jnp.bfloat16)
            out_ref[index, my_x ^ flip] = block


def sum_cores(ep, own, from_core, far, from_core_far, ctx):
    features = own.shape[1]
    return pl.pallas_call(
        sum_kernel,
        out_shape=jax.ShapeDtypeStruct((ctx, 2, CAP, features), jnp.bfloat16),
        in_specs=[SMEM_SPEC] + [VMEM_SPEC] * 4,
        out_specs=VMEM_SPEC,
        compiler_params=pltpu.CompilerParams(vmem_limit_bytes=16 * MIB),
        cost_estimate=pl.CostEstimate(flops=0, bytes_accessed=MIB, transcendentals=0),
        name="sum_cores",
    )(ep, own, from_core, far, from_core_far)


def combine_kernel(high_ref, low_ref, returned_ref, out_ref):
    returned = returned_ref[...]
    total = lax.dot_general(high_ref[...], returned, TN, preferred_element_type=jnp.float32)
    total = total + lax.dot_general(
        low_ref[...], returned, TN, preferred_element_type=jnp.float32
    )
    out_ref[...] = total.astype(jnp.bfloat16)


def combine(high, low, returned):
    slots, row_count = high.shape
    features = returned.shape[1]
    return pl.pallas_call(
        combine_kernel,
        out_shape=jax.ShapeDtypeStruct((row_count, features), jnp.bfloat16),
        in_specs=[VMEM_SPEC] * 3,
        out_specs=VMEM_SPEC,
        compiler_params=pltpu.CompilerParams(vmem_limit_bytes=LIMIT),
        cost_estimate=pl.CostEstimate(
            flops=4 * row_count * slots * features, bytes_accessed=MIB, transcendentals=0
        ),
        name="combine",
    )(high, low, returned)


def low_run(my_ctx, positions_ref):
    mine = my_ctx * (2 * HALF)
    return jnp.where(positions_ref[mine] < positions_ref[mine + HALF], 0, 1)


def fold_kernel(own_ref, positions_ref, q_nope_ref, q_rope_ref, w_uk_ref, out_ref):
    latent_width = w_uk_ref.shape[0]
    low = low_run(own_ref[0], positions_ref)
    for head in range(GROUP):
        columns = slice(head * NOPE, (head + 1) * NOPE)
        folded = lax.dot_general(
            q_nope_ref[:, columns], w_uk_ref[:, columns], NT, preferred_element_type=jnp.float32
        ).astype(jnp.bfloat16)
        rotated = q_rope_ref[:, head * ROPE : (head + 1) * ROPE]
        for run in range(2):
            rows = slice(run * HALF, (run + 1) * HALF)
            place = slice(head * HALF, (head + 1) * HALF)
            slot = 1 - (low ^ run)
            out_ref[0, slot, place, :latent_width] = folded[rows]
            out_ref[0, slot, place, latent_width:] = rotated[rows]


def fold(own, positions, q_nope, q_rope, w_uk):
    query_count, columns = q_nope.shape
    heads = columns // NOPE
    latent_width = w_uk.shape[0]
    width = latent_width + ROPE
    steps = heads // GROUP // 2
    queries = pl.pallas_call(
        fold_kernel,
        out_shape=jax.ShapeDtypeStruct((2, 2, heads // 2 * HALF, width), jnp.bfloat16),
        grid=(2 * steps,),
        in_specs=[
            SMEM_SPEC,
            SMEM_SPEC,
            pl.BlockSpec((query_count, GROUP * NOPE), lambda step: (0, step)),
            pl.BlockSpec((query_count, GROUP * ROPE), lambda step: (0, step)),
            pl.BlockSpec((latent_width, GROUP * NOPE), lambda step: (0, step)),
        ],
        out_specs=pl.BlockSpec(
            (1, 2, GROUP * HALF, width), lambda step: (step // steps, 0, step % steps, 0)
        ),
        compiler_params=pltpu.CompilerParams(vmem_limit_bytes=FULL),
        cost_estimate=pl.CostEstimate(
            flops=2 * query_count * columns * latent_width,
            bytes_accessed=6 * MIB,
            transcendentals=0,
        ),
        name="fold",
    )(own, positions, q_nope, q_rope, w_uk)
    return queries.reshape(2, heads * HALF, width)


def attention_kernel(
    own_ref,
    ep_ref,
    positions_ref,
    queries_hbm,
    w_uv_hbm,
    own_keys,
    core_keys,
    out_ref,
    keys,
    queries,
    w_uv,
    scores,
    tops,
    mixed,
    semaphores,
):
    query_copies = [
        pltpu.make_async_copy(queries_hbm.at[part], queries.at[part], semaphores.at[part])
        for part in range(2)
    ]
    w_uv_copy = pltpu.make_async_copy(w_uv_hbm, w_uv, semaphores.at[2])
    for copy in (query_copies[0], w_uv_copy, query_copies[1]):
        copy.start()
    blocks = own_keys.shape[0]
    my_ctx, my_ep = own_ref[0], ep_ref[0]
    for flip, source in enumerate((own_keys, core_keys)):
        for block in range(blocks):
            source_ctx = my_ctx
            for bit, step in enumerate(gather_order(blocks)):
                if block >> bit & 1:
                    source_ctx = source_ctx ^ step
            start = source_ctx * (2 * HALF) + ((my_ep % 2) ^ flip) * HALF
            place = pl.multiple_of(positions_ref[start], HALF)
            keys[pl.ds(place, HALF), :] = source[block]
    for part in range(2):
        query_copies[part].wait()
        attend_heads(
            own_ref,
            positions_ref,
            queries.at[part],
            w_uv,
            keys,
            out_ref,
            part * (w_uv.shape[1] // 2),
            scores,
            tops,
            mixed,
            w_uv_copy.wait if not part else lambda: None,
        )


def attend_heads(
    own_ref, positions_ref, queries, w_uv, keys, out_ref, skipped, scores, tops, mixed, wait
):
    latent_width = w_uv.shape[0]
    count = queries.shape[0] // 2
    heads = count // HALF
    mine = own_ref[0] * (2 * HALF)
    low = low_run(own_ref[0], positions_ref)
    high = 1 - low
    low_base = positions_ref[mine + low * HALF]
    high_base = positions_ref[mine + high * HALF]
    tops[...] = jnp.full(tops.shape, -jnp.inf, jnp.float32)
    offset = lax.broadcasted_iota(jnp.int32, (HALF, CHUNK), 1) - lax.broadcasted_iota(
        jnp.int32, (HALF, CHUNK), 0
    )
    low_chunks = (low_base + HALF + CHUNK - 1) // CHUNK
    high_chunks = (high_base + HALF + CHUNK - 1) // CHUNK

    def score(chunk, bases):
        start = pl.multiple_of(chunk * CHUNK, CHUNK)
        part = lax.dot_general(
            queries[: len(bases) * count, :],
            keys[pl.ds(start, CHUNK), :],
            NT,
            preferred_element_type=jnp.float32,
        )
        for index, base in enumerate(bases):
            visible = offset <= base - start
            for head in range(heads):
                rows = slice(index * count + head * HALF, index * count + (head + 1) * HALF)
                seen = jnp.where(visible, part[rows], -jnp.inf)
                scores[chunk, rows, :] = seen
                top = tops[rows, :]
                for lane in range(0, CHUNK, 128):
                    top = jnp.maximum(top, seen[:, lane : lane + 128])
                tops[rows, :] = top
        return 0

    lax.fori_loop(0, low_chunks, lambda c, _: score(c, (high_base, low_base)), 0)
    lax.fori_loop(low_chunks, high_chunks, lambda c, _: score(c, (high_base,)), 0)
    factor = math.log2(math.e) / math.sqrt(NOPE + ROPE)

    def mix(rows, chunks):
        top = jnp.max(tops[rows, :], axis=1, keepdims=True) * factor
        total = jnp.zeros((count, 128), jnp.float32)
        parts = []
        for chunk in range(chunks):
            part = jnp.exp2(scores[chunk, rows, :] * factor - top)
            for lane in range(0, CHUNK, 128):
                total = total + part[:, lane : lane + 128]
            parts.append(part.astype(jnp.bfloat16))
        summed = jnp.dot(
            jnp.concatenate(parts, axis=1),
            keys[: chunks * CHUNK, :latent_width],
            preferred_element_type=jnp.float32,
        )
        share = 1.0 / jnp.sum(total, axis=1, keepdims=True)
        mixed[rows, :] = (summed * share).astype(jnp.bfloat16)

    most = keys.shape[0] // CHUNK
    for chunks in range(1, most + 1):

        @pl.when(high_chunks == chunks)
        def _():
            mix(slice(0, count), chunks)

        @pl.when(low_chunks == chunks)
        def _():
            mix(slice(count, 2 * count), chunks)

    wait()
    high_rows = pl.ds(pl.multiple_of(high * HALF, HALF), HALF)
    low_rows = pl.ds(pl.multiple_of(low * HALF, HALF), HALF)
    for head in range(heads):
        both = jnp.concatenate(
            [
                mixed[head * HALF : (head + 1) * HALF, :],
                mixed[count + head * HALF : count + (head + 1) * HALF, :],
            ],
            axis=0,
        )
        columns = slice(skipped + head * VDIM, skipped + (head + 1) * VDIM)
        value = jnp.dot(
            both, w_uv[:, columns], preferred_element_type=jnp.float32
        ).astype(jnp.bfloat16)
        out_ref[high_rows, columns] = value[:HALF]
        out_ref[low_rows, columns] = value[HALF:]


def attend(own, ep, positions, queries, w_uv, own_keys, core_keys):
    latent_width, columns = w_uv.shape
    key_count = positions.shape[0]
    width = own_keys.shape[-1]
    rows = queries.shape[1]
    return pl.pallas_call(
        attention_kernel,
        out_shape=jax.ShapeDtypeStruct((2 * HALF, columns), jnp.bfloat16),
        in_specs=[SMEM_SPEC] * 3 + [HBM_SPEC] * 2 + [VMEM_SPEC] * 2,
        out_specs=VMEM_SPEC,
        scratch_shapes=[
            VMEM((key_count, width), jnp.bfloat16),
            VMEM(queries.shape, jnp.bfloat16),
            VMEM(w_uv.shape, jnp.bfloat16),
            VMEM((key_count // CHUNK, rows, CHUNK), jnp.float32),
            VMEM((rows, 128), jnp.float32),
            VMEM((rows, latent_width), jnp.bfloat16),
            pltpu.SemaphoreType.DMA((3,)),
        ],
        compiler_params=pltpu.CompilerParams(vmem_limit_bytes=52 * MIB),
        cost_estimate=pl.CostEstimate(flops=0, bytes_accessed=0, transcendentals=0),
        name="attention",
    )(own, ep, positions, queries, w_uv, own_keys, core_keys)


def shards(
    q_nope,
    q_rope,
    latent,
    k_rope,
    w_uk,
    w_uv,
    positions,
    moe_rows,
    expert_ids,
    expert_weights,
    w_gate,
    w_up,
    w_down,
):
    ctx = lax.axis_size("ctx")
    me = lax.axis_index("ctx").astype(jnp.int32).reshape(1)
    ep = lax.axis_index(("x", "core")).astype(jnp.int32).reshape(1)

    def over_ctx(value, flip):
        return lax.ppermute(value, "ctx", [(i, i ^ flip) for i in range(ctx)])

    def over(value, axis):
        return lax.ppermute(value, axis, [(0, 1), (1, 0)])

    outgoing, high, low, packed = route(
        ep, expert_ids, expert_weights, k_rope, moe_rows, latent, ctx
    )
    arrived = lax.all_to_all(outgoing, "ctx", split_axis=0, concat_axis=0, tiled=True)
    flips = gather_order(ctx)
    received = over_ctx(packed[None], flips[0])
    high, q_nope, received = lax.optimization_barrier((high, q_nope, received))
    queries = fold(me, positions, q_nope, q_rope, w_uk)
    own_keys = jnp.concatenate([packed[None], received], axis=0)
    for flip in flips[1:-1]:
        own_keys = jnp.concatenate([own_keys, over_ctx(own_keys, flip)], axis=0)
    arrived, queries, own_keys = lax.optimization_barrier((arrived, queries, own_keys))

    own = arrived.reshape(ctx * CAP, arrived.shape[2])
    far = over(own, "x")
    core = over(own, "core")
    received = over_ctx(own_keys, flips[-1])
    sums, far_gate, far_up, down = near_experts(ep, own, core, w_gate, w_up, w_down)
    far, sums = lax.optimization_barrier((far, sums))
    core_far = over(far, "core")
    own_out, core_out, far_out, core_far_out = far_experts(
        far, core_far, sums, far_gate, far_up, down
    )
    core_far_out, received = lax.optimization_barrier((core_far_out, received))
    from_core_far = over(core_far_out, "core")
    from_core = over(core_out, "core")
    own_keys = jnp.concatenate([own_keys, received], axis=0)
    own_keys, from_core_far = lax.optimization_barrier((own_keys, from_core_far))
    core_keys = over(own_keys, "core")
    returning = sum_cores(ep, own_out, from_core, far_out, from_core_far, ctx)
    returned = lax.all_to_all(
        returning.reshape(2 * ctx, CAP, returning.shape[3]),
        ("ctx", "x"),
        split_axis=0,
        concat_axis=0,
        tiled=True,
    )
    attention = attend(me, ep, positions, queries, w_uv, own_keys, core_keys)
    moe_out = combine(high, low, returned.reshape(2 * ctx * CAP, returned.shape[2]))
    return (attention, moe_out)


def solution(mesh):
    split = (mesh.shape["ctx"], mesh.shape["ep"] // 2, 2)
    mesh = jax.sharding.Mesh(mesh.devices.reshape(split), ("ctx", "x", "core"))
    ep = ("x", "core")
    return jax.shard_map(
        shards,
        mesh=mesh,
        in_specs=(
            P("ctx", ep),
            P("ctx", ep),
            P("ctx", None),
            P("ctx", None),
            P(None, ep),
            P(None, ep),
            P(),
            P("ctx", ep),
            P("ctx", None),
            P("ctx", None),
            P("ctx", None, ep),
            P("ctx", None, ep),
            P("ctx", ep, None),
        ),
        out_specs=(P("ctx", ep), P("ctx", ep)),
        check_vma=False,
    )
```

```python
import math

import jax
import jax.numpy as jnp
from jax import lax
from jax.experimental import pallas as pl
from jax.experimental.pallas import tpu as pltpu
from jax.sharding import PartitionSpec as P

NOPE = 128
ROPE = 64
VDIM = 128
TOP = 8
CAP = 8
HALF = 64
GROUP = 4
MIB = 1 << 20
LIMIT = 52 * MIB
FULL = 60 * MIB
SMALL = 24 * MIB
CHUNK = 256

NT = (((1,), (1,)), ((), ()))
TN = (((0,), (0,)), ((), ()))
VMEM = pltpu.VMEM
SMEM_SPEC = pl.BlockSpec(memory_space=pltpu.SMEM)
VMEM_SPEC = pl.BlockSpec(memory_space=pltpu.VMEM)
HBM_SPEC = pl.BlockSpec(memory_space=pltpu.HBM)


def gather_order(ctx):
    bits = ctx.bit_length() - 1
    return [1 << (bits - 1)] + [1 << bit for bit in range(bits - 1)]


def route_kernel(
    ep_ref,
    ids_ref,
    weights_ref,
    rope_ref,
    rows_ref,
    latent_ref,
    sent_ref,
    high_ref,
    low_ref,
    packed_ref,
):
    latent_width = latent_ref.shape[1]
    rope = rope_ref[...].astype(jnp.float32).T
    for core in range(2):

        @pl.when(ep_ref[0] % 2 == core)
        def _():
            rows = slice(core * HALF, (core + 1) * HALF)
            packed_ref[:, :latent_width] = latent_ref[rows, :]
            packed_ref[:, latent_width:] = rope[rows].astype(jnp.bfloat16)

    row_count = ids_ref.shape[1]
    slots = sent_ref.shape[0] * CAP
    slot = lax.broadcasted_iota(jnp.int32, (slots, row_count), 0)
    expert = slot // CAP
    named = jnp.zeros((slots, row_count), jnp.float32)
    gate = jnp.zeros((slots, row_count), jnp.float32)
    for choice in range(TOP):
        match = ids_ref[choice : choice + 1, :] == expert
        named = jnp.where(match, 1.0, named)
        gate = jnp.where(match, weights_ref[choice : choice + 1, :], gate)
    row = lax.broadcasted_iota(jnp.int32, (row_count, row_count), 0)
    other = lax.broadcasted_iota(jnp.int32, (row_count, row_count), 1)
    before = jnp.where(row < other, 1.0, 0.0).astype(jnp.bfloat16)
    rank = jnp.dot(named.astype(jnp.bfloat16), before, preferred_element_type=jnp.float32)
    taken = (named > 0.0) & (rank == (slot % CAP).astype(jnp.float32))
    select = jnp.where(taken, 1.0, 0.0).astype(jnp.bfloat16)
    gate = jnp.where(taken, gate, 0.0)
    blocks = [gate[index * CAP : (index + 1) * CAP] for index in range(slots // CAP)]
    gate = jnp.concatenate([block for block in blocks for _ in range(2)], axis=0)
    high = gate.astype(jnp.bfloat16)
    high_ref[...] = high
    low_ref[...] = (gate - high.astype(jnp.float32)).astype(jnp.bfloat16)
    sent = jnp.dot(select, rows_ref[...], preferred_element_type=jnp.float32)
    for index in range(slots // CAP):
        sent_ref[index] = sent[index * CAP : (index + 1) * CAP].astype(jnp.bfloat16)


def route(ep, expert_ids, expert_weights, k_rope, moe_rows, latent, ctx):
    row_count, features = moe_rows.shape
    slots = ctx * CAP
    return pl.pallas_call(
        route_kernel,
        out_shape=[
            jax.ShapeDtypeStruct((ctx, CAP, features), jnp.bfloat16),
            jax.ShapeDtypeStruct((2 * slots, row_count), jnp.bfloat16),
            jax.ShapeDtypeStruct((2 * slots, row_count), jnp.bfloat16),
            jax.ShapeDtypeStruct((HALF, latent.shape[1] + ROPE), jnp.bfloat16),
        ],
        in_specs=[SMEM_SPEC] + [VMEM_SPEC] * 5,
        out_specs=[VMEM_SPEC] * 4,
        compiler_params=pltpu.CompilerParams(vmem_limit_bytes=FULL),
        cost_estimate=pl.CostEstimate(
            flops=2 * row_count * slots * features, bytes_accessed=1 * MIB, transcendentals=0
        ),
        name="route",
    )(ep, expert_ids.T, expert_weights.T, k_rope.T, moe_rows, latent)


def weight_copies(ep_ref, flips, gate_hbm, up_hbm, gate, up, semaphores):
    features = gate.shape[1]
    copies = []
    for index, flip in enumerate(flips):
        place = pl.multiple_of((ep_ref[0] ^ flip) * features, features)
        for which, (source, target) in enumerate(((gate_hbm, gate), (up_hbm, up))):
            copy = pltpu.make_async_copy(
                source.at[0, pl.ds(place, features)], target.at[index], semaphores.at[index, which]
            )
            copy.start()
            copies.append(copy)
    return copies


def near_kernel(
    ep_ref,
    own_ref,
    core_ref,
    gate_hbm,
    up_hbm,
    down_hbm,
    sums_out,
    far_gate,
    far_up,
    down,
    gate,
    up,
    semaphores,
    far_semaphores,
    down_semaphores,
):
    units = gate.shape[2]
    features = gate.shape[1]
    copies = weight_copies(ep_ref, (0, 1), gate_hbm, up_hbm, gate, up, semaphores)
    later = weight_copies(ep_ref, (2, 3), gate_hbm, up_hbm, far_gate, far_up, far_semaphores)
    for flip in (3, 1, 2, 0):
        place = pl.multiple_of((ep_ref[0] ^ flip) * features, features)
        copy = pltpu.make_async_copy(
            down_hbm.at[0, :, pl.ds(place, features)], down.at[flip], down_semaphores.at[flip]
        )
        copy.start()
        later.append(copy)
    gate_sum, up_sum = None, None
    for index, x_ref in enumerate((own_ref, core_ref)):
        rows = x_ref[...]
        copies[2 * index].wait()
        part = jnp.dot(rows, gate[index], preferred_element_type=jnp.float32)
        gate_sum = part if gate_sum is None else gate_sum + part
        copies[2 * index + 1].wait()
        part = jnp.dot(rows, up[index], preferred_element_type=jnp.float32)
        up_sum = part if up_sum is None else up_sum + part
    sums_out[:, :units] = gate_sum
    sums_out[:, units:] = up_sum
    for copy in later:
        copy.wait()


def near_experts(ep, own, core, w_gate, w_up, w_down):
    slots, features = own.shape
    units = w_gate.shape[2]
    return pl.pallas_call(
        near_kernel,
        out_shape=[
            jax.ShapeDtypeStruct((slots, 2 * units), jnp.float32),
            jax.ShapeDtypeStruct((2, features, units), jnp.bfloat16),
            jax.ShapeDtypeStruct((2, features, units), jnp.bfloat16),
            jax.ShapeDtypeStruct((4, units, features), jnp.bfloat16),
        ],
        in_specs=[SMEM_SPEC] + [VMEM_SPEC] * 2 + [HBM_SPEC] * 3,
        out_specs=[VMEM_SPEC] * 4,
        scratch_shapes=[
            VMEM((2, features, units), jnp.bfloat16),
            VMEM((2, features, units), jnp.bfloat16),
            pltpu.SemaphoreType.DMA((2, 2)),
            pltpu.SemaphoreType.DMA((2, 2)),
            pltpu.SemaphoreType.DMA((4,)),
        ],
        compiler_params=pltpu.CompilerParams(vmem_limit_bytes=46 * MIB),
        cost_estimate=pl.CostEstimate(
            flops=8 * slots * features * units,
            bytes_accessed=24 * features * units,
            transcendentals=0,
        ),
        name="near_experts",
    )(ep, own, core, w_gate, w_up, w_down)


def far_kernel(
    far_ref, core_far_ref, sums_ref, gate, up, down, own_out, core_out, far_out, core_far_out
):
    units = gate.shape[2]
    gate_sum, up_sum = sums_ref[:, :units], sums_ref[:, units:]
    for index, x_ref in enumerate((far_ref, core_far_ref)):
        rows = x_ref[...]
        gate_sum = gate_sum + jnp.dot(rows, gate[index], preferred_element_type=jnp.float32)
        up_sum = up_sum + jnp.dot(rows, up[index], preferred_element_type=jnp.float32)
    hidden = (gate_sum / (1.0 + jnp.exp(-gate_sum)) * up_sum).astype(jnp.bfloat16)
    outs = (own_out, core_out, far_out, core_far_out)
    for flip in (3, 1, 2, 0):
        outs[flip][...] = jnp.dot(
            hidden, down[flip], preferred_element_type=jnp.float32
        ).astype(jnp.bfloat16)


def far_experts(far, core_far, sums, gate, up, down):
    slots, features = far.shape
    units = gate.shape[2]
    return pl.pallas_call(
        far_kernel,
        out_shape=[jax.ShapeDtypeStruct((slots, features), jnp.bfloat16)] * 4,
        in_specs=[VMEM_SPEC] * 6,
        out_specs=[VMEM_SPEC] * 4,
        compiler_params=pltpu.CompilerParams(vmem_limit_bytes=24 * MIB),
        cost_estimate=pl.CostEstimate(flops=0, bytes_accessed=0, transcendentals=0),
        name="far_experts",
    )(far, core_far, sums, gate, up, down)


def sum_kernel(ep_ref, own_ref, from_core_ref, far_ref, from_core_far_ref, out_ref):
    my_x = ep_ref[0] // 2
    for flip, (mine, other) in enumerate(
        ((own_ref, from_core_ref), (far_ref, from_core_far_ref))
    ):
        total = mine[...].astype(jnp.float32) + other[...].astype(jnp.float32)
        for index in range(out_ref.shape[0]):
            block = total[index * CAP : (index + 1) * CAP].astype(jnp.bfloat16)
            out_ref[index, my_x ^ flip] = block


def sum_cores(ep, own, from_core, far, from_core_far, ctx):
    features = own.shape[1]
    return pl.pallas_call(
        sum_kernel,
        out_shape=jax.ShapeDtypeStruct((ctx, 2, CAP, features), jnp.bfloat16),
        in_specs=[SMEM_SPEC] + [VMEM_SPEC] * 4,
        out_specs=VMEM_SPEC,
        compiler_params=pltpu.CompilerParams(vmem_limit_bytes=16 * MIB),
        cost_estimate=pl.CostEstimate(flops=0, bytes_accessed=MIB, transcendentals=0),
        name="sum_cores",
    )(ep, own, from_core, far, from_core_far)


def combine_kernel(high_ref, low_ref, returned_ref, out_ref):
    returned = returned_ref[...]
    total = lax.dot_general(high_ref[...], returned, TN, preferred_element_type=jnp.float32)
    total = total + lax.dot_general(
        low_ref[...], returned, TN, preferred_element_type=jnp.float32
    )
    out_ref[...] = total.astype(jnp.bfloat16)


def combine(high, low, returned):
    slots, row_count = high.shape
    features = returned.shape[1]
    return pl.pallas_call(
        combine_kernel,
        out_shape=jax.ShapeDtypeStruct((row_count, features), jnp.bfloat16),
        in_specs=[VMEM_SPEC] * 3,
        out_specs=VMEM_SPEC,
        compiler_params=pltpu.CompilerParams(vmem_limit_bytes=LIMIT),
        cost_estimate=pl.CostEstimate(
            flops=4 * row_count * slots * features, bytes_accessed=MIB, transcendentals=0
        ),
        name="combine",
    )(high, low, returned)


def low_run(my_ctx, positions_ref):
    mine = my_ctx * (2 * HALF)
    return jnp.where(positions_ref[mine] < positions_ref[mine + HALF], 0, 1)


def fold_kernel(own_ref, positions_ref, q_nope_ref, q_rope_ref, w_uk_ref, out_ref):
    latent_width = w_uk_ref.shape[0]
    low = low_run(own_ref[0], positions_ref)
    for head in range(GROUP):
        columns = slice(head * NOPE, (head + 1) * NOPE)
        folded = lax.dot_general(
            q_nope_ref[:, columns], w_uk_ref[:, columns], NT, preferred_element_type=jnp.float32
        ).astype(jnp.bfloat16)
        rotated = q_rope_ref[:, head * ROPE : (head + 1) * ROPE]
        for run in range(2):
            rows = slice(run * HALF, (run + 1) * HALF)
            place = slice(head * HALF, (head + 1) * HALF)
            slot = 1 - (low ^ run)
            out_ref[0, slot, place, :latent_width] = folded[rows]
            out_ref[0, slot, place, latent_width:] = rotated[rows]


def fold(own, positions, q_nope, q_rope, w_uk):
    query_count, columns = q_nope.shape
    heads = columns // NOPE
    latent_width = w_uk.shape[0]
    width = latent_width + ROPE
    steps = heads // GROUP // 2
    queries = pl.pallas_call(
        fold_kernel,
        out_shape=jax.ShapeDtypeStruct((2, 2, heads // 2 * HALF, width), jnp.bfloat16),
        grid=(2 * steps,),
        in_specs=[
            SMEM_SPEC,
            SMEM_SPEC,
            pl.BlockSpec((query_count, GROUP * NOPE), lambda step: (0, step)),
            pl.BlockSpec((query_count, GROUP * ROPE), lambda step: (0, step)),
            pl.BlockSpec((latent_width, GROUP * NOPE), lambda step: (0, step)),
        ],
        out_specs=pl.BlockSpec(
            (1, 2, GROUP * HALF, width), lambda step: (step // steps, 0, step % steps, 0)
        ),
        compiler_params=pltpu.CompilerParams(vmem_limit_bytes=FULL),
        cost_estimate=pl.CostEstimate(
            flops=2 * query_count * columns * latent_width,
            bytes_accessed=6 * MIB,
            transcendentals=0,
        ),
        name="fold",
    )(own, positions, q_nope, q_rope, w_uk)
    return queries.reshape(2, heads * HALF, width)


def attention_kernel(
    own_ref,
    ep_ref,
    positions_ref,
    queries_hbm,
    w_uv_hbm,
    own_keys,
    core_keys,
    out_ref,
    keys,
    queries,
    w_uv,
    scores,
    tops,
    mixed,
    semaphores,
):
    query_copies = [
        pltpu.make_async_copy(queries_hbm.at[part], queries.at[part], semaphores.at[part])
        for part in range(2)
    ]
    w_uv_copy = pltpu.make_async_copy(w_uv_hbm, w_uv, semaphores.at[2])
    for copy in (query_copies[0], w_uv_copy, query_copies[1]):
        copy.start()
    blocks = own_keys.shape[0]
    my_ctx, my_ep = own_ref[0], ep_ref[0]
    for flip, source in enumerate((own_keys, core_keys)):
        for block in range(blocks):
            source_ctx = my_ctx
            for bit, step in enumerate(gather_order(blocks)):
                if block >> bit & 1:
                    source_ctx = source_ctx ^ step
            start = source_ctx * (2 * HALF) + ((my_ep % 2) ^ flip) * HALF
            place = pl.multiple_of(positions_ref[start], HALF)
            keys[pl.ds(place, HALF), :] = source[block]
    for part in range(2):
        query_copies[part].wait()
        attend_heads(
            own_ref,
            positions_ref,
            queries.at[part],
            w_uv,
            keys,
            out_ref,
            part * (w_uv.shape[1] // 2),
            scores,
            tops,
            mixed,
            w_uv_copy.wait if not part else lambda: None,
        )


def attend_heads(
    own_ref, positions_ref, queries, w_uv, keys, out_ref, skipped, scores, tops, mixed, wait
):
    latent_width = w_uv.shape[0]
    count = queries.shape[0] // 2
    heads = count // HALF
    mine = own_ref[0] * (2 * HALF)
    low = low_run(own_ref[0], positions_ref)
    high = 1 - low
    low_base = positions_ref[mine + low * HALF]
    high_base = positions_ref[mine + high * HALF]
    tops[...] = jnp.full(tops.shape, -jnp.inf, jnp.float32)
    offset = lax.broadcasted_iota(jnp.int32, (HALF, CHUNK), 1) - lax.broadcasted_iota(
        jnp.int32, (HALF, CHUNK), 0
    )
    low_chunks = (low_base + HALF + CHUNK - 1) // CHUNK
    high_chunks = (high_base + HALF + CHUNK - 1) // CHUNK

    def score(chunk, bases):
        start = pl.multiple_of(chunk * CHUNK, CHUNK)
        part = lax.dot_general(
            queries[: len(bases) * count, :],
            keys[pl.ds(start, CHUNK), :],
            NT,
            preferred_element_type=jnp.float32,
        )
        for index, base in enumerate(bases):
            visible = offset <= base - start
            for head in range(heads):
                rows = slice(index * count + head * HALF, index * count + (head + 1) * HALF)
                seen = jnp.where(visible, part[rows], -jnp.inf)
                scores[chunk, rows, :] = seen
                top = tops[rows, :]
                for lane in range(0, CHUNK, 128):
                    top = jnp.maximum(top, seen[:, lane : lane + 128])
                tops[rows, :] = top
        return 0

    lax.fori_loop(0, low_chunks, lambda c, _: score(c, (high_base, low_base)), 0)
    lax.fori_loop(low_chunks, high_chunks, lambda c, _: score(c, (high_base,)), 0)
    factor = math.log2(math.e) / math.sqrt(NOPE + ROPE)

    def mix(rows, chunks):
        top = jnp.max(tops[rows, :], axis=1, keepdims=True) * factor
        total = jnp.zeros((count, 128), jnp.float32)
        parts = []
        for chunk in range(chunks):
            part = jnp.exp2(scores[chunk, rows, :] * factor - top)
            for lane in range(0, CHUNK, 128):
                total = total + part[:, lane : lane + 128]
            parts.append(part.astype(jnp.bfloat16))
        summed = jnp.dot(
            jnp.concatenate(parts, axis=1),
            keys[: chunks * CHUNK, :latent_width],
            preferred_element_type=jnp.float32,
        )
        share = 1.0 / jnp.sum(total, axis=1, keepdims=True)
        mixed[rows, :] = (summed * share).astype(jnp.bfloat16)

    most = keys.shape[0] // CHUNK
    for chunks in range(1, most + 1):

        @pl.when(high_chunks == chunks)
        def _():
            mix(slice(0, count), chunks)

        @pl.when(low_chunks == chunks)
        def _():
            mix(slice(count, 2 * count), chunks)

    wait()
    high_rows = pl.ds(pl.multiple_of(high * HALF, HALF), HALF)
    low_rows = pl.ds(pl.multiple_of(low * HALF, HALF), HALF)
    for head in range(heads):
        both = jnp.concatenate(
            [
                mixed[head * HALF : (head + 1) * HALF, :],
                mixed[count + head * HALF : count + (head + 1) * HALF, :],
            ],
            axis=0,
        )
        columns = slice(skipped + head * VDIM, skipped + (head + 1) * VDIM)
        value = jnp.dot(
            both, w_uv[:, columns], preferred_element_type=jnp.float32
        ).astype(jnp.bfloat16)
        out_ref[high_rows, columns] = value[:HALF]
        out_ref[low_rows, columns] = value[HALF:]


def attend(own, ep, positions, queries, w_uv, own_keys, core_keys):
    latent_width, columns = w_uv.shape
    key_count = positions.shape[0]
    width = own_keys.shape[-1]
    rows = queries.shape[1]
    return pl.pallas_call(
        attention_kernel,
        out_shape=jax.ShapeDtypeStruct((2 * HALF, columns), jnp.bfloat16),
        in_specs=[SMEM_SPEC] * 3 + [HBM_SPEC] * 2 + [VMEM_SPEC] * 2,
        out_specs=VMEM_SPEC,
        scratch_shapes=[
            VMEM((key_count, width), jnp.bfloat16),
            VMEM(queries.shape, jnp.bfloat16),
            VMEM(w_uv.shape, jnp.bfloat16),
            VMEM((key_count // CHUNK, rows, CHUNK), jnp.float32),
            VMEM((rows, 128), jnp.float32),
            VMEM((rows, latent_width), jnp.bfloat16),
            pltpu.SemaphoreType.DMA((3,)),
        ],
        compiler_params=pltpu.CompilerParams(vmem_limit_bytes=52 * MIB),
        cost_estimate=pl.CostEstimate(flops=0, bytes_accessed=0, transcendentals=0),
        name="attention",
    )(own, ep, positions, queries, w_uv, own_keys, core_keys)


def shards(
    q_nope,
    q_rope,
    latent,
    k_rope,
    w_uk,
    w_uv,
    positions,
    moe_rows,
    expert_ids,
    expert_weights,
    w_gate,
    w_up,
    w_down,
):
    ctx = lax.axis_size("ctx")
    me = lax.axis_index("ctx").astype(jnp.int32).reshape(1)
    ep = lax.axis_index(("x", "core")).astype(jnp.int32).reshape(1)

    def over_ctx(value, flip):
        return lax.ppermute(value, "ctx", [(i, i ^ flip) for i in range(ctx)])

    def over(value, axis):
        return lax.ppermute(value, axis, [(0, 1), (1, 0)])

    outgoing, high, low, packed = route(
        ep, expert_ids, expert_weights, k_rope, moe_rows, latent, ctx
    )
    arrived = lax.all_to_all(outgoing, "ctx", split_axis=0, concat_axis=0, tiled=True)
    flips = gather_order(ctx)
    received = over_ctx(packed[None], flips[0])
    high, q_nope, received = lax.optimization_barrier((high, q_nope, received))
    queries = fold(me, positions, q_nope, q_rope, w_uk)
    own_keys = jnp.concatenate([packed[None], received], axis=0)
    for flip in flips[1:-1]:
        own_keys = jnp.concatenate([own_keys, over_ctx(own_keys, flip)], axis=0)
    arrived, queries, own_keys = lax.optimization_barrier((arrived, queries, own_keys))

    own = arrived.reshape(ctx * CAP, arrived.shape[2])
    far = over(own, "x")
    core = over(own, "core")
    received = over_ctx(own_keys, flips[-1])
    sums, far_gate, far_up, down = near_experts(ep, own, core, w_gate, w_up, w_down)
    far, sums = lax.optimization_barrier((far, sums))
    core_far = over(far, "core")
    own_out, core_out, far_out, core_far_out = far_experts(
        far, core_far, sums, far_gate, far_up, down
    )
    core_far_out, received = lax.optimization_barrier((core_far_out, received))
    from_core_far = over(core_far_out, "core")
    from_core = over(core_out, "core")
    own_keys = jnp.concatenate([own_keys, received], axis=0)
    own_keys, from_core_far = lax.optimization_barrier((own_keys, from_core_far))
    core_keys = over(own_keys, "core")
    returning = sum_cores(ep, own_out, from_core, far_out, from_core_far, ctx)
    returning, core_keys = lax.optimization_barrier((returning, core_keys))
    returned = lax.all_to_all(
        returning.reshape(2 * ctx, CAP, returning.shape[3]),
        ("ctx", "x"),
        split_axis=0,
        concat_axis=0,
        tiled=True,
    )
    attention = attend(me, ep, positions, queries, w_uv, own_keys, core_keys)
    moe_out = combine(high, low, returned.reshape(2 * ctx * CAP, returned.shape[2]))
    return (attention, moe_out)


def solution(mesh):
    split = (mesh.shape["ctx"], mesh.shape["ep"] // 2, 2)
    mesh = jax.sharding.Mesh(mesh.devices.reshape(split), ("ctx", "x", "core"))
    ep = ("x", "core")
    return jax.shard_map(
        shards,
        mesh=mesh,
        in_specs=(
            P("ctx", ep),
            P("ctx", ep),
            P("ctx", None),
            P("ctx", None),
            P(None, ep),
            P(None, ep),
            P(),
            P("ctx", ep),
            P("ctx", None),
            P("ctx", None),
            P("ctx", None, ep),
            P("ctx", None, ep),
            P("ctx", ep, None),
        ),
        out_specs=(P("ctx", ep), P("ctx", ep)),
        check_vma=False,
    )
```

```python
import math

import jax
import jax.numpy as jnp
from jax import lax
from jax.experimental import pallas as pl
from jax.experimental.pallas import tpu as pltpu
from jax.sharding import PartitionSpec as P

NOPE = 128
ROPE = 64
VDIM = 128
TOP = 8
CAP = 8
HALF = 64
GROUP = 4
MIB = 1 << 20
LIMIT = 52 * MIB
FULL = 60 * MIB
SMALL = 24 * MIB
CHUNK = 256

NT = (((1,), (1,)), ((), ()))
TN = (((0,), (0,)), ((), ()))
VMEM = pltpu.VMEM
SMEM_SPEC = pl.BlockSpec(memory_space=pltpu.SMEM)
VMEM_SPEC = pl.BlockSpec(memory_space=pltpu.VMEM)
HBM_SPEC = pl.BlockSpec(memory_space=pltpu.HBM)


def gather_order(ctx):
    bits = ctx.bit_length() - 1
    return [1 << (bits - 1)] + [1 << bit for bit in range(bits - 1)]


def route_kernel(
    ep_ref,
    ids_ref,
    weights_ref,
    rope_ref,
    rows_ref,
    latent_ref,
    sent_ref,
    high_ref,
    low_ref,
    packed_ref,
):
    latent_width = latent_ref.shape[1]
    rope = rope_ref[...].astype(jnp.float32).T
    for core in range(2):

        @pl.when(ep_ref[0] % 2 == core)
        def _():
            rows = slice(core * HALF, (core + 1) * HALF)
            packed_ref[:, :latent_width] = latent_ref[rows, :]
            packed_ref[:, latent_width:] = rope[rows].astype(jnp.bfloat16)

    row_count = ids_ref.shape[1]
    slots = sent_ref.shape[0] * CAP
    slot = lax.broadcasted_iota(jnp.int32, (slots, row_count), 0)
    expert = slot // CAP
    named = jnp.zeros((slots, row_count), jnp.float32)
    gate = jnp.zeros((slots, row_count), jnp.float32)
    for choice in range(TOP):
        match = ids_ref[choice : choice + 1, :] == expert
        named = jnp.where(match, 1.0, named)
        gate = jnp.where(match, weights_ref[choice : choice + 1, :], gate)
    row = lax.broadcasted_iota(jnp.int32, (row_count, row_count), 0)
    other = lax.broadcasted_iota(jnp.int32, (row_count, row_count), 1)
    before = jnp.where(row < other, 1.0, 0.0).astype(jnp.bfloat16)
    rank = jnp.dot(named.astype(jnp.bfloat16), before, preferred_element_type=jnp.float32)
    taken = (named > 0.0) & (rank == (slot % CAP).astype(jnp.float32))
    select = jnp.where(taken, 1.0, 0.0).astype(jnp.bfloat16)
    gate = jnp.where(taken, gate, 0.0)
    blocks = [gate[index * CAP : (index + 1) * CAP] for index in range(slots // CAP)]
    gate = jnp.concatenate([block for block in blocks for _ in range(2)], axis=0)
    high = gate.astype(jnp.bfloat16)
    high_ref[...] = high
    low_ref[...] = (gate - high.astype(jnp.float32)).astype(jnp.bfloat16)
    sent = jnp.dot(select, rows_ref[...], preferred_element_type=jnp.float32)
    for index in range(slots // CAP):
        sent_ref[index] = sent[index * CAP : (index + 1) * CAP].astype(jnp.bfloat16)


def route(ep, expert_ids, expert_weights, k_rope, moe_rows, latent, ctx):
    row_count, features = moe_rows.shape
    slots = ctx * CAP
    return pl.pallas_call(
        route_kernel,
        out_shape=[
            jax.ShapeDtypeStruct((ctx, CAP, features), jnp.bfloat16),
            jax.ShapeDtypeStruct((2 * slots, row_count), jnp.bfloat16),
            jax.ShapeDtypeStruct((2 * slots, row_count), jnp.bfloat16),
            jax.ShapeDtypeStruct((HALF, latent.shape[1] + ROPE), jnp.bfloat16),
        ],
        in_specs=[SMEM_SPEC] + [VMEM_SPEC] * 5,
        out_specs=[VMEM_SPEC] * 4,
        compiler_params=pltpu.CompilerParams(vmem_limit_bytes=FULL),
        cost_estimate=pl.CostEstimate(
            flops=2 * row_count * slots * features, bytes_accessed=1 * MIB, transcendentals=0
        ),
        name="route",
    )(ep, expert_ids.T, expert_weights.T, k_rope.T, moe_rows, latent)


def weight_copies(ep_ref, flips, gate_hbm, up_hbm, gate, up, semaphores):
    features = gate.shape[1]
    copies = []
    for index, flip in enumerate(flips):
        place = pl.multiple_of((ep_ref[0] ^ flip) * features, features)
        for which, (source, target) in enumerate(((gate_hbm, gate), (up_hbm, up))):
            copy = pltpu.make_async_copy(
                source.at[0, pl.ds(place, features)], target.at[index], semaphores.at[index, which]
            )
            copy.start()
            copies.append(copy)
    return copies


def near_kernel(
    ep_ref,
    own_ref,
    core_ref,
    gate_hbm,
    up_hbm,
    down_hbm,
    sums_out,
    far_gate,
    far_up,
    down,
    gate,
    up,
    semaphores,
    far_semaphores,
    down_semaphores,
):
    units = gate.shape[2]
    features = gate.shape[1]
    copies = weight_copies(ep_ref, (0, 1), gate_hbm, up_hbm, gate, up, semaphores)
    later = weight_copies(ep_ref, (2, 3), gate_hbm, up_hbm, far_gate, far_up, far_semaphores)
    for flip in (3, 1, 2, 0):
        place = pl.multiple_of((ep_ref[0] ^ flip) * features, features)
        copy = pltpu.make_async_copy(
            down_hbm.at[0, :, pl.ds(place, features)], down.at[flip], down_semaphores.at[flip]
        )
        copy.start()
        later.append(copy)
    gate_sum, up_sum = None, None
    for index, x_ref in enumerate((own_ref, core_ref)):
        rows = x_ref[...]
        copies[2 * index].wait()
        part = jnp.dot(rows, gate[index], preferred_element_type=jnp.float32)
        gate_sum = part if gate_sum is None else gate_sum + part
        copies[2 * index + 1].wait()
        part = jnp.dot(rows, up[index], preferred_element_type=jnp.float32)
        up_sum = part if up_sum is None else up_sum + part
    sums_out[:, :units] = gate_sum
    sums_out[:, units:] = up_sum
    for copy in later:
        copy.wait()


def near_experts(ep, own, core, w_gate, w_up, w_down):
    slots, features = own.shape
    units = w_gate.shape[2]
    return pl.pallas_call(
        near_kernel,
        out_shape=[
            jax.ShapeDtypeStruct((slots, 2 * units), jnp.float32),
            jax.ShapeDtypeStruct((2, features, units), jnp.bfloat16),
            jax.ShapeDtypeStruct((2, features, units), jnp.bfloat16),
            jax.ShapeDtypeStruct((4, units, features), jnp.bfloat16),
        ],
        in_specs=[SMEM_SPEC] + [VMEM_SPEC] * 2 + [HBM_SPEC] * 3,
        out_specs=[VMEM_SPEC] * 4,
        scratch_shapes=[
            VMEM((2, features, units), jnp.bfloat16),
            VMEM((2, features, units), jnp.bfloat16),
            pltpu.SemaphoreType.DMA((2, 2)),
            pltpu.SemaphoreType.DMA((2, 2)),
            pltpu.SemaphoreType.DMA((4,)),
        ],
        compiler_params=pltpu.CompilerParams(vmem_limit_bytes=46 * MIB),
        cost_estimate=pl.CostEstimate(
            flops=8 * slots * features * units,
            bytes_accessed=24 * features * units,
            transcendentals=0,
        ),
        name="near_experts",
    )(ep, own, core, w_gate, w_up, w_down)


def far_kernel(
    far_ref, core_far_ref, sums_ref, gate, up, down, own_out, core_out, far_out, core_far_out
):
    units = gate.shape[2]
    gate_sum, up_sum = sums_ref[:, :units], sums_ref[:, units:]
    for index, x_ref in enumerate((far_ref, core_far_ref)):
        rows = x_ref[...]
        gate_sum = gate_sum + jnp.dot(rows, gate[index], preferred_element_type=jnp.float32)
        up_sum = up_sum + jnp.dot(rows, up[index], preferred_element_type=jnp.float32)
    hidden = (gate_sum / (1.0 + jnp.exp(-gate_sum)) * up_sum).astype(jnp.bfloat16)
    outs = (own_out, core_out, far_out, core_far_out)
    for flip in (3, 1, 2, 0):
        outs[flip][...] = jnp.dot(
            hidden, down[flip], preferred_element_type=jnp.float32
        ).astype(jnp.bfloat16)


def far_experts(far, core_far, sums, gate, up, down):
    slots, features = far.shape
    units = gate.shape[2]
    return pl.pallas_call(
        far_kernel,
        out_shape=[jax.ShapeDtypeStruct((slots, features), jnp.bfloat16)] * 4,
        in_specs=[VMEM_SPEC] * 6,
        out_specs=[VMEM_SPEC] * 4,
        compiler_params=pltpu.CompilerParams(vmem_limit_bytes=24 * MIB),
        cost_estimate=pl.CostEstimate(flops=0, bytes_accessed=0, transcendentals=0),
        name="far_experts",
    )(far, core_far, sums, gate, up, down)


def sum_kernel(ep_ref, own_ref, from_core_ref, far_ref, from_core_far_ref, out_ref):
    my_x = ep_ref[0] // 2
    for flip, (mine, other) in enumerate(
        ((own_ref, from_core_ref), (far_ref, from_core_far_ref))
    ):
        total = mine[...].astype(jnp.float32) + other[...].astype(jnp.float32)
        for index in range(out_ref.shape[0]):
            block = total[index * CAP : (index + 1) * CAP].astype(jnp.bfloat16)
            out_ref[index, my_x ^ flip] = block


def sum_cores(ep, own, from_core, far, from_core_far, ctx):
    features = own.shape[1]
    return pl.pallas_call(
        sum_kernel,
        out_shape=jax.ShapeDtypeStruct((ctx, 2, CAP, features), jnp.bfloat16),
        in_specs=[SMEM_SPEC] + [VMEM_SPEC] * 4,
        out_specs=VMEM_SPEC,
        compiler_params=pltpu.CompilerParams(vmem_limit_bytes=16 * MIB),
        cost_estimate=pl.CostEstimate(flops=0, bytes_accessed=MIB, transcendentals=0),
        name="sum_cores",
    )(ep, own, from_core, far, from_core_far)


def combine_kernel(high_ref, low_ref, returned_ref, out_ref):
    returned = returned_ref[...]
    total = lax.dot_general(high_ref[...], returned, TN, preferred_element_type=jnp.float32)
    total = total + lax.dot_general(
        low_ref[...], returned, TN, preferred_element_type=jnp.float32
    )
    out_ref[...] = total.astype(jnp.bfloat16)


def combine(high, low, returned):
    slots, row_count = high.shape
    features = returned.shape[1]
    return pl.pallas_call(
        combine_kernel,
        out_shape=jax.ShapeDtypeStruct((row_count, features), jnp.bfloat16),
        in_specs=[VMEM_SPEC] * 3,
        out_specs=VMEM_SPEC,
        compiler_params=pltpu.CompilerParams(vmem_limit_bytes=LIMIT),
        cost_estimate=pl.CostEstimate(
            flops=4 * row_count * slots * features, bytes_accessed=MIB, transcendentals=0
        ),
        name="combine",
    )(high, low, returned)


def low_run(my_ctx, positions_ref):
    mine = my_ctx * (2 * HALF)
    return jnp.where(positions_ref[mine] < positions_ref[mine + HALF], 0, 1)


def fold_kernel(own_ref, positions_ref, q_nope_ref, q_rope_ref, w_uk_ref, out_ref):
    latent_width = w_uk_ref.shape[0]
    low = low_run(own_ref[0], positions_ref)
    for head in range(GROUP):
        columns = slice(head * NOPE, (head + 1) * NOPE)
        folded = lax.dot_general(
            q_nope_ref[:, columns], w_uk_ref[:, columns], NT, preferred_element_type=jnp.float32
        ).astype(jnp.bfloat16)
        rotated = q_rope_ref[:, head * ROPE : (head + 1) * ROPE]
        for run in range(2):
            rows = slice(run * HALF, (run + 1) * HALF)
            place = slice(head * HALF, (head + 1) * HALF)
            slot = 1 - (low ^ run)
            out_ref[0, slot, place, :latent_width] = folded[rows]
            out_ref[0, slot, place, latent_width:] = rotated[rows]


def fold(own, positions, q_nope, q_rope, w_uk):
    query_count, columns = q_nope.shape
    heads = columns // NOPE
    latent_width = w_uk.shape[0]
    width = latent_width + ROPE
    steps = heads // GROUP // 2
    queries = pl.pallas_call(
        fold_kernel,
        out_shape=jax.ShapeDtypeStruct((2, 2, heads // 2 * HALF, width), jnp.bfloat16),
        grid=(2 * steps,),
        in_specs=[
            SMEM_SPEC,
            SMEM_SPEC,
            pl.BlockSpec((query_count, GROUP * NOPE), lambda step: (0, step)),
            pl.BlockSpec((query_count, GROUP * ROPE), lambda step: (0, step)),
            pl.BlockSpec((latent_width, GROUP * NOPE), lambda step: (0, step)),
        ],
        out_specs=pl.BlockSpec(
            (1, 2, GROUP * HALF, width), lambda step: (step // steps, 0, step % steps, 0)
        ),
        compiler_params=pltpu.CompilerParams(vmem_limit_bytes=FULL),
        cost_estimate=pl.CostEstimate(
            flops=2 * query_count * columns * latent_width,
            bytes_accessed=6 * MIB,
            transcendentals=0,
        ),
        name="fold",
    )(own, positions, q_nope, q_rope, w_uk)
    return queries.reshape(2, heads * HALF, width)


def attention_kernel(
    own_ref,
    ep_ref,
    positions_ref,
    queries_hbm,
    w_uv_hbm,
    own_keys,
    core_keys,
    out_ref,
    keys,
    queries,
    w_uv,
    scores,
    tops,
    mixed,
    semaphores,
):
    query_copies = [
        pltpu.make_async_copy(queries_hbm.at[part], queries.at[part], semaphores.at[part])
        for part in range(2)
    ]
    w_uv_copy = pltpu.make_async_copy(w_uv_hbm, w_uv, semaphores.at[2])
    for copy in (query_copies[0], w_uv_copy, query_copies[1]):
        copy.start()
    blocks = own_keys.shape[0]
    my_ctx, my_ep = own_ref[0], ep_ref[0]
    for flip, source in enumerate((own_keys, core_keys)):
        for block in range(blocks):
            source_ctx = my_ctx
            for bit, step in enumerate(gather_order(blocks)):
                if block >> bit & 1:
                    source_ctx = source_ctx ^ step
            start = source_ctx * (2 * HALF) + ((my_ep % 2) ^ flip) * HALF
            place = pl.multiple_of(positions_ref[start], HALF)
            keys[pl.ds(place, HALF), :] = source[block]
    for part in range(2):
        query_copies[part].wait()
        attend_heads(
            own_ref,
            positions_ref,
            queries.at[part],
            w_uv,
            keys,
            out_ref,
            part * (w_uv.shape[1] // 2),
            scores,
            tops,
            mixed,
            w_uv_copy.wait if not part else lambda: None,
        )


def attend_heads(
    own_ref, positions_ref, queries, w_uv, keys, out_ref, skipped, scores, tops, mixed, wait
):
    latent_width = w_uv.shape[0]
    count = queries.shape[0] // 2
    heads = count // HALF
    mine = own_ref[0] * (2 * HALF)
    low = low_run(own_ref[0], positions_ref)
    high = 1 - low
    low_base = positions_ref[mine + low * HALF]
    high_base = positions_ref[mine + high * HALF]
    tops[...] = jnp.full(tops.shape, -jnp.inf, jnp.float32)
    offset = lax.broadcasted_iota(jnp.int32, (HALF, CHUNK), 1) - lax.broadcasted_iota(
        jnp.int32, (HALF, CHUNK), 0
    )
    low_chunks = (low_base + HALF + CHUNK - 1) // CHUNK
    high_chunks = (high_base + HALF + CHUNK - 1) // CHUNK

    def score(chunk, bases):
        start = pl.multiple_of(chunk * CHUNK, CHUNK)
        part = lax.dot_general(
            queries[: len(bases) * count, :],
            keys[pl.ds(start, CHUNK), :],
            NT,
            preferred_element_type=jnp.float32,
        )
        for index, base in enumerate(bases):
            visible = offset <= base - start
            for head in range(heads):
                rows = slice(index * count + head * HALF, index * count + (head + 1) * HALF)
                seen = jnp.where(visible, part[rows], -jnp.inf)
                scores[chunk, rows, :] = seen
                top = tops[rows, :]
                for lane in range(0, CHUNK, 128):
                    top = jnp.maximum(top, seen[:, lane : lane + 128])
                tops[rows, :] = top
        return 0

    lax.fori_loop(0, low_chunks, lambda c, _: score(c, (high_base, low_base)), 0)
    lax.fori_loop(low_chunks, high_chunks, lambda c, _: score(c, (high_base,)), 0)
    factor = math.log2(math.e) / math.sqrt(NOPE + ROPE)

    def mix(rows, chunks):
        top = jnp.max(tops[rows, :], axis=1, keepdims=True) * factor
        total = jnp.zeros((count, 128), jnp.float32)
        parts = []
        for chunk in range(chunks):
            part = jnp.exp2(scores[chunk, rows, :] * factor - top)
            for lane in range(0, CHUNK, 128):
                total = total + part[:, lane : lane + 128]
            parts.append(part.astype(jnp.bfloat16))
        summed = jnp.dot(
            jnp.concatenate(parts, axis=1),
            keys[: chunks * CHUNK, :latent_width],
            preferred_element_type=jnp.float32,
        )
        share = 1.0 / jnp.sum(total, axis=1, keepdims=True)
        mixed[rows, :] = (summed * share).astype(jnp.bfloat16)

    most = keys.shape[0] // CHUNK
    for chunks in range(1, most + 1):

        @pl.when(high_chunks == chunks)
        def _():
            mix(slice(0, count), chunks)

        @pl.when(low_chunks == chunks)
        def _():
            mix(slice(count, 2 * count), chunks)

    wait()
    high_rows = pl.ds(pl.multiple_of(high * HALF, HALF), HALF)
    low_rows = pl.ds(pl.multiple_of(low * HALF, HALF), HALF)
    for head in range(heads):
        both = jnp.concatenate(
            [
                mixed[head * HALF : (head + 1) * HALF, :],
                mixed[count + head * HALF : count + (head + 1) * HALF, :],
            ],
            axis=0,
        )
        columns = slice(skipped + head * VDIM, skipped + (head + 1) * VDIM)
        value = jnp.dot(
            both, w_uv[:, columns], preferred_element_type=jnp.float32
        ).astype(jnp.bfloat16)
        out_ref[high_rows, columns] = value[:HALF]
        out_ref[low_rows, columns] = value[HALF:]


def attend(own, ep, positions, queries, w_uv, own_keys, core_keys):
    latent_width, columns = w_uv.shape
    key_count = positions.shape[0]
    width = own_keys.shape[-1]
    rows = queries.shape[1]
    return pl.pallas_call(
        attention_kernel,
        out_shape=jax.ShapeDtypeStruct((2 * HALF, columns), jnp.bfloat16),
        in_specs=[SMEM_SPEC] * 3 + [HBM_SPEC] * 2 + [VMEM_SPEC] * 2,
        out_specs=VMEM_SPEC,
        scratch_shapes=[
            VMEM((key_count, width), jnp.bfloat16),
            VMEM(queries.shape, jnp.bfloat16),
            VMEM(w_uv.shape, jnp.bfloat16),
            VMEM((key_count // CHUNK, rows, CHUNK), jnp.float32),
            VMEM((rows, 128), jnp.float32),
            VMEM((rows, latent_width), jnp.bfloat16),
            pltpu.SemaphoreType.DMA((3,)),
        ],
        compiler_params=pltpu.CompilerParams(vmem_limit_bytes=52 * MIB),
        cost_estimate=pl.CostEstimate(
            flops=24 * rows * key_count * width,
            bytes_accessed=8 * MIB,
            transcendentals=rows * key_count,
        ),
        name="attention",
    )(own, ep, positions, queries, w_uv, own_keys, core_keys)


def shards(
    q_nope,
    q_rope,
    latent,
    k_rope,
    w_uk,
    w_uv,
    positions,
    moe_rows,
    expert_ids,
    expert_weights,
    w_gate,
    w_up,
    w_down,
):
    ctx = lax.axis_size("ctx")
    me = lax.axis_index("ctx").astype(jnp.int32).reshape(1)
    ep = lax.axis_index(("x", "core")).astype(jnp.int32).reshape(1)

    def over_ctx(value, flip):
        return lax.ppermute(value, "ctx", [(i, i ^ flip) for i in range(ctx)])

    def over(value, axis):
        return lax.ppermute(value, axis, [(0, 1), (1, 0)])

    outgoing, high, low, packed = route(
        ep, expert_ids, expert_weights, k_rope, moe_rows, latent, ctx
    )
    arrived = lax.all_to_all(outgoing, "ctx", split_axis=0, concat_axis=0, tiled=True)
    flips = gather_order(ctx)
    received = over_ctx(packed[None], flips[0])
    high, q_nope, received = lax.optimization_barrier((high, q_nope, received))
    queries = fold(me, positions, q_nope, q_rope, w_uk)
    own_keys = jnp.concatenate([packed[None], received], axis=0)
    for flip in flips[1:-1]:
        own_keys = jnp.concatenate([own_keys, over_ctx(own_keys, flip)], axis=0)
    arrived, queries, own_keys = lax.optimization_barrier((arrived, queries, own_keys))

    own = arrived.reshape(ctx * CAP, arrived.shape[2])
    far = over(own, "x")
    core = over(own, "core")
    received = over_ctx(own_keys, flips[-1])
    sums, far_gate, far_up, down = near_experts(ep, own, core, w_gate, w_up, w_down)
    far, sums = lax.optimization_barrier((far, sums))
    core_far = over(far, "core")
    own_out, core_out, far_out, core_far_out = far_experts(
        far, core_far, sums, far_gate, far_up, down
    )
    core_far_out, received = lax.optimization_barrier((core_far_out, received))
    from_core_far = over(core_far_out, "core")
    from_core = over(core_out, "core")
    own_keys = jnp.concatenate([own_keys, received], axis=0)
    own_keys, from_core_far = lax.optimization_barrier((own_keys, from_core_far))
    core_keys = over(own_keys, "core")
    returning = sum_cores(ep, own_out, from_core, far_out, from_core_far, ctx)
    returned = lax.all_to_all(
        returning.reshape(2 * ctx, CAP, returning.shape[3]),
        ("ctx", "x"),
        split_axis=0,
        concat_axis=0,
        tiled=True,
    )
    attention = attend(me, ep, positions, queries, w_uv, own_keys, core_keys)
    moe_out = combine(high, low, returned.reshape(2 * ctx * CAP, returned.shape[2]))
    return (attention, moe_out)


def solution(mesh):
    split = (mesh.shape["ctx"], mesh.shape["ep"] // 2, 2)
    mesh = jax.sharding.Mesh(mesh.devices.reshape(split), ("ctx", "x", "core"))
    ep = ("x", "core")
    return jax.shard_map(
        shards,
        mesh=mesh,
        in_specs=(
            P("ctx", ep),
            P("ctx", ep),
            P("ctx", None),
            P("ctx", None),
            P(None, ep),
            P(None, ep),
            P(),
            P("ctx", ep),
            P("ctx", None),
            P("ctx", None),
            P("ctx", None, ep),
            P("ctx", None, ep),
            P("ctx", ep, None),
        ),
        out_specs=(P("ctx", ep), P("ctx", ep)),
        check_vma=False,
    )
```

```python
import math

import jax
import jax.numpy as jnp
from jax import lax
from jax.experimental import pallas as pl
from jax.experimental.pallas import tpu as pltpu
from jax.sharding import PartitionSpec as P

NOPE = 128
ROPE = 64
VDIM = 128
TOP = 8
CAP = 8
HALF = 64
GROUP = 4
MIB = 1 << 20
LIMIT = 52 * MIB
FULL = 60 * MIB
SMALL = 24 * MIB
CHUNK = 256

NT = (((1,), (1,)), ((), ()))
TN = (((0,), (0,)), ((), ()))
VMEM = pltpu.VMEM
SMEM_SPEC = pl.BlockSpec(memory_space=pltpu.SMEM)
VMEM_SPEC = pl.BlockSpec(memory_space=pltpu.VMEM)
HBM_SPEC = pl.BlockSpec(memory_space=pltpu.HBM)


def gather_order(ctx):
    bits = ctx.bit_length() - 1
    return [1 << (bits - 1)] + [1 << bit for bit in range(bits - 1)]


def route_kernel(
    ep_ref,
    ids_ref,
    weights_ref,
    rope_ref,
    rows_ref,
    latent_ref,
    sent_ref,
    high_ref,
    low_ref,
    packed_ref,
):
    latent_width = latent_ref.shape[1]
    rope = rope_ref[...].astype(jnp.float32).T
    for core in range(2):

        @pl.when(ep_ref[0] % 2 == core)
        def _():
            rows = slice(core * HALF, (core + 1) * HALF)
            packed_ref[:, :latent_width] = latent_ref[rows, :]
            packed_ref[:, latent_width:] = rope[rows].astype(jnp.bfloat16)

    row_count = ids_ref.shape[1]
    slots = sent_ref.shape[0] * CAP
    slot = lax.broadcasted_iota(jnp.int32, (slots, row_count), 0)
    expert = slot // CAP
    named = jnp.zeros((slots, row_count), jnp.float32)
    gate = jnp.zeros((slots, row_count), jnp.float32)
    for choice in range(TOP):
        match = ids_ref[choice : choice + 1, :] == expert
        named = jnp.where(match, 1.0, named)
        gate = jnp.where(match, weights_ref[choice : choice + 1, :], gate)
    row = lax.broadcasted_iota(jnp.int32, (row_count, row_count), 0)
    other = lax.broadcasted_iota(jnp.int32, (row_count, row_count), 1)
    before = jnp.where(row < other, 1.0, 0.0).astype(jnp.bfloat16)
    rank = jnp.dot(named.astype(jnp.bfloat16), before, preferred_element_type=jnp.float32)
    taken = (named > 0.0) & (rank == (slot % CAP).astype(jnp.float32))
    select = jnp.where(taken, 1.0, 0.0).astype(jnp.bfloat16)
    gate = jnp.where(taken, gate, 0.0)
    blocks = [gate[index * CAP : (index + 1) * CAP] for index in range(slots // CAP)]
    gate = jnp.concatenate([block for block in blocks for _ in range(2)], axis=0)
    high = gate.astype(jnp.bfloat16)
    high_ref[...] = high
    low_ref[...] = (gate - high.astype(jnp.float32)).astype(jnp.bfloat16)
    sent = jnp.dot(select, rows_ref[...], preferred_element_type=jnp.float32)
    for index in range(slots // CAP):
        sent_ref[index] = sent[index * CAP : (index + 1) * CAP].astype(jnp.bfloat16)


def route(ep, expert_ids, expert_weights, k_rope, moe_rows, latent, ctx):
    row_count, features = moe_rows.shape
    slots = ctx * CAP
    return pl.pallas_call(
        route_kernel,
        out_shape=[
            jax.ShapeDtypeStruct((ctx, CAP, features), jnp.bfloat16),
            jax.ShapeDtypeStruct((2 * slots, row_count), jnp.bfloat16),
            jax.ShapeDtypeStruct((2 * slots, row_count), jnp.bfloat16),
            jax.ShapeDtypeStruct((HALF, latent.shape[1] + ROPE), jnp.bfloat16),
        ],
        in_specs=[SMEM_SPEC] + [VMEM_SPEC] * 5,
        out_specs=[VMEM_SPEC] * 4,
        compiler_params=pltpu.CompilerParams(vmem_limit_bytes=FULL),
        cost_estimate=pl.CostEstimate(
            flops=2 * row_count * slots * features, bytes_accessed=1 * MIB, transcendentals=0
        ),
        name="route",
    )(ep, expert_ids.T, expert_weights.T, k_rope.T, moe_rows, latent)


def weight_copies(ep_ref, flips, gate_hbm, up_hbm, gate, up, semaphores):
    features = gate.shape[1]
    copies = []
    for index, flip in enumerate(flips):
        place = pl.multiple_of((ep_ref[0] ^ flip) * features, features)
        for which, (source, target) in enumerate(((gate_hbm, gate), (up_hbm, up))):
            copy = pltpu.make_async_copy(
                source.at[0, pl.ds(place, features)], target.at[index], semaphores.at[index, which]
            )
            copy.start()
            copies.append(copy)
    return copies


def near_kernel(
    ep_ref,
    own_ref,
    core_ref,
    gate_hbm,
    up_hbm,
    down_hbm,
    sums_out,
    far_gate,
    far_up,
    down,
    gate,
    up,
    semaphores,
    far_semaphores,
    down_semaphores,
):
    units = gate.shape[2]
    features = gate.shape[1]
    copies = weight_copies(ep_ref, (0, 1), gate_hbm, up_hbm, gate, up, semaphores)
    later = weight_copies(ep_ref, (2, 3), gate_hbm, up_hbm, far_gate, far_up, far_semaphores)
    for flip in (3, 1, 2, 0):
        place = pl.multiple_of((ep_ref[0] ^ flip) * features, features)
        copy = pltpu.make_async_copy(
            down_hbm.at[0, :, pl.ds(place, features)], down.at[flip], down_semaphores.at[flip]
        )
        copy.start()
        later.append(copy)
    gate_sum, up_sum = None, None
    for index, x_ref in enumerate((own_ref, core_ref)):
        rows = x_ref[...]
        copies[2 * index].wait()
        part = jnp.dot(rows, gate[index], preferred_element_type=jnp.float32)
        gate_sum = part if gate_sum is None else gate_sum + part
        copies[2 * index + 1].wait()
        part = jnp.dot(rows, up[index], preferred_element_type=jnp.float32)
        up_sum = part if up_sum is None else up_sum + part
    sums_out[:, :units] = gate_sum
    sums_out[:, units:] = up_sum
    for copy in later:
        copy.wait()


def near_experts(ep, own, core, w_gate, w_up, w_down):
    slots, features = own.shape
    units = w_gate.shape[2]
    return pl.pallas_call(
        near_kernel,
        out_shape=[
            jax.ShapeDtypeStruct((slots, 2 * units), jnp.float32),
            jax.ShapeDtypeStruct((2, features, units), jnp.bfloat16),
            jax.ShapeDtypeStruct((2, features, units), jnp.bfloat16),
            jax.ShapeDtypeStruct((4, units, features), jnp.bfloat16),
        ],
        in_specs=[SMEM_SPEC] + [VMEM_SPEC] * 2 + [HBM_SPEC] * 3,
        out_specs=[VMEM_SPEC] * 4,
        scratch_shapes=[
            VMEM((2, features, units), jnp.bfloat16),
            VMEM((2, features, units), jnp.bfloat16),
            pltpu.SemaphoreType.DMA((2, 2)),
            pltpu.SemaphoreType.DMA((2, 2)),
            pltpu.SemaphoreType.DMA((4,)),
        ],
        compiler_params=pltpu.CompilerParams(vmem_limit_bytes=46 * MIB),
        cost_estimate=pl.CostEstimate(
            flops=8 * slots * features * units,
            bytes_accessed=24 * features * units,
            transcendentals=0,
        ),
        name="near_experts",
    )(ep, own, core, w_gate, w_up, w_down)


def far_kernel(
    far_ref, core_far_ref, sums_ref, gate, up, down, kept_out, sent_out
):
    units = gate.shape[2]
    gate_sum, up_sum = sums_ref[:, :units], sums_ref[:, units:]
    for index, x_ref in enumerate((far_ref, core_far_ref)):
        rows = x_ref[...]
        gate_sum = gate_sum + jnp.dot(rows, gate[index], preferred_element_type=jnp.float32)
        up_sum = up_sum + jnp.dot(rows, up[index], preferred_element_type=jnp.float32)
    hidden = (gate_sum / (1.0 + jnp.exp(-gate_sum)) * up_sum).astype(jnp.bfloat16)
    for flip in range(4):
        out = sent_out if flip % 2 else kept_out
        out[flip // 2] = jnp.dot(
            hidden, down[flip], preferred_element_type=jnp.float32
        ).astype(jnp.bfloat16)


def far_experts(far, core_far, sums, gate, up, down):
    slots, features = far.shape
    units = gate.shape[2]
    return pl.pallas_call(
        far_kernel,
        out_shape=[jax.ShapeDtypeStruct((2, slots, features), jnp.bfloat16)] * 2,
        in_specs=[VMEM_SPEC] * 6,
        out_specs=[VMEM_SPEC] * 2,
        compiler_params=pltpu.CompilerParams(vmem_limit_bytes=24 * MIB),
        cost_estimate=pl.CostEstimate(flops=0, bytes_accessed=0, transcendentals=0),
        name="far_experts",
    )(far, core_far, sums, gate, up, down)


def sum_kernel(ep_ref, kept_ref, received_ref, out_ref):
    my_x = ep_ref[0] // 2
    for flip in range(2):
        total = kept_ref[flip].astype(jnp.float32) + received_ref[flip].astype(jnp.float32)
        for index in range(out_ref.shape[0]):
            block = total[index * CAP : (index + 1) * CAP].astype(jnp.bfloat16)
            out_ref[index, my_x ^ flip] = block


def sum_cores(ep, kept, received, ctx):
    features = kept.shape[2]
    return pl.pallas_call(
        sum_kernel,
        out_shape=jax.ShapeDtypeStruct((ctx, 2, CAP, features), jnp.bfloat16),
        in_specs=[SMEM_SPEC] + [VMEM_SPEC] * 2,
        out_specs=VMEM_SPEC,
        compiler_params=pltpu.CompilerParams(vmem_limit_bytes=16 * MIB),
        cost_estimate=pl.CostEstimate(flops=0, bytes_accessed=MIB, transcendentals=0),
        name="sum_cores",
    )(ep, kept, received)


def combine_kernel(high_ref, low_ref, returned_ref, out_ref):
    returned = returned_ref[...]
    total = lax.dot_general(high_ref[...], returned, TN, preferred_element_type=jnp.float32)
    total = total + lax.dot_general(
        low_ref[...], returned, TN, preferred_element_type=jnp.float32
    )
    out_ref[...] = total.astype(jnp.bfloat16)


def combine(high, low, returned):
    slots, row_count = high.shape
    features = returned.shape[1]
    return pl.pallas_call(
        combine_kernel,
        out_shape=jax.ShapeDtypeStruct((row_count, features), jnp.bfloat16),
        in_specs=[VMEM_SPEC] * 3,
        out_specs=VMEM_SPEC,
        compiler_params=pltpu.CompilerParams(vmem_limit_bytes=LIMIT),
        cost_estimate=pl.CostEstimate(
            flops=4 * row_count * slots * features, bytes_accessed=MIB, transcendentals=0
        ),
        name="combine",
    )(high, low, returned)


def low_run(my_ctx, positions_ref):
    mine = my_ctx * (2 * HALF)
    return jnp.where(positions_ref[mine] < positions_ref[mine + HALF], 0, 1)


def fold_kernel(own_ref, positions_ref, q_nope_ref, q_rope_ref, w_uk_ref, out_ref):
    latent_width = w_uk_ref.shape[0]
    low = low_run(own_ref[0], positions_ref)
    for head in range(GROUP):
        columns = slice(head * NOPE, (head + 1) * NOPE)
        folded = lax.dot_general(
            q_nope_ref[:, columns], w_uk_ref[:, columns], NT, preferred_element_type=jnp.float32
        ).astype(jnp.bfloat16)
        rotated = q_rope_ref[:, head * ROPE : (head + 1) * ROPE]
        for run in range(2):
            rows = slice(run * HALF, (run + 1) * HALF)
            place = slice(head * HALF, (head + 1) * HALF)
            slot = 1 - (low ^ run)
            out_ref[0, slot, place, :latent_width] = folded[rows]
            out_ref[0, slot, place, latent_width:] = rotated[rows]


def fold(own, positions, q_nope, q_rope, w_uk):
    query_count, columns = q_nope.shape
    heads = columns // NOPE
    latent_width = w_uk.shape[0]
    width = latent_width + ROPE
    steps = heads // GROUP // 2
    queries = pl.pallas_call(
        fold_kernel,
        out_shape=jax.ShapeDtypeStruct((2, 2, heads // 2 * HALF, width), jnp.bfloat16),
        grid=(2 * steps,),
        in_specs=[
            SMEM_SPEC,
            SMEM_SPEC,
            pl.BlockSpec((query_count, GROUP * NOPE), lambda step: (0, step)),
            pl.BlockSpec((query_count, GROUP * ROPE), lambda step: (0, step)),
            pl.BlockSpec((latent_width, GROUP * NOPE), lambda step: (0, step)),
        ],
        out_specs=pl.BlockSpec(
            (1, 2, GROUP * HALF, width), lambda step: (step // steps, 0, step % steps, 0)
        ),
        compiler_params=pltpu.CompilerParams(vmem_limit_bytes=FULL),
        cost_estimate=pl.CostEstimate(
            flops=2 * query_count * columns * latent_width,
            bytes_accessed=6 * MIB,
            transcendentals=0,
        ),
        name="fold",
    )(own, positions, q_nope, q_rope, w_uk)
    return queries.reshape(2, heads * HALF, width)


def attention_kernel(
    own_ref,
    ep_ref,
    positions_ref,
    queries_hbm,
    w_uv_hbm,
    own_near,
    own_far,
    core_near,
    core_far,
    out_ref,
    keys,
    queries,
    w_uv,
    scores,
    tops,
    mixed,
    semaphores,
):
    query_copies = [
        pltpu.make_async_copy(queries_hbm.at[part], queries.at[part], semaphores.at[part])
        for part in range(2)
    ]
    w_uv_copy = pltpu.make_async_copy(w_uv_hbm, w_uv, semaphores.at[2])
    for copy in (query_copies[0], w_uv_copy, query_copies[1]):
        copy.start()
    blocks = own_near.shape[0]
    my_ctx, my_ep = own_ref[0], ep_ref[0]
    flips = gather_order(2 * blocks)
    sources = ((own_near, 0, 0), (own_far, 0, 1), (core_near, 1, 0), (core_far, 1, 1))
    for source, flip, last in sources:
        for block in range(blocks):
            source_ctx = my_ctx ^ flips[-1] if last else my_ctx
            for bit, step in enumerate(flips[:-1]):
                if block >> bit & 1:
                    source_ctx = source_ctx ^ step
            start = source_ctx * (2 * HALF) + ((my_ep % 2) ^ flip) * HALF
            place = pl.multiple_of(positions_ref[start], HALF)
            keys[pl.ds(place, HALF), :] = source[block]
    for part in range(2):
        query_copies[part].wait()
        attend_heads(
            own_ref,
            positions_ref,
            queries.at[part],
            w_uv,
            keys,
            out_ref,
            part * (w_uv.shape[1] // 2),
            scores,
            tops,
            mixed,
            w_uv_copy.wait if not part else lambda: None,
        )


def attend_heads(
    own_ref, positions_ref, queries, w_uv, keys, out_ref, skipped, scores, tops, mixed, wait
):
    latent_width = w_uv.shape[0]
    count = queries.shape[0] // 2
    heads = count // HALF
    mine = own_ref[0] * (2 * HALF)
    low = low_run(own_ref[0], positions_ref)
    high = 1 - low
    low_base = positions_ref[mine + low * HALF]
    high_base = positions_ref[mine + high * HALF]
    tops[...] = jnp.full(tops.shape, -jnp.inf, jnp.float32)
    offset = lax.broadcasted_iota(jnp.int32, (HALF, CHUNK), 1) - lax.broadcasted_iota(
        jnp.int32, (HALF, CHUNK), 0
    )
    low_chunks = (low_base + HALF + CHUNK - 1) // CHUNK
    high_chunks = (high_base + HALF + CHUNK - 1) // CHUNK

    def score(chunk, bases):
        start = pl.multiple_of(chunk * CHUNK, CHUNK)
        part = lax.dot_general(
            queries[: len(bases) * count, :],
            keys[pl.ds(start, CHUNK), :],
            NT,
            preferred_element_type=jnp.float32,
        )
        for index, base in enumerate(bases):
            visible = offset <= base - start
            for head in range(heads):
                rows = slice(index * count + head * HALF, index * count + (head + 1) * HALF)
                seen = jnp.where(visible, part[rows], -jnp.inf)
                scores[chunk, rows, :] = seen
                top = tops[rows, :]
                for lane in range(0, CHUNK, 128):
                    top = jnp.maximum(top, seen[:, lane : lane + 128])
                tops[rows, :] = top
        return 0

    lax.fori_loop(0, low_chunks, lambda c, _: score(c, (high_base, low_base)), 0)
    lax.fori_loop(low_chunks, high_chunks, lambda c, _: score(c, (high_base,)), 0)
    factor = math.log2(math.e) / math.sqrt(NOPE + ROPE)

    def mix(rows, chunks):
        top = jnp.max(tops[rows, :], axis=1, keepdims=True) * factor
        total = jnp.zeros((count, 128), jnp.float32)
        parts = []
        for chunk in range(chunks):
            part = jnp.exp2(scores[chunk, rows, :] * factor - top)
            for lane in range(0, CHUNK, 128):
                total = total + part[:, lane : lane + 128]
            parts.append(part.astype(jnp.bfloat16))
        summed = jnp.dot(
            jnp.concatenate(parts, axis=1),
            keys[: chunks * CHUNK, :latent_width],
            preferred_element_type=jnp.float32,
        )
        share = 1.0 / jnp.sum(total, axis=1, keepdims=True)
        mixed[rows, :] = (summed * share).astype(jnp.bfloat16)

    most = keys.shape[0] // CHUNK
    for chunks in range(1, most + 1):

        @pl.when(high_chunks == chunks)
        def _():
            mix(slice(0, count), chunks)

        @pl.when(low_chunks == chunks)
        def _():
            mix(slice(count, 2 * count), chunks)

    wait()
    high_rows = pl.ds(pl.multiple_of(high * HALF, HALF), HALF)
    low_rows = pl.ds(pl.multiple_of(low * HALF, HALF), HALF)
    for head in range(heads):
        both = jnp.concatenate(
            [
                mixed[head * HALF : (head + 1) * HALF, :],
                mixed[count + head * HALF : count + (head + 1) * HALF, :],
            ],
            axis=0,
        )
        columns = slice(skipped + head * VDIM, skipped + (head + 1) * VDIM)
        value = jnp.dot(
            both, w_uv[:, columns], preferred_element_type=jnp.float32
        ).astype(jnp.bfloat16)
        out_ref[high_rows, columns] = value[:HALF]
        out_ref[low_rows, columns] = value[HALF:]


def attend(own, ep, positions, queries, w_uv, *pieces):
    latent_width, columns = w_uv.shape
    key_count = positions.shape[0]
    width = pieces[0].shape[-1]
    rows = queries.shape[1]
    return pl.pallas_call(
        attention_kernel,
        out_shape=jax.ShapeDtypeStruct((2 * HALF, columns), jnp.bfloat16),
        in_specs=[SMEM_SPEC] * 3 + [HBM_SPEC] * 2 + [VMEM_SPEC] * 4,
        out_specs=VMEM_SPEC,
        scratch_shapes=[
            VMEM((key_count, width), jnp.bfloat16),
            VMEM(queries.shape, jnp.bfloat16),
            VMEM(w_uv.shape, jnp.bfloat16),
            VMEM((key_count // CHUNK, rows, CHUNK), jnp.float32),
            VMEM((rows, 128), jnp.float32),
            VMEM((rows, latent_width), jnp.bfloat16),
            pltpu.SemaphoreType.DMA((3,)),
        ],
        compiler_params=pltpu.CompilerParams(vmem_limit_bytes=52 * MIB),
        cost_estimate=pl.CostEstimate(
            flops=24 * rows * key_count * width,
            bytes_accessed=8 * MIB,
            transcendentals=rows * key_count,
        ),
        name="attention",
    )(own, ep, positions, queries, w_uv, *pieces)


def shards(
    q_nope,
    q_rope,
    latent,
    k_rope,
    w_uk,
    w_uv,
    positions,
    moe_rows,
    expert_ids,
    expert_weights,
    w_gate,
    w_up,
    w_down,
):
    ctx = lax.axis_size("ctx")
    me = lax.axis_index("ctx").astype(jnp.int32).reshape(1)
    ep = lax.axis_index(("x", "core")).astype(jnp.int32).reshape(1)

    def over_ctx(value, flip):
        return lax.ppermute(value, "ctx", [(i, i ^ flip) for i in range(ctx)])

    def over(value, axis):
        return lax.ppermute(value, axis, [(0, 1), (1, 0)])

    outgoing, high, low, packed = route(
        ep, expert_ids, expert_weights, k_rope, moe_rows, latent, ctx
    )
    arrived = lax.all_to_all(outgoing, "ctx", split_axis=0, concat_axis=0, tiled=True)
    flips = gather_order(ctx)
    received = over_ctx(packed[None], flips[0])
    high, q_nope, received = lax.optimization_barrier((high, q_nope, received))
    queries = fold(me, positions, q_nope, q_rope, w_uk)
    own_keys = jnp.concatenate([packed[None], received], axis=0)
    for flip in flips[1:-1]:
        own_keys = jnp.concatenate([own_keys, over_ctx(own_keys, flip)], axis=0)
    arrived, queries, own_keys = lax.optimization_barrier((arrived, queries, own_keys))

    own = arrived.reshape(ctx * CAP, arrived.shape[2])
    far = over(own, "x")
    core = over(own, "core")
    far_keys = over_ctx(own_keys, flips[-1])
    sums, far_gate, far_up, down = near_experts(ep, own, core, w_gate, w_up, w_down)
    core_keys = over(own_keys, "core")
    far, sums, core_keys = lax.optimization_barrier((far, sums, core_keys))
    core_far = over(far, "core")
    kept, sent = far_experts(far, core_far, sums, far_gate, far_up, down)
    sent, far_keys = lax.optimization_barrier((sent, far_keys))
    received = over(sent, "core")
    far_keys, received = lax.optimization_barrier((far_keys, received))
    core_far_keys = over(far_keys, "core")
    returning = sum_cores(ep, kept, received, ctx)
    returned = lax.all_to_all(
        returning.reshape(2 * ctx, CAP, returning.shape[3]),
        ("ctx", "x"),
        split_axis=0,
        concat_axis=0,
        tiled=True,
    )
    attention = attend(
        me, ep, positions, queries, w_uv, own_keys, far_keys, core_keys, core_far_keys
    )
    moe_out = combine(high, low, returned.reshape(2 * ctx * CAP, returned.shape[2]))
    return (attention, moe_out)


def solution(mesh):
    split = (mesh.shape["ctx"], mesh.shape["ep"] // 2, 2)
    mesh = jax.sharding.Mesh(mesh.devices.reshape(split), ("ctx", "x", "core"))
    ep = ("x", "core")
    return jax.shard_map(
        shards,
        mesh=mesh,
        in_specs=(
            P("ctx", ep),
            P("ctx", ep),
            P("ctx", None),
            P("ctx", None),
            P(None, ep),
            P(None, ep),
            P(),
            P("ctx", ep),
            P("ctx", None),
            P("ctx", None),
            P("ctx", None, ep),
            P("ctx", None, ep),
            P("ctx", ep, None),
        ),
        out_specs=(P("ctx", ep), P("ctx", ep)),
        check_vma=False,
    )
```

```python
import math

import jax
import jax.numpy as jnp
from jax import lax
from jax.experimental import pallas as pl
from jax.experimental.pallas import tpu as pltpu
from jax.sharding import PartitionSpec as P

NOPE = 128
ROPE = 64
VDIM = 128
TOP = 8
CAP = 8
HALF = 64
GROUP = 4
MIB = 1 << 20
LIMIT = 52 * MIB
FULL = 60 * MIB
SMALL = 24 * MIB
CHUNK = 256

NT = (((1,), (1,)), ((), ()))
TN = (((0,), (0,)), ((), ()))
VMEM = pltpu.VMEM
SMEM_SPEC = pl.BlockSpec(memory_space=pltpu.SMEM)
VMEM_SPEC = pl.BlockSpec(memory_space=pltpu.VMEM)
HBM_SPEC = pl.BlockSpec(memory_space=pltpu.HBM)


def gather_order(ctx):
    bits = ctx.bit_length() - 1
    return [1 << (bits - 1)] + [1 << bit for bit in range(bits - 1)]


def route_kernel(
    ep_ref,
    ids_ref,
    weights_ref,
    rope_ref,
    rows_ref,
    latent_ref,
    sent_ref,
    high_ref,
    low_ref,
    packed_ref,
):
    latent_width = latent_ref.shape[1]
    rope = rope_ref[...].astype(jnp.float32).T
    for core in range(2):

        @pl.when(ep_ref[0] % 2 == core)
        def _():
            rows = slice(core * HALF, (core + 1) * HALF)
            packed_ref[:, :latent_width] = latent_ref[rows, :]
            packed_ref[:, latent_width:] = rope[rows].astype(jnp.bfloat16)

    row_count = ids_ref.shape[1]
    slots = sent_ref.shape[0] * CAP
    slot = lax.broadcasted_iota(jnp.int32, (slots, row_count), 0)
    expert = slot // CAP
    named = jnp.zeros((slots, row_count), jnp.float32)
    gate = jnp.zeros((slots, row_count), jnp.float32)
    for choice in range(TOP):
        match = ids_ref[choice : choice + 1, :] == expert
        named = jnp.where(match, 1.0, named)
        gate = jnp.where(match, weights_ref[choice : choice + 1, :], gate)
    row = lax.broadcasted_iota(jnp.int32, (row_count, row_count), 0)
    other = lax.broadcasted_iota(jnp.int32, (row_count, row_count), 1)
    before = jnp.where(row < other, 1.0, 0.0).astype(jnp.bfloat16)
    rank = jnp.dot(named.astype(jnp.bfloat16), before, preferred_element_type=jnp.float32)
    taken = (named > 0.0) & (rank == (slot % CAP).astype(jnp.float32))
    select = jnp.where(taken, 1.0, 0.0).astype(jnp.bfloat16)
    gate = jnp.where(taken, gate, 0.0)
    blocks = [gate[index * CAP : (index + 1) * CAP] for index in range(slots // CAP)]
    gate = jnp.concatenate([block for block in blocks for _ in range(2)], axis=0)
    high = gate.astype(jnp.bfloat16)
    high_ref[...] = high
    low_ref[...] = (gate - high.astype(jnp.float32)).astype(jnp.bfloat16)
    sent = jnp.dot(select, rows_ref[...], preferred_element_type=jnp.float32)
    for index in range(slots // CAP):
        sent_ref[index] = sent[index * CAP : (index + 1) * CAP].astype(jnp.bfloat16)


def route(ep, expert_ids, expert_weights, k_rope, moe_rows, latent, ctx):
    row_count, features = moe_rows.shape
    slots = ctx * CAP
    return pl.pallas_call(
        route_kernel,
        out_shape=[
            jax.ShapeDtypeStruct((ctx, CAP, features), jnp.bfloat16),
            jax.ShapeDtypeStruct((2 * slots, row_count), jnp.bfloat16),
            jax.ShapeDtypeStruct((2 * slots, row_count), jnp.bfloat16),
            jax.ShapeDtypeStruct((HALF, latent.shape[1] + ROPE), jnp.bfloat16),
        ],
        in_specs=[SMEM_SPEC] + [VMEM_SPEC] * 5,
        out_specs=[VMEM_SPEC] * 4,
        compiler_params=pltpu.CompilerParams(vmem_limit_bytes=FULL),
        cost_estimate=pl.CostEstimate(
            flops=2 * row_count * slots * features, bytes_accessed=1 * MIB, transcendentals=0
        ),
        name="route",
    )(ep, expert_ids.T, expert_weights.T, k_rope.T, moe_rows, latent)


def weight_copies(ep_ref, flips, gate_hbm, up_hbm, gate, up, semaphores):
    features = gate.shape[1]
    copies = []
    for index, flip in enumerate(flips):
        place = pl.multiple_of((ep_ref[0] ^ flip) * features, features)
        for which, (source, target) in enumerate(((gate_hbm, gate), (up_hbm, up))):
            copy = pltpu.make_async_copy(
                source.at[0, pl.ds(place, features)], target.at[index], semaphores.at[index, which]
            )
            copy.start()
            copies.append(copy)
    return copies


def near_kernel(
    ep_ref,
    own_ref,
    core_ref,
    gate_hbm,
    up_hbm,
    down_hbm,
    sums_out,
    far_gate,
    far_up,
    down,
    gate,
    up,
    semaphores,
    far_semaphores,
    down_semaphores,
):
    units = gate.shape[2]
    features = gate.shape[1]
    copies = weight_copies(ep_ref, (0, 1), gate_hbm, up_hbm, gate, up, semaphores)
    later = weight_copies(ep_ref, (2, 3), gate_hbm, up_hbm, far_gate, far_up, far_semaphores)
    for flip in (3, 1, 2, 0):
        place = pl.multiple_of((ep_ref[0] ^ flip) * features, features)
        copy = pltpu.make_async_copy(
            down_hbm.at[0, :, pl.ds(place, features)], down.at[flip], down_semaphores.at[flip]
        )
        copy.start()
        later.append(copy)
    gate_sum, up_sum = None, None
    for index, x_ref in enumerate((own_ref, core_ref)):
        rows = x_ref[...]
        copies[2 * index].wait()
        part = jnp.dot(rows, gate[index], preferred_element_type=jnp.float32)
        gate_sum = part if gate_sum is None else gate_sum + part
        copies[2 * index + 1].wait()
        part = jnp.dot(rows, up[index], preferred_element_type=jnp.float32)
        up_sum = part if up_sum is None else up_sum + part
    sums_out[:, :units] = gate_sum
    sums_out[:, units:] = up_sum
    for copy in later:
        copy.wait()


def near_experts(ep, own, core, w_gate, w_up, w_down):
    slots, features = own.shape
    units = w_gate.shape[2]
    return pl.pallas_call(
        near_kernel,
        out_shape=[
            jax.ShapeDtypeStruct((slots, 2 * units), jnp.float32),
            jax.ShapeDtypeStruct((2, features, units), jnp.bfloat16),
            jax.ShapeDtypeStruct((2, features, units), jnp.bfloat16),
            jax.ShapeDtypeStruct((4, units, features), jnp.bfloat16),
        ],
        in_specs=[SMEM_SPEC] + [VMEM_SPEC] * 2 + [HBM_SPEC] * 3,
        out_specs=[VMEM_SPEC] * 4,
        scratch_shapes=[
            VMEM((2, features, units), jnp.bfloat16),
            VMEM((2, features, units), jnp.bfloat16),
            pltpu.SemaphoreType.DMA((2, 2)),
            pltpu.SemaphoreType.DMA((2, 2)),
            pltpu.SemaphoreType.DMA((4,)),
        ],
        compiler_params=pltpu.CompilerParams(vmem_limit_bytes=46 * MIB),
        cost_estimate=pl.CostEstimate(
            flops=8 * slots * features * units,
            bytes_accessed=24 * features * units,
            transcendentals=0,
        ),
        name="near_experts",
    )(ep, own, core, w_gate, w_up, w_down)


def far_kernel(far_ref, sums_ref, gate, up, sums_out):
    units = gate.shape[2]
    rows = far_ref[...]
    for place, weights in ((slice(0, units), gate), (slice(units, 2 * units), up)):
        sums_out[:, place] = sums_ref[:, place] + jnp.dot(
            rows, weights[0], preferred_element_type=jnp.float32
        )


def sent_kernel(core_far_ref, sums_ref, gate, up, down, hidden_out, sent_out):
    units = gate.shape[2]
    rows = core_far_ref[...]
    gate_sum = sums_ref[:, :units] + jnp.dot(
        rows, gate[1], preferred_element_type=jnp.float32
    )
    up_sum = sums_ref[:, units:] + jnp.dot(rows, up[1], preferred_element_type=jnp.float32)
    hidden = (gate_sum / (1.0 + jnp.exp(-gate_sum)) * up_sum).astype(jnp.bfloat16)
    hidden_out[...] = hidden
    for index in range(2):
        sent_out[index] = jnp.dot(
            hidden, down[2 * index + 1], preferred_element_type=jnp.float32
        ).astype(jnp.bfloat16)


def kept_kernel(hidden_ref, down, kept_out):
    for index in range(2):
        kept_out[index] = jnp.dot(
            hidden_ref[...], down[2 * index], preferred_element_type=jnp.float32
        ).astype(jnp.bfloat16)


def expert_step(kernel, name, out_shape, *operands):
    return pl.pallas_call(
        kernel,
        out_shape=out_shape,
        in_specs=[VMEM_SPEC] * len(operands),
        out_specs=jax.tree.map(lambda _: VMEM_SPEC, out_shape),
        compiler_params=pltpu.CompilerParams(vmem_limit_bytes=SMALL),
        cost_estimate=pl.CostEstimate(
            flops=1 << 28, bytes_accessed=2 * MIB, transcendentals=1 << 14
        ),
        name=name,
    )(*operands)


def sum_kernel(ep_ref, kept_ref, received_ref, out_ref):
    my_x = ep_ref[0] // 2
    for flip in range(2):
        total = kept_ref[flip].astype(jnp.float32) + received_ref[flip].astype(jnp.float32)
        for index in range(out_ref.shape[0]):
            block = total[index * CAP : (index + 1) * CAP].astype(jnp.bfloat16)
            out_ref[index, my_x ^ flip] = block


def sum_cores(ep, kept, received, ctx):
    features = kept.shape[2]
    return pl.pallas_call(
        sum_kernel,
        out_shape=jax.ShapeDtypeStruct((ctx, 2, CAP, features), jnp.bfloat16),
        in_specs=[SMEM_SPEC] + [VMEM_SPEC] * 2,
        out_specs=VMEM_SPEC,
        compiler_params=pltpu.CompilerParams(vmem_limit_bytes=16 * MIB),
        cost_estimate=pl.CostEstimate(flops=0, bytes_accessed=MIB, transcendentals=0),
        name="sum_cores",
    )(ep, kept, received)


def combine_kernel(high_ref, low_ref, returned_ref, out_ref):
    returned = returned_ref[...]
    total = lax.dot_general(high_ref[...], returned, TN, preferred_element_type=jnp.float32)
    total = total + lax.dot_general(
        low_ref[...], returned, TN, preferred_element_type=jnp.float32
    )
    out_ref[...] = total.astype(jnp.bfloat16)


def combine(high, low, returned):
    slots, row_count = high.shape
    features = returned.shape[1]
    return pl.pallas_call(
        combine_kernel,
        out_shape=jax.ShapeDtypeStruct((row_count, features), jnp.bfloat16),
        in_specs=[VMEM_SPEC] * 3,
        out_specs=VMEM_SPEC,
        compiler_params=pltpu.CompilerParams(vmem_limit_bytes=LIMIT),
        cost_estimate=pl.CostEstimate(
            flops=4 * row_count * slots * features, bytes_accessed=MIB, transcendentals=0
        ),
        name="combine",
    )(high, low, returned)


def low_run(my_ctx, positions_ref):
    mine = my_ctx * (2 * HALF)
    return jnp.where(positions_ref[mine] < positions_ref[mine + HALF], 0, 1)


def fold_kernel(own_ref, positions_ref, q_nope_ref, q_rope_ref, w_uk_ref, out_ref):
    latent_width = w_uk_ref.shape[0]
    low = low_run(own_ref[0], positions_ref)
    for head in range(GROUP):
        columns = slice(head * NOPE, (head + 1) * NOPE)
        folded = lax.dot_general(
            q_nope_ref[:, columns], w_uk_ref[:, columns], NT, preferred_element_type=jnp.float32
        ).astype(jnp.bfloat16)
        rotated = q_rope_ref[:, head * ROPE : (head + 1) * ROPE]
        for run in range(2):
            rows = slice(run * HALF, (run + 1) * HALF)
            place = slice(head * HALF, (head + 1) * HALF)
            slot = 1 - (low ^ run)
            out_ref[0, slot, place, :latent_width] = folded[rows]
            out_ref[0, slot, place, latent_width:] = rotated[rows]


def fold(own, positions, q_nope, q_rope, w_uk):
    query_count, columns = q_nope.shape
    heads = columns // NOPE
    latent_width = w_uk.shape[0]
    width = latent_width + ROPE
    steps = heads // GROUP // 2
    queries = pl.pallas_call(
        fold_kernel,
        out_shape=jax.ShapeDtypeStruct((2, 2, heads // 2 * HALF, width), jnp.bfloat16),
        grid=(2 * steps,),
        in_specs=[
            SMEM_SPEC,
            SMEM_SPEC,
            pl.BlockSpec((query_count, GROUP * NOPE), lambda step: (0, step)),
            pl.BlockSpec((query_count, GROUP * ROPE), lambda step: (0, step)),
            pl.BlockSpec((latent_width, GROUP * NOPE), lambda step: (0, step)),
        ],
        out_specs=pl.BlockSpec(
            (1, 2, GROUP * HALF, width), lambda step: (step // steps, 0, step % steps, 0)
        ),
        compiler_params=pltpu.CompilerParams(vmem_limit_bytes=FULL),
        cost_estimate=pl.CostEstimate(
            flops=2 * query_count * columns * latent_width,
            bytes_accessed=6 * MIB,
            transcendentals=0,
        ),
        name="fold",
    )(own, positions, q_nope, q_rope, w_uk)
    return queries.reshape(2, heads * HALF, width)


def attention_kernel(
    own_ref,
    ep_ref,
    positions_ref,
    queries_hbm,
    w_uv_hbm,
    own_near,
    own_far,
    core_near,
    core_far,
    out_ref,
    keys,
    queries,
    w_uv,
    scores,
    tops,
    mixed,
    semaphores,
):
    query_copies = [
        pltpu.make_async_copy(queries_hbm.at[part], queries.at[part], semaphores.at[part])
        for part in range(2)
    ]
    w_uv_copy = pltpu.make_async_copy(w_uv_hbm, w_uv, semaphores.at[2])
    for copy in (query_copies[0], w_uv_copy, query_copies[1]):
        copy.start()
    blocks = own_near.shape[0]
    my_ctx, my_ep = own_ref[0], ep_ref[0]
    flips = gather_order(2 * blocks)
    sources = ((own_near, 0, 0), (own_far, 0, 1), (core_near, 1, 0), (core_far, 1, 1))
    for source, flip, last in sources:
        for block in range(blocks):
            source_ctx = my_ctx ^ flips[-1] if last else my_ctx
            for bit, step in enumerate(flips[:-1]):
                if block >> bit & 1:
                    source_ctx = source_ctx ^ step
            start = source_ctx * (2 * HALF) + ((my_ep % 2) ^ flip) * HALF
            place = pl.multiple_of(positions_ref[start], HALF)
            keys[pl.ds(place, HALF), :] = source[block]
    for part in range(2):
        query_copies[part].wait()
        attend_heads(
            own_ref,
            positions_ref,
            queries.at[part],
            w_uv,
            keys,
            out_ref,
            part * (w_uv.shape[1] // 2),
            scores,
            tops,
            mixed,
            w_uv_copy.wait if not part else lambda: None,
        )


def attend_heads(
    own_ref, positions_ref, queries, w_uv, keys, out_ref, skipped, scores, tops, mixed, wait
):
    latent_width = w_uv.shape[0]
    count = queries.shape[0] // 2
    heads = count // HALF
    mine = own_ref[0] * (2 * HALF)
    low = low_run(own_ref[0], positions_ref)
    high = 1 - low
    low_base = positions_ref[mine + low * HALF]
    high_base = positions_ref[mine + high * HALF]
    tops[...] = jnp.full(tops.shape, -jnp.inf, jnp.float32)
    offset = lax.broadcasted_iota(jnp.int32, (HALF, CHUNK), 1) - lax.broadcasted_iota(
        jnp.int32, (HALF, CHUNK), 0
    )
    low_chunks = (low_base + HALF + CHUNK - 1) // CHUNK
    high_chunks = (high_base + HALF + CHUNK - 1) // CHUNK

    def score(chunk, bases):
        start = pl.multiple_of(chunk * CHUNK, CHUNK)
        part = lax.dot_general(
            queries[: len(bases) * count, :],
            keys[pl.ds(start, CHUNK), :],
            NT,
            preferred_element_type=jnp.float32,
        )
        for index, base in enumerate(bases):
            visible = offset <= base - start
            for head in range(heads):
                rows = slice(index * count + head * HALF, index * count + (head + 1) * HALF)
                seen = jnp.where(visible, part[rows], -jnp.inf)
                scores[chunk, rows, :] = seen
                top = tops[rows, :]
                for lane in range(0, CHUNK, 128):
                    top = jnp.maximum(top, seen[:, lane : lane + 128])
                tops[rows, :] = top
        return 0

    lax.fori_loop(0, low_chunks, lambda c, _: score(c, (high_base, low_base)), 0)
    lax.fori_loop(low_chunks, high_chunks, lambda c, _: score(c, (high_base,)), 0)
    factor = math.log2(math.e) / math.sqrt(NOPE + ROPE)

    def mix(rows, chunks):
        top = jnp.max(tops[rows, :], axis=1, keepdims=True) * factor
        total = jnp.zeros((count, 128), jnp.float32)
        parts = []
        for chunk in range(chunks):
            part = jnp.exp2(scores[chunk, rows, :] * factor - top)
            for lane in range(0, CHUNK, 128):
                total = total + part[:, lane : lane + 128]
            parts.append(part.astype(jnp.bfloat16))
        summed = jnp.dot(
            jnp.concatenate(parts, axis=1),
            keys[: chunks * CHUNK, :latent_width],
            preferred_element_type=jnp.float32,
        )
        share = 1.0 / jnp.sum(total, axis=1, keepdims=True)
        mixed[rows, :] = (summed * share).astype(jnp.bfloat16)

    most = keys.shape[0] // CHUNK
    for chunks in range(1, most + 1):

        @pl.when(high_chunks == chunks)
        def _():
            mix(slice(0, count), chunks)

        @pl.when(low_chunks == chunks)
        def _():
            mix(slice(count, 2 * count), chunks)

    wait()
    high_rows = pl.ds(pl.multiple_of(high * HALF, HALF), HALF)
    low_rows = pl.ds(pl.multiple_of(low * HALF, HALF), HALF)
    for head in range(heads):
        both = jnp.concatenate(
            [
                mixed[head * HALF : (head + 1) * HALF, :],
                mixed[count + head * HALF : count + (head + 1) * HALF, :],
            ],
            axis=0,
        )
        columns = slice(skipped + head * VDIM, skipped + (head + 1) * VDIM)
        value = jnp.dot(
            both, w_uv[:, columns], preferred_element_type=jnp.float32
        ).astype(jnp.bfloat16)
        out_ref[high_rows, columns] = value[:HALF]
        out_ref[low_rows, columns] = value[HALF:]


def attend(own, ep, positions, queries, w_uv, *pieces):
    latent_width, columns = w_uv.shape
    key_count = positions.shape[0]
    width = pieces[0].shape[-1]
    rows = queries.shape[1]
    return pl.pallas_call(
        attention_kernel,
        out_shape=jax.ShapeDtypeStruct((2 * HALF, columns), jnp.bfloat16),
        in_specs=[SMEM_SPEC] * 3 + [HBM_SPEC] * 2 + [VMEM_SPEC] * 4,
        out_specs=VMEM_SPEC,
        scratch_shapes=[
            VMEM((key_count, width), jnp.bfloat16),
            VMEM(queries.shape, jnp.bfloat16),
            VMEM(w_uv.shape, jnp.bfloat16),
            VMEM((key_count // CHUNK, rows, CHUNK), jnp.float32),
            VMEM((rows, 128), jnp.float32),
            VMEM((rows, latent_width), jnp.bfloat16),
            pltpu.SemaphoreType.DMA((3,)),
        ],
        compiler_params=pltpu.CompilerParams(vmem_limit_bytes=52 * MIB),
        cost_estimate=pl.CostEstimate(
            flops=24 * rows * key_count * width,
            bytes_accessed=8 * MIB,
            transcendentals=rows * key_count,
        ),
        name="attention",
    )(own, ep, positions, queries, w_uv, *pieces)


def shards(
    q_nope,
    q_rope,
    latent,
    k_rope,
    w_uk,
    w_uv,
    positions,
    moe_rows,
    expert_ids,
    expert_weights,
    w_gate,
    w_up,
    w_down,
):
    ctx = lax.axis_size("ctx")
    me = lax.axis_index("ctx").astype(jnp.int32).reshape(1)
    ep = lax.axis_index(("x", "core")).astype(jnp.int32).reshape(1)

    def over_ctx(value, flip):
        return lax.ppermute(value, "ctx", [(i, i ^ flip) for i in range(ctx)])

    def over(value, axis):
        return lax.ppermute(value, axis, [(0, 1), (1, 0)])

    outgoing, high, low, packed = route(
        ep, expert_ids, expert_weights, k_rope, moe_rows, latent, ctx
    )
    arrived = lax.all_to_all(outgoing, "ctx", split_axis=0, concat_axis=0, tiled=True)
    flips = gather_order(ctx)
    received = over_ctx(packed[None], flips[0])
    high, q_nope, received = lax.optimization_barrier((high, q_nope, received))
    queries = fold(me, positions, q_nope, q_rope, w_uk)
    own_keys = jnp.concatenate([packed[None], received], axis=0)
    for flip in flips[1:-1]:
        own_keys = jnp.concatenate([own_keys, over_ctx(own_keys, flip)], axis=0)
    arrived, queries, own_keys = lax.optimization_barrier((arrived, queries, own_keys))

    own = arrived.reshape(ctx * CAP, arrived.shape[2])
    far = over(own, "x")
    core = over(own, "core")
    far_keys = over_ctx(own_keys, flips[-1])
    sums, far_gate, far_up, down = near_experts(ep, own, core, w_gate, w_up, w_down)
    far, sums = lax.optimization_barrier((far, sums))
    core_far = over(far, "core")
    slots, features = own.shape
    pieces = jax.ShapeDtypeStruct((2, slots, features), jnp.bfloat16)
    sums = expert_step(
        far_kernel,
        "far_rows",
        jax.ShapeDtypeStruct(sums.shape, jnp.float32),
        far,
        sums,
        far_gate,
        far_up,
    )
    hidden, sent = expert_step(
        sent_kernel,
        "sent_pieces",
        (jax.ShapeDtypeStruct((slots, down.shape[1]), jnp.bfloat16), pieces),
        core_far,
        sums,
        far_gate,
        far_up,
        down,
    )
    sent, far_keys = lax.optimization_barrier((sent, far_keys))
    received = over(sent, "core")
    kept = expert_step(kept_kernel, "kept_pieces", pieces, hidden, down)
    own_keys, far_keys, received = lax.optimization_barrier((own_keys, far_keys, received))
    core_keys = over(own_keys, "core")
    core_far_keys = over(far_keys, "core")
    returning = sum_cores(ep, kept, received, ctx)
    returned = lax.all_to_all(
        returning.reshape(2 * ctx, CAP, returning.shape[3]),
        ("ctx", "x"),
        split_axis=0,
        concat_axis=0,
        tiled=True,
    )
    attention = attend(
        me, ep, positions, queries, w_uv, own_keys, far_keys, core_keys, core_far_keys
    )
    moe_out = combine(high, low, returned.reshape(2 * ctx * CAP, returned.shape[2]))
    return (attention, moe_out)


def solution(mesh):
    split = (mesh.shape["ctx"], mesh.shape["ep"] // 2, 2)
    mesh = jax.sharding.Mesh(mesh.devices.reshape(split), ("ctx", "x", "core"))
    ep = ("x", "core")
    return jax.shard_map(
        shards,
        mesh=mesh,
        in_specs=(
            P("ctx", ep),
            P("ctx", ep),
            P("ctx", None),
            P("ctx", None),
            P(None, ep),
            P(None, ep),
            P(),
            P("ctx", ep),
            P("ctx", None),
            P("ctx", None),
            P("ctx", None, ep),
            P("ctx", None, ep),
            P("ctx", ep, None),
        ),
        out_specs=(P("ctx", ep), P("ctx", ep)),
        check_vma=False,
    )
```

```python
import math

import jax
import jax.numpy as jnp
from jax import lax
from jax.experimental import pallas as pl
from jax.experimental.pallas import tpu as pltpu
from jax.sharding import PartitionSpec as P

NOPE = 128
ROPE = 64
VDIM = 128
TOP = 8
CAP = 8
HALF = 64
GROUP = 4
MIB = 1 << 20
LIMIT = 52 * MIB
FULL = 60 * MIB
SMALL = 24 * MIB
CHUNK = 256

NT = (((1,), (1,)), ((), ()))
TN = (((0,), (0,)), ((), ()))
VMEM = pltpu.VMEM
SMEM_SPEC = pl.BlockSpec(memory_space=pltpu.SMEM)
VMEM_SPEC = pl.BlockSpec(memory_space=pltpu.VMEM)
HBM_SPEC = pl.BlockSpec(memory_space=pltpu.HBM)


def gather_order(ctx):
    bits = ctx.bit_length() - 1
    return [1 << (bits - 1)] + [1 << bit for bit in range(bits - 1)]


def route_kernel(
    ep_ref,
    ids_ref,
    weights_ref,
    rope_ref,
    rows_ref,
    latent_ref,
    sent_ref,
    high_ref,
    low_ref,
    packed_ref,
):
    latent_width = latent_ref.shape[1]
    rope = rope_ref[...].astype(jnp.float32).T
    for core in range(2):

        @pl.when(ep_ref[0] % 2 == core)
        def _():
            rows = slice(core * HALF, (core + 1) * HALF)
            packed_ref[:, :latent_width] = latent_ref[rows, :]
            packed_ref[:, latent_width:] = rope[rows].astype(jnp.bfloat16)

    row_count = ids_ref.shape[1]
    slots = sent_ref.shape[0] * CAP
    slot = lax.broadcasted_iota(jnp.int32, (slots, row_count), 0)
    expert = slot // CAP
    named = jnp.zeros((slots, row_count), jnp.float32)
    gate = jnp.zeros((slots, row_count), jnp.float32)
    for choice in range(TOP):
        match = ids_ref[choice : choice + 1, :] == expert
        named = jnp.where(match, 1.0, named)
        gate = jnp.where(match, weights_ref[choice : choice + 1, :], gate)
    row = lax.broadcasted_iota(jnp.int32, (row_count, row_count), 0)
    other = lax.broadcasted_iota(jnp.int32, (row_count, row_count), 1)
    before = jnp.where(row < other, 1.0, 0.0).astype(jnp.bfloat16)
    rank = jnp.dot(named.astype(jnp.bfloat16), before, preferred_element_type=jnp.float32)
    taken = (named > 0.0) & (rank == (slot % CAP).astype(jnp.float32))
    select = jnp.where(taken, 1.0, 0.0).astype(jnp.bfloat16)
    gate = jnp.where(taken, gate, 0.0)
    blocks = [gate[index * CAP : (index + 1) * CAP] for index in range(slots // CAP)]
    gate = jnp.concatenate([block for block in blocks for _ in range(2)], axis=0)
    high = gate.astype(jnp.bfloat16)
    high_ref[...] = high
    low_ref[...] = (gate - high.astype(jnp.float32)).astype(jnp.bfloat16)
    sent = jnp.dot(select, rows_ref[...], preferred_element_type=jnp.float32)
    for index in range(slots // CAP):
        sent_ref[index] = sent[index * CAP : (index + 1) * CAP].astype(jnp.bfloat16)


def route(ep, expert_ids, expert_weights, k_rope, moe_rows, latent, ctx):
    row_count, features = moe_rows.shape
    slots = ctx * CAP
    return pl.pallas_call(
        route_kernel,
        out_shape=[
            jax.ShapeDtypeStruct((ctx, CAP, features), jnp.bfloat16),
            jax.ShapeDtypeStruct((2 * slots, row_count), jnp.bfloat16),
            jax.ShapeDtypeStruct((2 * slots, row_count), jnp.bfloat16),
            jax.ShapeDtypeStruct((HALF, latent.shape[1] + ROPE), jnp.bfloat16),
        ],
        in_specs=[SMEM_SPEC] + [VMEM_SPEC] * 5,
        out_specs=[VMEM_SPEC] * 4,
        compiler_params=pltpu.CompilerParams(vmem_limit_bytes=FULL),
        cost_estimate=pl.CostEstimate(
            flops=2 * row_count * slots * features, bytes_accessed=1 * MIB, transcendentals=0
        ),
        name="route",
    )(ep, expert_ids.T, expert_weights.T, k_rope.T, moe_rows, latent)


def weight_copies(ep_ref, flips, gate_hbm, up_hbm, gate, up, semaphores):
    features = gate.shape[1]
    copies = []
    for index, flip in enumerate(flips):
        place = pl.multiple_of((ep_ref[0] ^ flip) * features, features)
        for which, (source, target) in enumerate(((gate_hbm, gate), (up_hbm, up))):
            copy = pltpu.make_async_copy(
                source.at[0, pl.ds(place, features)], target.at[index], semaphores.at[index, which]
            )
            copy.start()
            copies.append(copy)
    return copies


def near_kernel(
    ep_ref,
    own_ref,
    core_ref,
    gate_hbm,
    up_hbm,
    down_hbm,
    sums_out,
    far_gate,
    far_up,
    down,
    gate,
    up,
    semaphores,
    far_semaphores,
    down_semaphores,
):
    units = gate.shape[2]
    features = gate.shape[1]
    copies = weight_copies(ep_ref, (0, 1), gate_hbm, up_hbm, gate, up, semaphores)
    later = weight_copies(ep_ref, (2, 3), gate_hbm, up_hbm, far_gate, far_up, far_semaphores)
    for flip in (3, 1, 2, 0):
        place = pl.multiple_of((ep_ref[0] ^ flip) * features, features)
        copy = pltpu.make_async_copy(
            down_hbm.at[0, :, pl.ds(place, features)], down.at[flip], down_semaphores.at[flip]
        )
        copy.start()
        later.append(copy)
    gate_sum, up_sum = None, None
    for index, x_ref in enumerate((own_ref, core_ref)):
        rows = x_ref[...]
        copies[2 * index].wait()
        part = jnp.dot(rows, gate[index], preferred_element_type=jnp.float32)
        gate_sum = part if gate_sum is None else gate_sum + part
        copies[2 * index + 1].wait()
        part = jnp.dot(rows, up[index], preferred_element_type=jnp.float32)
        up_sum = part if up_sum is None else up_sum + part
    sums_out[:, :units] = gate_sum
    sums_out[:, units:] = up_sum
    for copy in later:
        copy.wait()


def near_experts(ep, own, core, w_gate, w_up, w_down):
    slots, features = own.shape
    units = w_gate.shape[2]
    return pl.pallas_call(
        near_kernel,
        out_shape=[
            jax.ShapeDtypeStruct((slots, 2 * units), jnp.float32),
            jax.ShapeDtypeStruct((2, features, units), jnp.bfloat16),
            jax.ShapeDtypeStruct((2, features, units), jnp.bfloat16),
            jax.ShapeDtypeStruct((4, units, features), jnp.bfloat16),
        ],
        in_specs=[SMEM_SPEC] + [VMEM_SPEC] * 2 + [HBM_SPEC] * 3,
        out_specs=[VMEM_SPEC] * 4,
        scratch_shapes=[
            VMEM((2, features, units), jnp.bfloat16),
            VMEM((2, features, units), jnp.bfloat16),
            pltpu.SemaphoreType.DMA((2, 2)),
            pltpu.SemaphoreType.DMA((2, 2)),
            pltpu.SemaphoreType.DMA((4,)),
        ],
        compiler_params=pltpu.CompilerParams(vmem_limit_bytes=46 * MIB),
        cost_estimate=pl.CostEstimate(
            flops=8 * slots * features * units,
            bytes_accessed=24 * features * units,
            transcendentals=0,
        ),
        name="near_experts",
    )(ep, own, core, w_gate, w_up, w_down)


def far_kernel(far_ref, sums_ref, gate, up, sums_out):
    units = gate.shape[2]
    rows = far_ref[...]
    for place, weights in ((slice(0, units), gate), (slice(units, 2 * units), up)):
        sums_out[:, place] = sums_ref[:, place] + jnp.dot(
            rows, weights[0], preferred_element_type=jnp.float32
        )


def sent_kernel(core_far_ref, sums_ref, gate, up, down, hidden_out, sent_out):
    units = gate.shape[2]
    rows = core_far_ref[...]
    gate_sum = sums_ref[:, :units] + jnp.dot(
        rows, gate[1], preferred_element_type=jnp.float32
    )
    up_sum = sums_ref[:, units:] + jnp.dot(rows, up[1], preferred_element_type=jnp.float32)
    hidden = (gate_sum / (1.0 + jnp.exp(-gate_sum)) * up_sum).astype(jnp.bfloat16)
    hidden_out[...] = hidden
    for index in range(2):
        sent_out[index] = jnp.dot(
            hidden, down[2 * index + 1], preferred_element_type=jnp.float32
        ).astype(jnp.bfloat16)


def kept_kernel(hidden_ref, down, kept_out):
    for index in range(2):
        kept_out[index] = jnp.dot(
            hidden_ref[...], down[2 * index], preferred_element_type=jnp.float32
        ).astype(jnp.bfloat16)


def expert_step(kernel, name, out_shape, *operands):
    return pl.pallas_call(
        kernel,
        out_shape=out_shape,
        in_specs=[VMEM_SPEC] * len(operands),
        out_specs=jax.tree.map(lambda _: VMEM_SPEC, out_shape),
        compiler_params=pltpu.CompilerParams(vmem_limit_bytes=SMALL),
        cost_estimate=pl.CostEstimate(
            flops=1 << 28, bytes_accessed=2 * MIB, transcendentals=1 << 14
        ),
        name=name,
    )(*operands)


def sum_kernel(ep_ref, kept_ref, received_ref, out_ref):
    my_x = ep_ref[0] // 2
    for flip in range(2):
        total = kept_ref[flip].astype(jnp.float32) + received_ref[flip].astype(jnp.float32)
        for index in range(out_ref.shape[0]):
            block = total[index * CAP : (index + 1) * CAP].astype(jnp.bfloat16)
            out_ref[index, my_x ^ flip] = block


def sum_cores(ep, kept, received, ctx):
    features = kept.shape[2]
    return pl.pallas_call(
        sum_kernel,
        out_shape=jax.ShapeDtypeStruct((ctx, 2, CAP, features), jnp.bfloat16),
        in_specs=[SMEM_SPEC] + [VMEM_SPEC] * 2,
        out_specs=VMEM_SPEC,
        compiler_params=pltpu.CompilerParams(vmem_limit_bytes=16 * MIB),
        cost_estimate=pl.CostEstimate(flops=0, bytes_accessed=MIB, transcendentals=0),
        name="sum_cores",
    )(ep, kept, received)


def combine_kernel(high_ref, low_ref, returned_ref, out_ref):
    returned = returned_ref[...]
    total = lax.dot_general(high_ref[...], returned, TN, preferred_element_type=jnp.float32)
    total = total + lax.dot_general(
        low_ref[...], returned, TN, preferred_element_type=jnp.float32
    )
    out_ref[...] = total.astype(jnp.bfloat16)


def combine(high, low, returned):
    slots, row_count = high.shape
    features = returned.shape[1]
    return pl.pallas_call(
        combine_kernel,
        out_shape=jax.ShapeDtypeStruct((row_count, features), jnp.bfloat16),
        in_specs=[VMEM_SPEC] * 3,
        out_specs=VMEM_SPEC,
        compiler_params=pltpu.CompilerParams(vmem_limit_bytes=LIMIT),
        cost_estimate=pl.CostEstimate(
            flops=4 * row_count * slots * features, bytes_accessed=MIB, transcendentals=0
        ),
        name="combine",
    )(high, low, returned)


def low_run(my_ctx, positions_ref):
    mine = my_ctx * (2 * HALF)
    return jnp.where(positions_ref[mine] < positions_ref[mine + HALF], 0, 1)


def fold_kernel(own_ref, positions_ref, q_nope_ref, q_rope_ref, w_uk_ref, out_ref):
    latent_width = w_uk_ref.shape[0]
    low = low_run(own_ref[0], positions_ref)
    for head in range(GROUP):
        columns = slice(head * NOPE, (head + 1) * NOPE)
        folded = lax.dot_general(
            q_nope_ref[:, columns], w_uk_ref[:, columns], NT, preferred_element_type=jnp.float32
        ).astype(jnp.bfloat16)
        rotated = q_rope_ref[:, head * ROPE : (head + 1) * ROPE]
        for run in range(2):
            rows = slice(run * HALF, (run + 1) * HALF)
            place = slice(head * HALF, (head + 1) * HALF)
            slot = 1 - (low ^ run)
            out_ref[0, slot, place, :latent_width] = folded[rows]
            out_ref[0, slot, place, latent_width:] = rotated[rows]


def fold(own, positions, q_nope, q_rope, w_uk):
    query_count, columns = q_nope.shape
    heads = columns // NOPE
    latent_width = w_uk.shape[0]
    width = latent_width + ROPE
    steps = heads // GROUP // 2
    queries = pl.pallas_call(
        fold_kernel,
        out_shape=jax.ShapeDtypeStruct((2, 2, heads // 2 * HALF, width), jnp.bfloat16),
        grid=(2 * steps,),
        in_specs=[
            SMEM_SPEC,
            SMEM_SPEC,
            pl.BlockSpec((query_count, GROUP * NOPE), lambda step: (0, step)),
            pl.BlockSpec((query_count, GROUP * ROPE), lambda step: (0, step)),
            pl.BlockSpec((latent_width, GROUP * NOPE), lambda step: (0, step)),
        ],
        out_specs=pl.BlockSpec(
            (1, 2, GROUP * HALF, width), lambda step: (step // steps, 0, step % steps, 0)
        ),
        compiler_params=pltpu.CompilerParams(vmem_limit_bytes=FULL),
        cost_estimate=pl.CostEstimate(
            flops=2 * query_count * columns * latent_width,
            bytes_accessed=6 * MIB,
            transcendentals=0,
        ),
        name="fold",
    )(own, positions, q_nope, q_rope, w_uk)
    return queries.reshape(2, heads * HALF, width)


def attention_kernel(
    own_ref,
    ep_ref,
    positions_ref,
    queries_hbm,
    w_uv_hbm,
    own_keys,
    core_keys,
    out_ref,
    keys,
    queries,
    w_uv,
    scores,
    tops,
    mixed,
    semaphores,
):
    query_copies = [
        pltpu.make_async_copy(queries_hbm.at[part], queries.at[part], semaphores.at[part])
        for part in range(2)
    ]
    w_uv_copy = pltpu.make_async_copy(w_uv_hbm, w_uv, semaphores.at[2])
    for copy in (query_copies[0], w_uv_copy, query_copies[1]):
        copy.start()
    blocks = own_keys.shape[0]
    my_ctx, my_ep = own_ref[0], ep_ref[0]
    for flip, source in enumerate((own_keys, core_keys)):
        for block in range(blocks):
            source_ctx = my_ctx
            for bit, step in enumerate(gather_order(blocks)):
                if block >> bit & 1:
                    source_ctx = source_ctx ^ step
            start = source_ctx * (2 * HALF) + ((my_ep % 2) ^ flip) * HALF
            place = pl.multiple_of(positions_ref[start], HALF)
            keys[pl.ds(place, HALF), :] = source[block]
    for part in range(2):
        query_copies[part].wait()
        attend_heads(
            own_ref,
            positions_ref,
            queries.at[part],
            w_uv,
            keys,
            out_ref,
            part * (w_uv.shape[1] // 2),
            scores,
            tops,
            mixed,
            w_uv_copy.wait if not part else lambda: None,
        )


def attend_heads(
    own_ref, positions_ref, queries, w_uv, keys, out_ref, skipped, scores, tops, mixed, wait
):
    latent_width = w_uv.shape[0]
    count = queries.shape[0] // 2
    heads = count // HALF
    mine = own_ref[0] * (2 * HALF)
    low = low_run(own_ref[0], positions_ref)
    high = 1 - low
    low_base = positions_ref[mine + low * HALF]
    high_base = positions_ref[mine + high * HALF]
    tops[...] = jnp.full(tops.shape, -jnp.inf, jnp.float32)
    offset = lax.broadcasted_iota(jnp.int32, (HALF, CHUNK), 1) - lax.broadcasted_iota(
        jnp.int32, (HALF, CHUNK), 0
    )
    low_chunks = (low_base + HALF + CHUNK - 1) // CHUNK
    high_chunks = (high_base + HALF + CHUNK - 1) // CHUNK

    def score(chunk, bases):
        start = pl.multiple_of(chunk * CHUNK, CHUNK)
        part = lax.dot_general(
            queries[: len(bases) * count, :],
            keys[pl.ds(start, CHUNK), :],
            NT,
            preferred_element_type=jnp.float32,
        )
        for index, base in enumerate(bases):
            visible = offset <= base - start
            for head in range(heads):
                rows = slice(index * count + head * HALF, index * count + (head + 1) * HALF)
                seen = jnp.where(visible, part[rows], -jnp.inf)
                scores[chunk, rows, :] = seen
                top = tops[rows, :]
                for lane in range(0, CHUNK, 128):
                    top = jnp.maximum(top, seen[:, lane : lane + 128])
                tops[rows, :] = top
        return 0

    lax.fori_loop(0, low_chunks, lambda c, _: score(c, (high_base, low_base)), 0)
    lax.fori_loop(low_chunks, high_chunks, lambda c, _: score(c, (high_base,)), 0)
    factor = math.log2(math.e) / math.sqrt(NOPE + ROPE)

    def mix(rows, chunks):
        top = jnp.max(tops[rows, :], axis=1, keepdims=True) * factor
        total = jnp.zeros((count, 128), jnp.float32)
        parts = []
        for chunk in range(chunks):
            part = jnp.exp2(scores[chunk, rows, :] * factor - top)
            for lane in range(0, CHUNK, 128):
                total = total + part[:, lane : lane + 128]
            parts.append(part.astype(jnp.bfloat16))
        summed = jnp.dot(
            jnp.concatenate(parts, axis=1),
            keys[: chunks * CHUNK, :latent_width],
            preferred_element_type=jnp.float32,
        )
        share = 1.0 / jnp.sum(total, axis=1, keepdims=True)
        mixed[rows, :] = (summed * share).astype(jnp.bfloat16)

    most = keys.shape[0] // CHUNK
    for chunks in range(1, most + 1):

        @pl.when(high_chunks == chunks)
        def _():
            mix(slice(0, count), chunks)

        @pl.when(low_chunks == chunks)
        def _():
            mix(slice(count, 2 * count), chunks)

    wait()
    high_rows = pl.ds(pl.multiple_of(high * HALF, HALF), HALF)
    low_rows = pl.ds(pl.multiple_of(low * HALF, HALF), HALF)
    for head in range(heads):
        both = jnp.concatenate(
            [
                mixed[head * HALF : (head + 1) * HALF, :],
                mixed[count + head * HALF : count + (head + 1) * HALF, :],
            ],
            axis=0,
        )
        columns = slice(skipped + head * VDIM, skipped + (head + 1) * VDIM)
        value = jnp.dot(
            both, w_uv[:, columns], preferred_element_type=jnp.float32
        ).astype(jnp.bfloat16)
        out_ref[high_rows, columns] = value[:HALF]
        out_ref[low_rows, columns] = value[HALF:]


def attend(own, ep, positions, queries, w_uv, *pieces):
    latent_width, columns = w_uv.shape
    key_count = positions.shape[0]
    width = pieces[0].shape[-1]
    rows = queries.shape[1]
    return pl.pallas_call(
        attention_kernel,
        out_shape=jax.ShapeDtypeStruct((2 * HALF, columns), jnp.bfloat16),
        in_specs=[SMEM_SPEC] * 3 + [HBM_SPEC] * 2 + [VMEM_SPEC] * 2,
        out_specs=VMEM_SPEC,
        scratch_shapes=[
            VMEM((key_count, width), jnp.bfloat16),
            VMEM(queries.shape, jnp.bfloat16),
            VMEM(w_uv.shape, jnp.bfloat16),
            VMEM((key_count // CHUNK, rows, CHUNK), jnp.float32),
            VMEM((rows, 128), jnp.float32),
            VMEM((rows, latent_width), jnp.bfloat16),
            pltpu.SemaphoreType.DMA((3,)),
        ],
        compiler_params=pltpu.CompilerParams(vmem_limit_bytes=52 * MIB),
        cost_estimate=pl.CostEstimate(
            flops=24 * rows * key_count * width,
            bytes_accessed=8 * MIB,
            transcendentals=rows * key_count,
        ),
        name="attention",
    )(own, ep, positions, queries, w_uv, *pieces)


def shards(
    q_nope,
    q_rope,
    latent,
    k_rope,
    w_uk,
    w_uv,
    positions,
    moe_rows,
    expert_ids,
    expert_weights,
    w_gate,
    w_up,
    w_down,
):
    ctx = lax.axis_size("ctx")
    me = lax.axis_index("ctx").astype(jnp.int32).reshape(1)
    ep = lax.axis_index(("x", "core")).astype(jnp.int32).reshape(1)

    def over_ctx(value, flip):
        return lax.ppermute(value, "ctx", [(i, i ^ flip) for i in range(ctx)])

    def over(value, axis):
        return lax.ppermute(value, axis, [(0, 1), (1, 0)])

    outgoing, high, low, packed = route(
        ep, expert_ids, expert_weights, k_rope, moe_rows, latent, ctx
    )
    arrived = lax.all_to_all(outgoing, "ctx", split_axis=0, concat_axis=0, tiled=True)
    flips = gather_order(ctx)
    received = over_ctx(packed[None], flips[0])
    high, q_nope, received = lax.optimization_barrier((high, q_nope, received))
    queries = fold(me, positions, q_nope, q_rope, w_uk)
    own_keys = jnp.concatenate([packed[None], received], axis=0)
    for flip in flips[1:-1]:
        own_keys = jnp.concatenate([own_keys, over_ctx(own_keys, flip)], axis=0)
    arrived, queries, own_keys = lax.optimization_barrier((arrived, queries, own_keys))

    own = arrived.reshape(ctx * CAP, arrived.shape[2])
    far = over(own, "x")
    core = over(own, "core")
    far_keys = over_ctx(own_keys, flips[-1])
    sums, far_gate, far_up, down = near_experts(ep, own, core, w_gate, w_up, w_down)
    far, sums = lax.optimization_barrier((far, sums))
    core_far = over(far, "core")
    slots, features = own.shape
    pieces = jax.ShapeDtypeStruct((2, slots, features), jnp.bfloat16)
    sums = expert_step(
        far_kernel,
        "far_rows",
        jax.ShapeDtypeStruct(sums.shape, jnp.float32),
        far,
        sums,
        far_gate,
        far_up,
    )
    hidden, sent = expert_step(
        sent_kernel,
        "sent_pieces",
        (jax.ShapeDtypeStruct((slots, down.shape[1]), jnp.bfloat16), pieces),
        core_far,
        sums,
        far_gate,
        far_up,
        down,
    )
    sent, far_keys = lax.optimization_barrier((sent, far_keys))
    received = over(sent, "core")
    kept = expert_step(kept_kernel, "kept_pieces", pieces, hidden, down)
    own_keys, far_keys, received, kept = lax.optimization_barrier(
        (own_keys, far_keys, received, kept)
    )
    own_keys = jnp.concatenate([own_keys, far_keys], axis=0)
    core_keys = over(own_keys, "core")
    returning = sum_cores(ep, kept, received, ctx)
    returned = lax.all_to_all(
        returning.reshape(2 * ctx, CAP, returning.shape[3]),
        ("ctx", "x"),
        split_axis=0,
        concat_axis=0,
        tiled=True,
    )
    attention = attend(me, ep, positions, queries, w_uv, own_keys, core_keys)
    moe_out = combine(high, low, returned.reshape(2 * ctx * CAP, returned.shape[2]))
    return (attention, moe_out)


def solution(mesh):
    split = (mesh.shape["ctx"], mesh.shape["ep"] // 2, 2)
    mesh = jax.sharding.Mesh(mesh.devices.reshape(split), ("ctx", "x", "core"))
    ep = ("x", "core")
    return jax.shard_map(
        shards,
        mesh=mesh,
        in_specs=(
            P("ctx", ep),
            P("ctx", ep),
            P("ctx", None),
            P("ctx", None),
            P(None, ep),
            P(None, ep),
            P(),
            P("ctx", ep),
            P("ctx", None),
            P("ctx", None),
            P("ctx", None, ep),
            P("ctx", None, ep),
            P("ctx", ep, None),
        ),
        out_specs=(P("ctx", ep), P("ctx", ep)),
        check_vma=False,
    )
```

```python
import math

import jax
import jax.numpy as jnp
from jax import lax
from jax.experimental import pallas as pl
from jax.experimental.pallas import tpu as pltpu
from jax.sharding import PartitionSpec as P

NOPE = 128
ROPE = 64
VDIM = 128
TOP = 8
CAP = 8
HALF = 64
GROUP = 4
MIB = 1 << 20
LIMIT = 52 * MIB
FULL = 60 * MIB
SMALL = 24 * MIB
CHUNK = 256

NT = (((1,), (1,)), ((), ()))
TN = (((0,), (0,)), ((), ()))
VMEM = pltpu.VMEM
SMEM_SPEC = pl.BlockSpec(memory_space=pltpu.SMEM)
VMEM_SPEC = pl.BlockSpec(memory_space=pltpu.VMEM)
HBM_SPEC = pl.BlockSpec(memory_space=pltpu.HBM)


def gather_order(ctx):
    bits = ctx.bit_length() - 1
    return [1 << (bits - 1)] + [1 << bit for bit in range(bits - 1)]


def route_kernel(
    ep_ref,
    ids_ref,
    weights_ref,
    rope_ref,
    rows_ref,
    latent_ref,
    sent_ref,
    high_ref,
    low_ref,
    packed_ref,
):
    latent_width = latent_ref.shape[1]
    rope = rope_ref[...].astype(jnp.float32).T
    for core in range(2):

        @pl.when(ep_ref[0] % 2 == core)
        def _():
            rows = slice(core * HALF, (core + 1) * HALF)
            packed_ref[:, :latent_width] = latent_ref[rows, :]
            packed_ref[:, latent_width:] = rope[rows].astype(jnp.bfloat16)

    row_count = ids_ref.shape[1]
    slots = sent_ref.shape[0] * CAP
    slot = lax.broadcasted_iota(jnp.int32, (slots, row_count), 0)
    expert = slot // CAP
    named = jnp.zeros((slots, row_count), jnp.float32)
    gate = jnp.zeros((slots, row_count), jnp.float32)
    for choice in range(TOP):
        match = ids_ref[choice : choice + 1, :] == expert
        named = jnp.where(match, 1.0, named)
        gate = jnp.where(match, weights_ref[choice : choice + 1, :], gate)
    row = lax.broadcasted_iota(jnp.int32, (row_count, row_count), 0)
    other = lax.broadcasted_iota(jnp.int32, (row_count, row_count), 1)
    before = jnp.where(row < other, 1.0, 0.0).astype(jnp.bfloat16)
    rank = jnp.dot(named.astype(jnp.bfloat16), before, preferred_element_type=jnp.float32)
    taken = (named > 0.0) & (rank == (slot % CAP).astype(jnp.float32))
    select = jnp.where(taken, 1.0, 0.0).astype(jnp.bfloat16)
    gate = jnp.where(taken, gate, 0.0)
    blocks = [gate[index * CAP : (index + 1) * CAP] for index in range(slots // CAP)]
    gate = jnp.concatenate([block for block in blocks for _ in range(2)], axis=0)
    high = gate.astype(jnp.bfloat16)
    high_ref[...] = high
    low_ref[...] = (gate - high.astype(jnp.float32)).astype(jnp.bfloat16)
    sent = jnp.dot(select, rows_ref[...], preferred_element_type=jnp.float32)
    for index in range(slots // CAP):
        sent_ref[index] = sent[index * CAP : (index + 1) * CAP].astype(jnp.bfloat16)


def route(ep, expert_ids, expert_weights, k_rope, moe_rows, latent, ctx):
    row_count, features = moe_rows.shape
    slots = ctx * CAP
    return pl.pallas_call(
        route_kernel,
        out_shape=[
            jax.ShapeDtypeStruct((ctx, CAP, features), jnp.bfloat16),
            jax.ShapeDtypeStruct((2 * slots, row_count), jnp.bfloat16),
            jax.ShapeDtypeStruct((2 * slots, row_count), jnp.bfloat16),
            jax.ShapeDtypeStruct((HALF, latent.shape[1] + ROPE), jnp.bfloat16),
        ],
        in_specs=[SMEM_SPEC] + [VMEM_SPEC] * 5,
        out_specs=[VMEM_SPEC] * 4,
        compiler_params=pltpu.CompilerParams(vmem_limit_bytes=FULL),
        cost_estimate=pl.CostEstimate(
            flops=2 * row_count * slots * features, bytes_accessed=1 * MIB, transcendentals=0
        ),
        name="route",
    )(ep, expert_ids.T, expert_weights.T, k_rope.T, moe_rows, latent)


def weight_copies(ep_ref, flips, gate_hbm, up_hbm, gate, up, semaphores):
    features = gate.shape[1]
    copies = []
    for index, flip in enumerate(flips):
        place = pl.multiple_of((ep_ref[0] ^ flip) * features, features)
        for which, (source, target) in enumerate(((gate_hbm, gate), (up_hbm, up))):
            copy = pltpu.make_async_copy(
                source.at[0, pl.ds(place, features)], target.at[index], semaphores.at[index, which]
            )
            copy.start()
            copies.append(copy)
    return copies


def near_kernel(
    ep_ref,
    own_ref,
    core_ref,
    gate_hbm,
    up_hbm,
    down_hbm,
    sums_out,
    far_gate,
    far_up,
    down,
    gate,
    up,
    semaphores,
    far_semaphores,
    down_semaphores,
):
    units = gate.shape[2]
    features = gate.shape[1]
    copies = weight_copies(ep_ref, (0, 1), gate_hbm, up_hbm, gate, up, semaphores)
    later = weight_copies(ep_ref, (2, 3), gate_hbm, up_hbm, far_gate, far_up, far_semaphores)
    for flip in (3, 1, 2, 0):
        place = pl.multiple_of((ep_ref[0] ^ flip) * features, features)
        copy = pltpu.make_async_copy(
            down_hbm.at[0, :, pl.ds(place, features)], down.at[flip], down_semaphores.at[flip]
        )
        copy.start()
        later.append(copy)
    gate_sum, up_sum = None, None
    for index, x_ref in enumerate((own_ref, core_ref)):
        rows = x_ref[...]
        copies[2 * index].wait()
        part = jnp.dot(rows, gate[index], preferred_element_type=jnp.float32)
        gate_sum = part if gate_sum is None else gate_sum + part
        copies[2 * index + 1].wait()
        part = jnp.dot(rows, up[index], preferred_element_type=jnp.float32)
        up_sum = part if up_sum is None else up_sum + part
    sums_out[:, :units] = gate_sum
    sums_out[:, units:] = up_sum
    for copy in later:
        copy.wait()


def near_experts(ep, own, core, w_gate, w_up, w_down):
    slots, features = own.shape
    units = w_gate.shape[2]
    return pl.pallas_call(
        near_kernel,
        out_shape=[
            jax.ShapeDtypeStruct((slots, 2 * units), jnp.float32),
            jax.ShapeDtypeStruct((2, features, units), jnp.bfloat16),
            jax.ShapeDtypeStruct((2, features, units), jnp.bfloat16),
            jax.ShapeDtypeStruct((4, units, features), jnp.bfloat16),
        ],
        in_specs=[SMEM_SPEC] + [VMEM_SPEC] * 2 + [HBM_SPEC] * 3,
        out_specs=[VMEM_SPEC] * 4,
        scratch_shapes=[
            VMEM((2, features, units), jnp.bfloat16),
            VMEM((2, features, units), jnp.bfloat16),
            pltpu.SemaphoreType.DMA((2, 2)),
            pltpu.SemaphoreType.DMA((2, 2)),
            pltpu.SemaphoreType.DMA((4,)),
        ],
        compiler_params=pltpu.CompilerParams(vmem_limit_bytes=46 * MIB),
        cost_estimate=pl.CostEstimate(
            flops=8 * slots * features * units,
            bytes_accessed=24 * features * units,
            transcendentals=0,
        ),
        name="near_experts",
    )(ep, own, core, w_gate, w_up, w_down)


def far_kernel(far_ref, sums_ref, gate, up, sums_out):
    units = gate.shape[2]
    rows = far_ref[...]
    for place, weights in ((slice(0, units), gate), (slice(units, 2 * units), up)):
        sums_out[:, place] = sums_ref[:, place] + jnp.dot(
            rows, weights[0], preferred_element_type=jnp.float32
        )


def sent_kernel(core_far_ref, sums_ref, gate, up, down, hidden_out, sent_out):
    units = gate.shape[2]
    rows = core_far_ref[...]
    gate_sum = sums_ref[:, :units] + jnp.dot(
        rows, gate[1], preferred_element_type=jnp.float32
    )
    up_sum = sums_ref[:, units:] + jnp.dot(rows, up[1], preferred_element_type=jnp.float32)
    hidden = (gate_sum / (1.0 + jnp.exp(-gate_sum)) * up_sum).astype(jnp.bfloat16)
    hidden_out[...] = hidden
    for index in range(2):
        sent_out[index] = jnp.dot(
            hidden, down[2 * index + 1], preferred_element_type=jnp.float32
        ).astype(jnp.bfloat16)


def kept_kernel(hidden_ref, down, kept_out):
    for index in range(2):
        kept_out[index] = jnp.dot(
            hidden_ref[...], down[2 * index], preferred_element_type=jnp.float32
        ).astype(jnp.bfloat16)


def expert_step(kernel, name, out_shape, *operands):
    return pl.pallas_call(
        kernel,
        out_shape=out_shape,
        in_specs=[VMEM_SPEC] * len(operands),
        out_specs=jax.tree.map(lambda _: VMEM_SPEC, out_shape),
        compiler_params=pltpu.CompilerParams(vmem_limit_bytes=SMALL),
        cost_estimate=pl.CostEstimate(
            flops=1 << 28, bytes_accessed=2 * MIB, transcendentals=1 << 14
        ),
        name=name,
    )(*operands)


def sum_kernel(ep_ref, kept_ref, received_ref, out_ref):
    my_x = ep_ref[0] // 2
    for flip in range(2):
        total = kept_ref[flip].astype(jnp.float32) + received_ref[flip].astype(jnp.float32)
        for index in range(out_ref.shape[0]):
            block = total[index * CAP : (index + 1) * CAP].astype(jnp.bfloat16)
            out_ref[index, my_x ^ flip] = block


def sum_cores(ep, kept, received, ctx):
    features = kept.shape[2]
    return pl.pallas_call(
        sum_kernel,
        out_shape=jax.ShapeDtypeStruct((ctx, 2, CAP, features), jnp.bfloat16),
        in_specs=[SMEM_SPEC] + [VMEM_SPEC] * 2,
        out_specs=VMEM_SPEC,
        compiler_params=pltpu.CompilerParams(vmem_limit_bytes=16 * MIB),
        cost_estimate=pl.CostEstimate(flops=0, bytes_accessed=MIB, transcendentals=0),
        name="sum_cores",
    )(ep, kept, received)


def combine_kernel(high_ref, low_ref, returned_ref, out_ref):
    returned = returned_ref[...]
    total = lax.dot_general(high_ref[...], returned, TN, preferred_element_type=jnp.float32)
    total = total + lax.dot_general(
        low_ref[...], returned, TN, preferred_element_type=jnp.float32
    )
    out_ref[...] = total.astype(jnp.bfloat16)


def combine(high, low, returned):
    slots, row_count = high.shape
    features = returned.shape[1]
    return pl.pallas_call(
        combine_kernel,
        out_shape=jax.ShapeDtypeStruct((row_count, features), jnp.bfloat16),
        in_specs=[VMEM_SPEC] * 3,
        out_specs=VMEM_SPEC,
        compiler_params=pltpu.CompilerParams(vmem_limit_bytes=LIMIT),
        cost_estimate=pl.CostEstimate(
            flops=4 * row_count * slots * features, bytes_accessed=MIB, transcendentals=0
        ),
        name="combine",
    )(high, low, returned)


def low_run(my_ctx, positions_ref):
    mine = my_ctx * (2 * HALF)
    return jnp.where(positions_ref[mine] < positions_ref[mine + HALF], 0, 1)


def fold_kernel(own_ref, positions_ref, q_nope_ref, q_rope_ref, w_uk_ref, out_ref):
    latent_width = w_uk_ref.shape[0]
    low = low_run(own_ref[0], positions_ref)
    for head in range(GROUP):
        columns = slice(head * NOPE, (head + 1) * NOPE)
        folded = lax.dot_general(
            q_nope_ref[:, columns], w_uk_ref[:, columns], NT, preferred_element_type=jnp.float32
        ).astype(jnp.bfloat16)
        rotated = q_rope_ref[:, head * ROPE : (head + 1) * ROPE]
        for run in range(2):
            rows = slice(run * HALF, (run + 1) * HALF)
            place = slice(head * HALF, (head + 1) * HALF)
            slot = 1 - (low ^ run)
            out_ref[0, slot, place, :latent_width] = folded[rows]
            out_ref[0, slot, place, latent_width:] = rotated[rows]


def fold(own, positions, q_nope, q_rope, w_uk):
    query_count, columns = q_nope.shape
    heads = columns // NOPE
    latent_width = w_uk.shape[0]
    width = latent_width + ROPE
    steps = heads // GROUP // 2
    queries = pl.pallas_call(
        fold_kernel,
        out_shape=jax.ShapeDtypeStruct((2, 2, heads // 2 * HALF, width), jnp.bfloat16),
        grid=(2 * steps,),
        in_specs=[
            SMEM_SPEC,
            SMEM_SPEC,
            pl.BlockSpec((query_count, GROUP * NOPE), lambda step: (0, step)),
            pl.BlockSpec((query_count, GROUP * ROPE), lambda step: (0, step)),
            pl.BlockSpec((latent_width, GROUP * NOPE), lambda step: (0, step)),
        ],
        out_specs=pl.BlockSpec(
            (1, 2, GROUP * HALF, width), lambda step: (step // steps, 0, step % steps, 0)
        ),
        compiler_params=pltpu.CompilerParams(vmem_limit_bytes=FULL),
        cost_estimate=pl.CostEstimate(
            flops=2 * query_count * columns * latent_width,
            bytes_accessed=6 * MIB,
            transcendentals=0,
        ),
        name="fold",
    )(own, positions, q_nope, q_rope, w_uk)
    return queries.reshape(2, heads * HALF, width)


def attention_kernel(
    own_ref,
    ep_ref,
    positions_ref,
    queries_hbm,
    w_uv_hbm,
    own_keys,
    core_keys,
    out_ref,
    keys,
    queries,
    w_uv,
    scores,
    tops,
    mixed,
    semaphores,
):
    query_copies = [
        pltpu.make_async_copy(queries_hbm.at[part], queries.at[part], semaphores.at[part])
        for part in range(2)
    ]
    w_uv_copy = pltpu.make_async_copy(w_uv_hbm, w_uv, semaphores.at[2])
    for copy in (query_copies[0], w_uv_copy, query_copies[1]):
        copy.start()
    blocks = own_keys.shape[0]
    my_ctx, my_ep = own_ref[0], ep_ref[0]
    for flip, source in enumerate((own_keys, core_keys)):
        for block in range(blocks):
            source_ctx = my_ctx
            for bit, step in enumerate(gather_order(blocks)):
                if block >> bit & 1:
                    source_ctx = source_ctx ^ step
            start = source_ctx * (2 * HALF) + ((my_ep % 2) ^ flip) * HALF
            place = pl.multiple_of(positions_ref[start], HALF)
            keys[pl.ds(place, HALF), :] = source[block]
    for part in range(2):
        query_copies[part].wait()
        attend_heads(
            own_ref,
            positions_ref,
            queries.at[part],
            w_uv,
            keys,
            out_ref,
            part * (w_uv.shape[1] // 2),
            scores,
            tops,
            mixed,
            w_uv_copy.wait if not part else lambda: None,
        )


def attend_heads(
    own_ref, positions_ref, queries, w_uv, keys, out_ref, skipped, scores, tops, mixed, wait
):
    latent_width = w_uv.shape[0]
    count = queries.shape[0] // 2
    heads = count // HALF
    mine = own_ref[0] * (2 * HALF)
    low = low_run(own_ref[0], positions_ref)
    high = 1 - low
    low_base = positions_ref[mine + low * HALF]
    high_base = positions_ref[mine + high * HALF]
    tops[...] = jnp.full(tops.shape, -jnp.inf, jnp.float32)
    offset = lax.broadcasted_iota(jnp.int32, (HALF, CHUNK), 1) - lax.broadcasted_iota(
        jnp.int32, (HALF, CHUNK), 0
    )
    low_chunks = (low_base + HALF + CHUNK - 1) // CHUNK
    high_chunks = (high_base + HALF + CHUNK - 1) // CHUNK

    def score(chunk, bases):
        start = pl.multiple_of(chunk * CHUNK, CHUNK)
        part = lax.dot_general(
            queries[: len(bases) * count, :],
            keys[pl.ds(start, CHUNK), :],
            NT,
            preferred_element_type=jnp.float32,
        )
        for index, base in enumerate(bases):
            visible = offset <= base - start
            for head in range(heads):
                rows = slice(index * count + head * HALF, index * count + (head + 1) * HALF)
                seen = jnp.where(visible, part[rows], -jnp.inf)
                scores[chunk, rows, :] = seen
                top = tops[rows, :]
                for lane in range(0, CHUNK, 128):
                    top = jnp.maximum(top, seen[:, lane : lane + 128])
                tops[rows, :] = top
        return 0

    lax.fori_loop(0, low_chunks, lambda c, _: score(c, (high_base, low_base)), 0)
    lax.fori_loop(low_chunks, high_chunks, lambda c, _: score(c, (high_base,)), 0)
    factor = math.log2(math.e) / math.sqrt(NOPE + ROPE)

    def mix(rows, chunks):
        top = jnp.max(tops[rows, :], axis=1, keepdims=True) * factor
        total = jnp.zeros((count, 128), jnp.float32)
        parts = []
        for chunk in range(chunks):
            part = jnp.exp2(scores[chunk, rows, :] * factor - top)
            for lane in range(0, CHUNK, 128):
                total = total + part[:, lane : lane + 128]
            parts.append(part.astype(jnp.bfloat16))
        summed = jnp.dot(
            jnp.concatenate(parts, axis=1),
            keys[: chunks * CHUNK, :latent_width],
            preferred_element_type=jnp.float32,
        )
        share = 1.0 / jnp.sum(total, axis=1, keepdims=True)
        mixed[rows, :] = (summed * share).astype(jnp.bfloat16)

    most = keys.shape[0] // CHUNK
    for chunks in range(1, most + 1):

        @pl.when(high_chunks == chunks)
        def _():
            mix(slice(0, count), chunks)

        @pl.when(low_chunks == chunks)
        def _():
            mix(slice(count, 2 * count), chunks)

    wait()
    high_rows = pl.ds(pl.multiple_of(high * HALF, HALF), HALF)
    low_rows = pl.ds(pl.multiple_of(low * HALF, HALF), HALF)
    for head in range(heads):
        both = jnp.concatenate(
            [
                mixed[head * HALF : (head + 1) * HALF, :],
                mixed[count + head * HALF : count + (head + 1) * HALF, :],
            ],
            axis=0,
        )
        columns = slice(skipped + head * VDIM, skipped + (head + 1) * VDIM)
        value = jnp.dot(
            both, w_uv[:, columns], preferred_element_type=jnp.float32
        ).astype(jnp.bfloat16)
        out_ref[high_rows, columns] = value[:HALF]
        out_ref[low_rows, columns] = value[HALF:]


def attend(own, ep, positions, queries, w_uv, *pieces):
    latent_width, columns = w_uv.shape
    key_count = positions.shape[0]
    width = pieces[0].shape[-1]
    rows = queries.shape[1]
    return pl.pallas_call(
        attention_kernel,
        out_shape=jax.ShapeDtypeStruct((2 * HALF, columns), jnp.bfloat16),
        in_specs=[SMEM_SPEC] * 3 + [HBM_SPEC] * 2 + [VMEM_SPEC] * 2,
        out_specs=VMEM_SPEC,
        scratch_shapes=[
            VMEM((key_count, width), jnp.bfloat16),
            VMEM(queries.shape, jnp.bfloat16),
            VMEM(w_uv.shape, jnp.bfloat16),
            VMEM((key_count // CHUNK, rows, CHUNK), jnp.float32),
            VMEM((rows, 128), jnp.float32),
            VMEM((rows, latent_width), jnp.bfloat16),
            pltpu.SemaphoreType.DMA((3,)),
        ],
        compiler_params=pltpu.CompilerParams(vmem_limit_bytes=52 * MIB),
        cost_estimate=pl.CostEstimate(
            flops=24 * rows * key_count * width,
            bytes_accessed=8 * MIB,
            transcendentals=rows * key_count,
        ),
        name="attention",
    )(own, ep, positions, queries, w_uv, *pieces)


def shards(
    q_nope,
    q_rope,
    latent,
    k_rope,
    w_uk,
    w_uv,
    positions,
    moe_rows,
    expert_ids,
    expert_weights,
    w_gate,
    w_up,
    w_down,
):
    ctx = lax.axis_size("ctx")
    me = lax.axis_index("ctx").astype(jnp.int32).reshape(1)
    ep = lax.axis_index(("x", "core")).astype(jnp.int32).reshape(1)

    def over_ctx(value, flip):
        return lax.ppermute(value, "ctx", [(i, i ^ flip) for i in range(ctx)])

    def over(value, axis):
        return lax.ppermute(value, axis, [(0, 1), (1, 0)])

    outgoing, high, low, packed = route(
        ep, expert_ids, expert_weights, k_rope, moe_rows, latent, ctx
    )
    arrived = lax.all_to_all(outgoing, "ctx", split_axis=0, concat_axis=0, tiled=True)
    flips = gather_order(ctx)
    received = over_ctx(packed[None], flips[0])
    high, q_nope, received = lax.optimization_barrier((high, q_nope, received))
    queries = fold(me, positions, q_nope, q_rope, w_uk)
    packed, received = lax.optimization_barrier((packed, received))
    blocks = [packed[None], received]
    blocks = blocks + [over_ctx(block, flips[1]) for block in blocks]
    own_keys = jnp.concatenate(blocks, axis=0)
    for flip in flips[2:-1]:
        own_keys = jnp.concatenate([own_keys, over_ctx(own_keys, flip)], axis=0)
    arrived, queries, own_keys = lax.optimization_barrier((arrived, queries, own_keys))

    own = arrived.reshape(ctx * CAP, arrived.shape[2])
    far = over(own, "x")
    core = over(own, "core")
    far_keys = over_ctx(own_keys, flips[-1])
    sums, far_gate, far_up, down = near_experts(ep, own, core, w_gate, w_up, w_down)
    far, sums = lax.optimization_barrier((far, sums))
    core_far = over(far, "core")
    slots, features = own.shape
    pieces = jax.ShapeDtypeStruct((2, slots, features), jnp.bfloat16)
    sums = expert_step(
        far_kernel,
        "far_rows",
        jax.ShapeDtypeStruct(sums.shape, jnp.float32),
        far,
        sums,
        far_gate,
        far_up,
    )
    hidden, sent = expert_step(
        sent_kernel,
        "sent_pieces",
        (jax.ShapeDtypeStruct((slots, down.shape[1]), jnp.bfloat16), pieces),
        core_far,
        sums,
        far_gate,
        far_up,
        down,
    )
    sent, far_keys = lax.optimization_barrier((sent, far_keys))
    received = over(sent, "core")
    kept = expert_step(kept_kernel, "kept_pieces", pieces, hidden, down)
    own_keys, far_keys, received, kept = lax.optimization_barrier(
        (own_keys, far_keys, received, kept)
    )
    own_keys = jnp.concatenate([own_keys, far_keys], axis=0)
    core_keys = over(own_keys, "core")
    returning = sum_cores(ep, kept, received, ctx)
    returned = lax.all_to_all(
        returning.reshape(2 * ctx, CAP, returning.shape[3]),
        ("ctx", "x"),
        split_axis=0,
        concat_axis=0,
        tiled=True,
    )
    attention = attend(me, ep, positions, queries, w_uv, own_keys, core_keys)
    moe_out = combine(high, low, returned.reshape(2 * ctx * CAP, returned.shape[2]))
    return (attention, moe_out)


def solution(mesh):
    split = (mesh.shape["ctx"], mesh.shape["ep"] // 2, 2)
    mesh = jax.sharding.Mesh(mesh.devices.reshape(split), ("ctx", "x", "core"))
    ep = ("x", "core")
    return jax.shard_map(
        shards,
        mesh=mesh,
        in_specs=(
            P("ctx", ep),
            P("ctx", ep),
            P("ctx", None),
            P("ctx", None),
            P(None, ep),
            P(None, ep),
            P(),
            P("ctx", ep),
            P("ctx", None),
            P("ctx", None),
            P("ctx", None, ep),
            P("ctx", None, ep),
            P("ctx", ep, None),
        ),
        out_specs=(P("ctx", ep), P("ctx", ep)),
        check_vma=False,
    )
```
